32 devices in a mesh: wide: 16 (over z, y, x), narrow: 2 (over core).
Axes of the slice: x: 2, y: 2, z: 4, core: 2. Of those that a mesh axis runs over, the one named last changes fastest.
Arguments:
- incoming_activations: bfloat16 [32768, 768], P(('wide', 'narrow')), may hold values from -6 to 6
- span_identifiers: int32 [64, 512], P(('wide', 'narrow')), may hold values from 0 to 7, never falling along the last dimension, each value on 1 to 128 neighbouring positions
- partner_global_index: int32 [512], replicated, may hold values from 0 to 511, as said below
- softmax_coolness: float32 [1], replicated, may hold values from 0.03 to 0.06
- triple_kernel_panel: bfloat16 [768, 2304], replicated, may hold values from -0.21875 to 0.21875
- asking_shift: float32 [768], replicated, may hold values from -0.6 to 0.6
- content_shift: float32 [768], replicated, may hold values from -0.6 to 0.6
- mixer_result_kernel: bfloat16 [768, 768], replicated, may hold values from -1.75 to 1.75
- mixer_result_shift: float32 [768], replicated, may hold values from -0.6 to 0.6
- initial_standardize_scale: float32 [768], replicated, may hold values from 0.5 to 1.5
- initial_standardize_shift: float32 [768], replicated, may hold values from -0.6 to 0.6
- perceptron_entry_kernel: bfloat16 [768, 3072], replicated, may hold values from -0.21875 to 0.21875
- perceptron_entry_shift: float32 [3072], replicated, may hold values from -0.6 to 0.6
- perceptron_result_kernel: bfloat16 [3072, 768], replicated, may hold values from -0.109375 to 0.109375
- perceptron_result_shift: float32 [768], replicated, may hold values from -0.6 to 0.6
- later_standardize_scale: float32 [768], replicated, may hold values from 0.5 to 1.5
- later_standardize_shift: float32 [768], replicated, may hold values from -0.6 to 0.6
Outputs:
- loss: float32 [1], replicated
- layer_out: bfloat16 [32768, 768], P(('wide', 'narrow'))
- input_grad: float32 [32768, 768], P(('wide', 'narrow'))
- attn_weight_grad: float32 [768, 2304], replicated
- query_bias_grad: float32 [768], replicated
- value_bias_grad: float32 [768], replicated
- merge_weight_grad: float32 [768, 768], replicated
- merge_bias_grad: float32 [768], replicated
- first_gain_grad: float32 [768], replicated
- first_shift_grad: float32 [768], replicated
- inner_weight_grad: float32 [768, 3072], replicated
- inner_bias_grad: float32 [3072], replicated
- outer_weight_grad: float32 [3072, 768], replicated
- outer_bias_grad: float32 [768], replicated
- second_gain_grad: float32 [768], replicated
- second_shift_grad: float32 [768], replicated
The draws below stay inside these ranges and needn't reach their ends.
Inputs may be any that keep to these rules, and one draw needn't show every extreme that they name: `span_identifiers`: in each packed row the segment numbers never fall and every number below 8 occurs, none on more than 128 tokens. `partner_global_index`: a permutation of the segments with no segment its own partner.
All inputs are finite; a program needn't handle non-finite values.
Results may differ from the reference program's by a relative error of at most 0.008.
Values may be sent and summed in bfloat16 or wider, within the bound.
No kernel may reach another device: no remote copies, remote signals or barrier semaphores. Data moves between devices by JAX's collectives and lax.ppermute only.
A program may use at most 192 MiB of HBM per device.

```python
import math
import jax
import jax.numpy as jnp
import numpy as np
from jax import lax

D = 768
HEADS = 12
HEAD = 64
FF = 3072
ROW_LEN = 512
S_ROW = 8
ROWS = 64
TOKENS = 32768
NSEG = 512
SEG_MOST = 128


def draw_partner_global_index(key, part):
    key = jax.random.fold_in(key, 7)
    order = jax.random.permutation(key, NSEG).astype(jnp.int32)
    return jnp.zeros((NSEG,), jnp.int32).at[order].set(jnp.roll(order, -1)).astype(jnp.int32)


def shard_levels(stream_key, extent, pieces, smallest, high):
    level, own = 1.0, jax.random.fold_in(stream_key, 6)
    for position, parts in pieces:
        draws = jnp.exp(jax.random.uniform(jax.random.fold_in(own, position), (parts,), jnp.float32, smallest / len(pieces), high / len(pieces)))
        level = level * jnp.repeat(draws, extent[position] // parts).reshape([-1 if axis == position else 1 for axis in range(len(extent))])
    return level


def length_profile(number_of, total, limit, lean):
    weights = [(1 << 20) // math.isqrt(standing ** lean) + 1 for standing in range(2, number_of + 1)]
    rest, given = total - limit - (number_of - 1), [1] * (number_of - 1)
    while rest > 0:
        candidates = [i for i in range(number_of - 1) if given[i] < limit]
        mass, remaining = sum([weights[i] for i in candidates]), rest
        for i in candidates:
            addition = min(limit - given[i], max(1, remaining * weights[i] // mass), rest)
            given[i] = given[i] + addition
            rest = rest - addition
    return np.array([limit] + given)


def uneven(rng, amount, total, limit, slope):
    if amount == 2:
        one = jax.random.randint(rng, (), max(1, total - limit), min(limit, total - 1) + 1)
        return jnp.stack([one, total - one])
    lengths = jnp.asarray(length_profile(amount, total, limit, slope), jnp.int32)
    couples = (amount - 1) // 2
    giver, receiver = lengths[1:1 + 2 * couples:2], lengths[2:2 + 2 * couples:2]
    room = jnp.minimum(giver - 1, limit - receiver)
    moved = jax.random.randint(jax.random.fold_in(rng, 1), (couples,), 0, 1 << 20) % (room + 1)
    lengths = lengths.at[1:1 + 2 * couples:2].set(giver - moved).at[2:2 + 2 * couples:2].set(receiver + moved)
    return lengths[jax.random.permutation(jax.random.fold_in(rng, 2), amount)]


def centred(key, shape, deviation, most, shards=(), dtype=jnp.bfloat16):
    drawn = jax.random.normal(key, shape, jnp.float32) * deviation
    if len(shards) > 0:
        drawn = shard_levels(key, shape, shards, -0.22, 0.18) * drawn
    return jnp.clip(drawn, min=-most, max=most).astype(dtype)


def setup_inputs(seed: int = 0) -> dict:
    splits = jax.random.split(jax.random.key(seed), 18)
    incoming_activations = centred(splits[0], (TOKENS, D), 1.0, 6.0, ((0, 32),))
    span_identifiers = jax.vmap(lambda own: jnp.searchsorted(jnp.cumsum(uneven(own, S_ROW, ROW_LEN, SEG_MOST, 2)), jnp.arange(ROW_LEN), side="right"))(jax.random.split(splits[1], ROWS)).reshape((ROWS, ROW_LEN)).astype(jnp.int32)
    partner_global_index = draw_partner_global_index(jax.random.fold_in(splits[17], 71), 0)
    softmax_coolness = jnp.clip(jnp.exp(jax.random.uniform(splits[3], (1,), jnp.float32, math.log(0.03), math.log(0.06))), 0.03, 0.06)
    triple_kernel_panel = centred(splits[4], (D, 3 * D), D ** -0.5, 0.21875)
    asking_shift = centred(splits[5], (D,), 0.1, 0.6, (), jnp.float32)
    content_shift = centred(splits[6], (D,), 0.1, 0.6, (), jnp.float32)
    mixer_result_kernel = centred(splits[7], (D, D), (max(D // 64, 12)) ** -0.5, 1.75)
    mixer_result_shift = centred(splits[8], (D,), 0.1, 0.6, (), jnp.float32)
    initial_standardize_scale = jnp.clip(1.0 + 0.1 * jax.random.normal(splits[9], (D,), jnp.float32), 0.5, 1.5)
    initial_standardize_shift = centred(splits[10], (D,), 0.1, 0.6, (), jnp.float32)
    perceptron_entry_kernel = centred(splits[11], (D, FF), D ** -0.5, 0.21875)
    perceptron_entry_shift = centred(splits[12], (FF,), 0.1, 0.6, (), jnp.float32)
    perceptron_result_kernel = centred(splits[13], (FF, D), FF ** -0.5, 0.109375)
    perceptron_result_shift = centred(splits[14], (D,), 0.1, 0.6, (), jnp.float32)
    later_standardize_scale = jnp.clip(1.0 + 0.1 * jax.random.normal(splits[15], (D,), jnp.float32), 0.5, 1.5)
    later_standardize_shift = centred(splits[16], (D,), 0.1, 0.6, (), jnp.float32)
    return dict(incoming_activations=incoming_activations, span_identifiers=span_identifiers, partner_global_index=partner_global_index, softmax_coolness=softmax_coolness, triple_kernel_panel=triple_kernel_panel, asking_shift=asking_shift, content_shift=content_shift, mixer_result_kernel=mixer_result_kernel, mixer_result_shift=mixer_result_shift, initial_standardize_scale=initial_standardize_scale, initial_standardize_shift=initial_standardize_shift, perceptron_entry_kernel=perceptron_entry_kernel, perceptron_entry_shift=perceptron_entry_shift, perceptron_result_kernel=perceptron_result_kernel, perceptron_result_shift=perceptron_result_shift, later_standardize_scale=later_standardize_scale, later_standardize_shift=later_standardize_shift)


@jax.custom_vjp
def low(v):
    return lax.optimization_barrier(v.astype(jnp.bfloat16)).astype(jnp.float32)

@jax.custom_vjp
def low_back(v):
    return v

def low_keep(v):
    return (low(v), None)

def low_pass(kept, grad):
    return (grad,)

def back_keep(v):
    return (v, None)

def back_low(kept, grad):
    return (low(grad),)
low.defvjp(low_keep, low_pass)
low_back.defvjp(back_keep, back_low)

def linear_map_result(left, right):
    return jnp.dot(left, right, precision=lax.Precision.HIGHEST, preferred_element_type=jnp.float32)

def layer_norm(values, gain, shift):
    center = values - lax.optimization_barrier(jnp.mean(values, axis=-1, keepdims=True))
    spread = lax.optimization_barrier(jnp.mean(center * center, axis=-1, keepdims=True))
    return center * lax.rsqrt(spread + 1e-05) * gain + shift

def one_row(params, row, segment_row):
    triple_kernel_panel, asking_shift, content_shift, mixer_result_kernel, mixer_result_shift, initial_standardize_scale, initial_standardize_shift, perceptron_entry_kernel, perceptron_entry_shift, perceptron_result_kernel, perceptron_result_shift, later_standardize_scale, later_standardize_shift = params
    length = row.shape[0]
    zero_bias = jnp.zeros_like(asking_shift)
    projected = linear_map_result(row, triple_kernel_panel) + jnp.concatenate([asking_shift, zero_bias, content_shift])
    projected = low_back(low(projected))
    split = projected.reshape(length, 3, HEADS, HEAD)
    queries = split[:, 0]
    keys_all = split[:, 1]
    values = split[:, 2]
    raw = jnp.einsum('qhd,khd->hqk', queries, keys_all, precision=lax.Precision.HIGHEST) * HEAD ** (-0.5)
    raw = low_back(raw)
    same = segment_row[:, None] == segment_row[None, :]
    masked = jnp.where(same[None], raw, -1000000000.0)
    top = lax.optimization_barrier(jnp.max(masked, axis=-1, keepdims=True))
    exps = jnp.exp(masked - top)
    probs = exps / lax.optimization_barrier(jnp.sum(exps, axis=-1, keepdims=True))
    mixed = jnp.einsum('hqk,khd->qhd', low(probs), values, precision=lax.Precision.HIGHEST).reshape(length, D)
    mixed = low_back(low(mixed))
    attn = low_back(linear_map_result(mixed, mixer_result_kernel) + mixer_result_shift)
    normed = layer_norm(row + attn, initial_standardize_scale, initial_standardize_shift)
    inner = low_back(linear_map_result(low(normed), perceptron_entry_kernel) + perceptron_entry_shift)
    active = low(jax.nn.gelu(inner, approximate=False))
    outer = low_back(linear_map_result(active, perceptron_result_kernel) + perceptron_result_shift)
    return layer_norm(normed + outer, later_standardize_scale, later_standardize_shift)

def pool(output, segment_row):
    onehot = (segment_row[:, None] == jnp.arange(S_ROW)[None, :]).astype(jnp.float32)
    counts = lax.optimization_barrier(jnp.sum(onehot, axis=0))
    return linear_map_result(onehot.T, output) / counts[:, None]

def infonce_objective(span_pooled_code, partner_global_index, softmax_coolness):
    count = span_pooled_code.shape[0]
    ident = jnp.arange(count)
    self_pair_filter = ident[:, None] == ident[None, :]
    hit_mask = partner_global_index[:, None] == ident[None, :]
    total = jnp.zeros((), jnp.float32)
    for factor in (12, 8, 4, 2, 1):
        width = D * factor // 12
        part = span_pooled_code[:, :width]
        normalized_directions = part * lax.rsqrt(lax.optimization_barrier(jnp.sum(part * part, axis=1, keepdims=True)) + 1e-06)
        cosine_logits = linear_map_result(normalized_directions, normalized_directions.T) / softmax_coolness[0]
        masked = jnp.where(self_pair_filter, -1000000000.0, cosine_logits)
        top = lax.optimization_barrier(jnp.max(masked, axis=1, keepdims=True))
        log_total = top[:, 0] + jnp.log(lax.optimization_barrier(jnp.sum(jnp.exp(masked - top), axis=1)))
        hits = lax.optimization_barrier(jnp.sum(jnp.where(hit_mask, masked, 0.0), axis=1))
        total = total + jnp.sum(log_total - hits)
    return total

def reference(incoming_activations, span_identifiers, partner_global_index, softmax_coolness, triple_kernel_panel, asking_shift, content_shift, mixer_result_kernel, mixer_result_shift, initial_standardize_scale, initial_standardize_shift, perceptron_entry_kernel, perceptron_entry_shift, perceptron_result_kernel, perceptron_result_shift, later_standardize_scale, later_standardize_shift):
    params = tuple((item.astype(jnp.float32) for item in (triple_kernel_panel, asking_shift, content_shift, mixer_result_kernel, mixer_result_shift, initial_standardize_scale, initial_standardize_shift, perceptron_entry_kernel, perceptron_entry_shift, perceptron_result_kernel, perceptron_result_shift, later_standardize_scale, later_standardize_shift)))
    inputs = incoming_activations.astype(jnp.float32).reshape(ROWS, ROW_LEN, D)

    def total_loss(params, inputs):

        def row_step(pair):
            row, segment_row = pair
            output = one_row(params, row, segment_row)
            return (output, low(pool(output, segment_row)))
        encoder_results, span_pooled_codes = lax.map(jax.checkpoint(row_step), (inputs, span_identifiers))
        span_pooled_codes = span_pooled_codes.reshape(NSEG, D)
        return (infonce_objective(span_pooled_codes, partner_global_index, softmax_coolness), encoder_results)
    loss, pullback, encoder_results = jax.vjp(total_loss, params, inputs, has_aux=True)
    grad_params, grad_inputs = pullback(jnp.ones_like(loss))
    return (loss.reshape(1), encoder_results.reshape(TOKENS, D).astype(jnp.bfloat16), grad_inputs.reshape(TOKENS, D), grad_params[0], grad_params[1], grad_params[2], grad_params[3], grad_params[4], grad_params[5], grad_params[6], grad_params[7], grad_params[8], grad_params[9], grad_params[10], grad_params[11], grad_params[12])
```

```python
from functools import partial

import jax
import jax.numpy as jnp
from jax import lax
from jax.experimental import pallas as pl
from jax.experimental.pallas import tpu as pltpu
from jax.sharding import PartitionSpec as P

HEADS = 12
S_ROW = 8
BOTH = ("wide", "narrow")
BF = jnp.bfloat16
F32 = jnp.float32
HIGHEST = lax.Precision.HIGHEST


class Place:
    def __init__(self):
        self.wide, self.narrow = lax.axis_size("wide"), lax.axis_size("narrow")
        self.count = self.wide * self.narrow
        self.core = lax.axis_index("narrow")
        self.me = lax.axis_index("wide") * self.narrow + self.core
        bits = [self.narrow << i for i in range(self.wide.bit_length() - 1)]
        swapped = bits[:2][::-1] + bits[2:]
        self.steps = [(1, 1)] + list(zip(bits, swapped))

    def exchange(self, value, step):
        pairs = [(i, i ^ step[i % 2]) for i in range(self.count)]
        return lax.ppermute(value, BOTH, pairs)

    def bit(self, step):
        if step[0] == step[1]:
            return (self.me // step[0]) % 2
        return jnp.where(self.core == 0, (self.me // step[0]) % 2, (self.me // step[1]) % 2)


def scatter_step(total, step, place):
    half = total.shape[0] // 2
    bit = place.bit(step)
    keep = lax.dynamic_slice_in_dim(total, bit * half, half)
    send = lax.dynamic_slice_in_dim(total, (1 - bit) * half, half).astype(BF)
    return keep.astype(F32) + place.exchange(send, step).astype(F32)


def gather_step(part, step, place):
    bit = place.bit(step)
    got = place.exchange(part, step)
    return jnp.where(bit == 0, jnp.concatenate([part, got]), jnp.concatenate([got, part]))


def sum_everywhere(total, place):
    for step in place.steps:
        total = scatter_step(total, step, place)
    part = total.astype(BF)
    for step in place.steps[::-1]:
        part = gather_step(part, step, place)
    return part.astype(F32)


def sum_small(total, place):
    for step in place.steps:
        total = total + place.exchange(total, step)
    return total


def nt_dot(left, right, precision=None):
    return lax.dot_general(
        left, right, (((1,), (1,)), ((), ())), precision=precision, preferred_element_type=F32
    )


def contrast_kernel(block, me_ref, cool_ref, all_ref, own_ref, ids_row_ref, ids_col_ref, partner_row_ref,
                    partner_col_ref, partner_own_ref, loss_ref, grad_ref, sums_ref, rnorm_ref):
    count, width_all = all_ref.shape
    owned = own_ref.shape[0]
    widths = [width_all * f // 12 for f in (1, 2, 4, 8, 12)]
    warm = 1.0 / cool_ref[0]
    ones = jnp.ones((8, 1), F32)
    lane = lax.broadcasted_iota(jnp.int32, (1, 128), 1)
    first_mask = (lane < widths[0]).astype(F32)

    def spans():
        return [(0, 128, True), (0, 128, False), (128, widths[2], False),
                (widths[2], widths[3], False), (widths[3], widths[4], False)]

    squares = jnp.zeros((8, count), F32)
    for index, (lo, hi, masked) in enumerate(spans()):
        part = all_ref[:, lo:hi].astype(F32)
        if masked:
            part = part * first_mask
        term = nt_dot(jnp.ones((8, hi - lo), F32), part * part, HIGHEST)
        squares = term if index <= 1 else squares + term
        rnorm_ref[index] = lax.rsqrt(squares[:1] + 1e-06)
    sums_ref[...] = jnp.zeros_like(sums_ref)
    col = ids_row_ref[...]
    hits = jnp.zeros((1, 1), F32)
    for b in range(count // block):
        rows = pl.ds(b * block, block)
        diagonal = ids_col_ref[rows, :] == col
        positive = partner_col_ref[rows, :] == col
        gram = jnp.zeros((block, count), F32)
        norms = jnp.zeros((block, 1), F32)
        for index, (lo, hi, masked) in enumerate(spans()):
            mine = all_ref[rows, lo:hi]
            if masked:
                mine = mine * first_mask.astype(BF)
            wide = mine.astype(F32)
            term = nt_dot(mine, all_ref[:, lo:hi])
            square = jnp.sum(wide * wide, axis=1, keepdims=True)
            gram, norms = (term, square) if index <= 1 else (gram + term, norms + square)
            scores = gram * (lax.rsqrt(norms + 1e-06) * warm) * rnorm_ref[index]
            sums_ref[index] += jnp.sum(
                jnp.where(diagonal, 0.0, jnp.exp(scores)), axis=0, keepdims=True
            )
            hits += jnp.sum(
                jnp.sum(jnp.where(positive, scores, 0.0), axis=0, keepdims=True), axis=1, keepdims=True
            )
    logs = jnp.zeros((1, count), F32)
    for index in range(5):
        logs += jnp.log(sums_ref[index])
    loss_ref[...] = jnp.sum(logs, axis=1, keepdims=True) - hits

    first = me_ref[0] * owned
    orow = lax.broadcasted_iota(jnp.int32, (owned, count), 0) + first
    diagonal = orow == col
    picks = (partner_own_ref[...] == col).astype(F32) + (partner_row_ref[...] == orow).astype(F32)
    gram = jnp.zeros((owned, count), F32)
    norms = jnp.zeros((owned, 1), F32)
    weights, inverses = [], []
    for index, (lo, hi, masked) in enumerate(spans()):
        mine = own_ref[:, lo:hi]
        if masked:
            mine = mine * first_mask.astype(BF)
        wide = mine.astype(F32)
        term = nt_dot(mine, all_ref[:, lo:hi])
        square = jnp.sum(wide * wide, axis=1, keepdims=True)
        gram, norms = (term, square) if index <= 1 else (gram + term, norms + square)
        inverse = lax.rsqrt(norms + 1e-06)
        raised = jnp.where(diagonal, 0.0, jnp.exp(gram * (inverse * warm) * rnorm_ref[index]))
        own_sum = jnp.sum(raised, axis=1, keepdims=True)
        pull = raised * (1.0 / own_sum + 1.0 / sums_ref[index]) - picks
        weights.append(pull * (rnorm_ref[index] * warm))
        inverses.append(inverse)
    stack = jnp.concatenate(weights, axis=0)
    top = stack.astype(BF)
    rest = stack - top.astype(F32)
    middle = rest.astype(BF)
    low = (rest - middle.astype(F32)).astype(BF)
    parts = jnp.dot(
        jnp.concatenate([top, middle, low], axis=0), all_ref[...], preferred_element_type=F32
    )
    unit_grads = parts[: 5 * owned] + parts[5 * owned : 10 * owned] + parts[10 * owned :]
    total = jnp.zeros((owned, width_all), F32)
    column = lax.broadcasted_iota(jnp.int32, (owned, width_all), 1)
    embed = own_ref[...].astype(F32)
    for index in range(5):
        inside = column < widths[index]
        mine = jnp.where(inside, embed, 0.0)
        grad = jnp.where(inside, unit_grads[index * owned : (index + 1) * owned], 0.0)
        along = jnp.sum(mine * grad, axis=1, keepdims=True)
        inverse = inverses[index]
        total += inverse * grad - (inverse * inverse * inverse * along) * mine
    grad_ref[...] = total


def contrast(everyone, own, partner, coolness, place):
    count, width = everyone.shape
    owned = own.shape[0]
    block = min(count, 256)
    bits = len(place.steps)
    ids = jnp.arange(count, dtype=jnp.int32).reshape([2] * bits + [owned])
    ids = ids.transpose(list(range(bits))[::-1] + [bits]).reshape(count)
    partner_there = partner[ids]
    own_partner = lax.dynamic_slice_in_dim(partner, place.me * owned, owned)
    whole = pl.BlockSpec(memory_space=pltpu.VMEM)
    smem = pl.BlockSpec(memory_space=pltpu.SMEM)
    return pl.pallas_call(
        partial(contrast_kernel, block),
        out_shape=(
            jax.ShapeDtypeStruct((1, 1), F32),
            jax.ShapeDtypeStruct((owned, width), F32),
        ),
        in_specs=[smem, smem] + [whole] * 7,
        out_specs=(whole, whole),
        scratch_shapes=[pltpu.VMEM((5, 1, count), F32), pltpu.VMEM((5, 1, count), F32)],
        compiler_params=pltpu.CompilerParams(vmem_limit_bytes=56 * 1024 * 1024),
        name="contrast",
    )(place.me.reshape(1), coolness, everyone, own, ids[None, :], ids[:, None],
      partner_there[None, :], partner_there[:, None], own_partner[:, None])

def layer_norm(values, gain, shift):
    center = values - jnp.mean(values, axis=-1, keepdims=True)
    spread = jnp.mean(center * center, axis=-1, keepdims=True)
    return center * lax.rsqrt(spread + 1e-05) * gain + shift


def left_dot(left, right):
    return lax.dot_general(
        left, right, (((0,), (0,)), ((), ())), preferred_element_type=jnp.float32
    )


def right_dot(left, right):
    return lax.dot_general(
        left, right, (((1,), (1,)), ((), ())), preferred_element_type=jnp.float32
    )


def row_scores(packed, segment_row):
    length = packed.shape[0]
    width = packed.shape[1] // 3
    head_size = width // HEADS
    split = packed.reshape(length, 3, HEADS, head_size)
    raw = jnp.einsum(
        "qhd,khd->hqk", split[:, 0], split[:, 1], preferred_element_type=jnp.float32
    ) * head_size ** (-0.5)
    same = segment_row[:, None] == segment_row[None, :]
    return (split, jnp.where(same[None], raw, -1000000000.0))


def attend_row(pair):
    packed, segment_row = pair
    split, masked = row_scores(packed, segment_row)
    top = jnp.max(masked, axis=-1, keepdims=True)
    exps = jnp.exp(masked - top)
    summed = jnp.sum(exps, axis=-1, keepdims=True)
    probs = exps / summed
    mixed = jnp.einsum(
        "hqk,khd->qhd", probs.astype(jnp.bfloat16), split[:, 2], preferred_element_type=jnp.float32
    )
    return (mixed.reshape(packed.shape[0], -1).astype(jnp.bfloat16), top + jnp.log(summed))


def attend_back(group):
    packed, segment_row, log_total, grad_mixed = group
    length = packed.shape[0]
    width = packed.shape[1] // 3
    head_size = width // HEADS
    split, masked = row_scores(packed, segment_row)
    probs = jnp.exp(masked - log_total)
    grad_split = grad_mixed.reshape(length, HEADS, head_size)
    grad_probs = jnp.einsum(
        "qhd,khd->hqk", grad_split, split[:, 2], preferred_element_type=jnp.float32
    )
    grad_values = jnp.einsum(
        "hqk,qhd->khd", probs.astype(jnp.bfloat16), grad_split, preferred_element_type=jnp.float32
    )
    inner_sum = jnp.sum(probs * grad_probs, axis=-1, keepdims=True)
    grad_raw = (probs * (grad_probs - inner_sum)).astype(jnp.bfloat16)
    scale = head_size ** (-0.5)
    grad_queries = (
        jnp.einsum("hqk,khd->qhd", grad_raw, split[:, 1], preferred_element_type=jnp.float32)
        * scale
    )
    grad_keys = (
        jnp.einsum("hqk,qhd->khd", grad_raw, split[:, 0], preferred_element_type=jnp.float32)
        * scale
    )
    stacked = jnp.stack([grad_queries, grad_keys, grad_values], axis=1)
    return stacked.reshape(length, 3 * width).astype(jnp.bfloat16)


def on_device(
    incoming_activations,
    span_identifiers,
    partner_global_index,
    softmax_coolness,
    triple_kernel_panel,
    asking_shift,
    content_shift,
    mixer_result_kernel,
    mixer_result_shift,
    initial_standardize_scale,
    initial_standardize_shift,
    perceptron_entry_kernel,
    perceptron_entry_shift,
    perceptron_result_kernel,
    perceptron_result_shift,
    later_standardize_scale,
    later_standardize_shift,
):
    row_count, length = span_identifiers.shape
    width = incoming_activations.shape[1]
    seg_dev = row_count * S_ROW
    inputs = incoming_activations.astype(jnp.float32)
    zero_bias = jnp.zeros_like(asking_shift)
    projected = (
        jnp.dot(incoming_activations, triple_kernel_panel, preferred_element_type=jnp.float32)
        + jnp.concatenate([asking_shift, zero_bias, content_shift])
    ).astype(jnp.bfloat16)
    packed_rows = projected.reshape(row_count, length, 3 * width)
    mixed_rows, log_totals = lax.map(attend_row, (packed_rows, span_identifiers))
    mixed = mixed_rows.reshape(row_count * length, width)
    attn = (
        jnp.dot(mixed, mixer_result_kernel, preferred_element_type=jnp.float32) + mixer_result_shift
    )
    normed, first_back = jax.vjp(
        layer_norm, inputs + attn, initial_standardize_scale, initial_standardize_shift
    )
    normed_low = normed.astype(jnp.bfloat16)
    inner = (
        jnp.dot(normed_low, perceptron_entry_kernel, preferred_element_type=jnp.float32)
        + perceptron_entry_shift
    )
    active_full, gelu_back = jax.vjp(partial(jax.nn.gelu, approximate=False), inner)
    active = active_full.astype(jnp.bfloat16)
    outer = (
        jnp.dot(active, perceptron_result_kernel, preferred_element_type=jnp.float32)
        + perceptron_result_shift
    )
    output, second_back = jax.vjp(
        layer_norm, normed + outer, later_standardize_scale, later_standardize_shift
    )
    layer_out = output.astype(jnp.bfloat16)
    onehot = (span_identifiers[:, :, None] == jnp.arange(S_ROW)[None, None, :]).astype(jnp.float32)
    counts = jnp.sum(onehot, axis=1)
    pooled = (
        jnp.einsum(
            "rls,rld->rsd", onehot, output.reshape(row_count, length, width), precision=HIGHEST
        )
        / counts[..., None]
    )
    span_pooled_code = pooled.reshape(seg_dev, width).astype(jnp.bfloat16)
    place = Place()
    everyone = span_pooled_code
    for step in [(m, m) for m in (s[0] for s in place.steps[::-1])]:
        everyone = gather_step(everyone, step, place)
    loss, grad_embed = contrast(
        everyone, span_pooled_code, partner_global_index, softmax_coolness, place
    )
    per_segment = grad_embed.reshape(row_count, S_ROW, width) / counts[..., None]
    grad_output = jnp.einsum("rls,rsd->rld", onehot, per_segment, precision=HIGHEST).reshape(
        row_count * length, width
    )
    grad_second, grad_second_gain, grad_second_shift = second_back(grad_output)
    grad_outer = grad_second.astype(jnp.bfloat16)
    grad_outer_weight = left_dot(active, grad_outer)
    grad_outer_bias = jnp.sum(grad_outer.astype(jnp.float32), axis=0)
    grad_active = right_dot(grad_outer, perceptron_result_kernel)
    grad_inner = gelu_back(grad_active)[0].astype(jnp.bfloat16)
    grad_inner_weight = left_dot(normed_low, grad_inner)
    grad_inner_bias = jnp.sum(grad_inner.astype(jnp.float32), axis=0)
    grad_normed = grad_second + right_dot(grad_inner, perceptron_entry_kernel)
    grad_first, grad_first_gain, grad_first_shift = first_back(grad_normed)
    grad_attn = grad_first.astype(jnp.bfloat16)
    grad_merge_weight = left_dot(mixed, grad_attn)
    grad_merge_bias = jnp.sum(grad_attn.astype(jnp.float32), axis=0)
    grad_mixed = right_dot(grad_attn, mixer_result_kernel).astype(jnp.bfloat16)
    grad_packed = lax.map(
        attend_back,
        (packed_rows, span_identifiers, log_totals, grad_mixed.reshape(row_count, length, width)),
    )
    grad_packed = grad_packed.reshape(row_count * length, 3 * width)
    grad_attn_weight = left_dot(incoming_activations, grad_packed)
    bias_sums = jnp.sum(grad_packed.astype(jnp.float32), axis=0)
    grad_query_bias = bias_sums[:width]
    grad_value_bias = bias_sums[2 * width :]
    input_grad = grad_first + right_dot(grad_packed, triple_kernel_panel)
    small = [
        grad_query_bias, grad_value_bias, grad_merge_bias, grad_first_gain, grad_first_shift,
        grad_inner_bias, grad_outer_bias, grad_second_gain, grad_second_shift,
    ]
    sizes = [v.shape[0] for v in small]
    small = jnp.concatenate(small)
    small = jnp.pad(small, (0, -small.shape[0] % (place.count * 128))).reshape(place.count, -1)
    grad_outer_weight = sum_everywhere(grad_outer_weight, place)
    grad_inner_weight = sum_everywhere(grad_inner_weight, place)
    merged = sum_everywhere(jnp.concatenate([grad_attn_weight, grad_merge_weight], axis=1), place)
    grad_attn_weight, grad_merge_weight = merged[:, : 3 * width], merged[:, 3 * width :]
    small = sum_small(small, place).reshape(-1)
    cuts, at = [], 0
    for size in sizes:
        cuts.append(small[at : at + size])
        at += size
    (
        grad_query_bias, grad_value_bias, grad_merge_bias, grad_first_gain, grad_first_shift,
        grad_inner_bias, grad_outer_bias, grad_second_gain, grad_second_shift,
    ) = cuts
    return (
        loss.reshape(1),
        layer_out,
        input_grad,
        grad_attn_weight,
        grad_query_bias,
        grad_value_bias,
        grad_merge_weight,
        grad_merge_bias,
        grad_first_gain,
        grad_first_shift,
        grad_inner_weight,
        grad_inner_bias,
        grad_outer_weight,
        grad_outer_bias,
        grad_second_gain,
        grad_second_shift,
    )


def solution(mesh):
    return jax.shard_map(
        on_device,
        mesh=mesh,
        in_specs=(
            P(("wide", "narrow"), None),
            P(("wide", "narrow"), None),
            P(),
            P(),
            P(),
            P(),
            P(),
            P(),
            P(),
            P(),
            P(),
            P(),
            P(),
            P(),
            P(),
            P(),
            P(),
        ),
        out_specs=(
            P(),
            P(("wide", "narrow"), None),
            P(("wide", "narrow"), None),
            P(),
            P(),
            P(),
            P(),
            P(),
            P(),
            P(),
            P(),
            P(),
            P(),
            P(),
            P(),
            P(),
        ),
        check_vma=False,
    )
```

```python
from functools import partial

import jax
import jax.numpy as jnp
from jax import lax
from jax.experimental import pallas as pl
from jax.experimental.pallas import tpu as pltpu
from jax.sharding import PartitionSpec as P

HEADS = 12
S_ROW = 8
BOTH = ("wide", "narrow")
BF = jnp.bfloat16
F32 = jnp.float32


def tie(values, *others):
    return lax.optimization_barrier((values, others))[0]


class Place:
    def __init__(self):
        self.wide, self.narrow = lax.axis_size("wide"), lax.axis_size("narrow")
        self.count = self.wide * self.narrow
        self.core = lax.axis_index("narrow")
        self.me = lax.axis_index("wide") * self.narrow + self.core
        bits = [self.narrow << i for i in range(self.wide.bit_length() - 1)]
        self.own = [(1, 1)]
        self.pairs = [bits[i : i + 2] for i in range(0, len(bits), 2)]
        first, second = bits[0], bits[1]
        self.stages = [[(first, second)], [(second, first)]]
        self.stages += [self.combine(pair) for pair in self.pairs[1:]]
        self.spread = [self.combine(pair) for pair in self.pairs[::-1]] + [self.own]

    def combine(self, bits):
        if len(bits) == 1:
            return [(bits[0],) * 2]
        return [(m, m) for m in (bits[0], bits[1], bits[0] | bits[1])]

    def exchange(self, value, masks):
        pairs = [(i, i ^ masks[i % 2]) for i in range(self.count)]
        return lax.ppermute(value, BOTH, pairs)

    def index(self, stage):
        bit = lambda mask: (self.me // mask) % 2
        if len(stage) == 1:
            one, other = stage[0]
            return bit(one) if one == other else jnp.where(self.core == 0, bit(one), bit(other))
        return bit(stage[0][0]) + 2 * bit(stage[1][0])


class Sum:
    def __init__(self, place, send):
        self.place = place
        self.down, self.up = list(place.stages), list(place.stages[::-1]) + [place.own]
        self.sent = [send]
        self.got = [place.exchange(send, place.own[0])]
        self.stage = None

    def receive(self, order):
        got = [order.after(g) for g in self.got]
        if self.stage is None:
            return [self.kept] + got
        index = self.place.index(self.stage)
        parts = [self.kept] + got
        for bit in range(len(parts).bit_length() - 1):
            swap = (index // (1 << bit)) % 2 == 1
            parts = [
                jnp.where(swap, jnp.concatenate([b, a]), jnp.concatenate([a, b]))
                for a, b in zip(parts[::2], parts[1::2])
            ]
        return parts

    def advance(self, order):
        if not self.up:
            return
        terms = self.receive(order)
        if self.down:
            stage = self.down.pop(0)
            parts = len(stage) + 1
            index = self.place.index(stage)
            size = terms[0].shape[0] // parts
            cut = lambda at: sum(
                lax.dynamic_slice_in_dim(t, at * size, size).astype(F32) for t in terms
            )
            self.sent = [cut(index ^ (i + 1)).astype(BF) for i in range(len(stage))]
            self.kept = cut(index)
        else:
            self.stage = stage = self.up.pop(0)
            self.kept = sum(t.astype(F32) for t in terms).astype(BF) if len(terms) > 1 else terms[0]
            self.sent = [self.kept] * len(stage)
        self.got = [self.place.exchange(s, m) for s, m in zip(self.sent, stage)]
        order.done(*self.sent)


class Order:
    def __init__(self):
        self.last = ()

    def after(self, value):
        return tie(value, *self.last)

    def done(self, *values):
        self.last = values


def add_everywhere(total, place, order):
    for stage in [place.own] + place.spread[:-1]:
        got = [place.exchange(total, masks) for masks in stage]
        order.done(total)
        yield
        for part in got:
            total = total + order.after(part)
    order.done(total)
    yield total


def nt_dot(left, right):
    return lax.dot_general(left, right, (((1,), (1,)), ((), ())), preferred_element_type=F32)


def thirds(value):
    top = value.astype(BF)
    rest = value - top.astype(F32)
    middle = rest.astype(BF)
    return top, middle, (rest - middle.astype(F32)).astype(BF)


def column_sum(value):
    return jnp.sum(value, axis=0, keepdims=True)


def contrast_into(block, masks, me, cool_ref, pick_ref, there_ref, own_ref, partner_ref, loss_ref, grad_ref,
                  all_ref, sums_ref, rnorm_ref):
    count, width_all = all_ref.shape
    owned = own_ref.shape[0]
    for position, mask in enumerate(masks):
        at = pl.multiple_of((me ^ mask) * owned, owned)
        all_ref[pl.ds(at, owned), :] = there_ref[position * owned : (position + 1) * owned, :]
    widths = [width_all * f // 12 for f in (1, 2, 4, 8, 12)]
    warm = 1.0 / cool_ref[0]
    lane = lax.broadcasted_iota(jnp.int32, (1, 128), 1)
    first_mask = (lane < widths[0]).astype(F32)
    spans = [(0, 128, True), (0, 128, False), (128, widths[2], False), (widths[2], widths[3], False),
             (widths[3], widths[4], False)]
    partner = partner_ref[...][None, :]

    squares = jnp.zeros((8, count), F32)
    for index, (lo, hi, masked) in enumerate(spans):
        part = all_ref[:, lo:hi].astype(F32)
        if masked:
            part = part * first_mask
        term = sum(nt_dot(jnp.ones((8, hi - lo), BF), p) for p in thirds(part * part))
        squares = term if index <= 1 else squares + term
        rnorm_ref[index] = lax.rsqrt(squares[:1] + 1e-06)
    sums_ref[...] = jnp.zeros_like(sums_ref)
    hits = jnp.zeros((1, count), F32)
    for b in range(count // block):
        rows = pl.ds(b * block, block)
        row = lax.broadcasted_iota(jnp.int32, (block, count), 0) + b * block
        diagonal = row == lax.broadcasted_iota(jnp.int32, (block, count), 1)
        positive = row == partner
        gram = norms = None
        for index, (lo, hi, masked) in enumerate(spans):
            mine = all_ref[rows, lo:hi]
            if masked:
                mine = mine * first_mask.astype(BF)
            wide = mine.astype(F32)
            term = nt_dot(mine, all_ref[:, lo:hi])
            square = jnp.sum(wide * wide, axis=1, keepdims=True)
            gram, norms = (term, square) if index <= 1 else (gram + term, norms + square)
            scores = gram * (lax.rsqrt(norms + 1e-06) * warm) * rnorm_ref[index]
            sums_ref[index] += column_sum(jnp.where(diagonal, 0.0, jnp.exp(scores)))
            hits += column_sum(jnp.where(positive, scores, 0.0))
    logs = -hits
    for index in range(5):
        logs += jnp.log(sums_ref[index])
    loss_ref[...] = jnp.sum(logs, axis=1, keepdims=True)

    first = me * owned
    col = lax.broadcasted_iota(jnp.int32, (owned, count), 1)
    line = lax.broadcasted_iota(jnp.int32, (owned, count), 0)
    chosen = jnp.zeros((owned, count), jnp.int32)
    for i in range(owned):
        chosen = jnp.where(line == i, pick_ref[first + i], chosen)
    diagonal = line + first == col
    picks = (chosen == col).astype(F32) + (partner == line + first).astype(F32)
    gram = norms = None
    weights, inverses = [], []
    for index, (lo, hi, masked) in enumerate(spans):
        mine = own_ref[:, lo:hi]
        if masked:
            mine = mine * first_mask.astype(BF)
        wide = mine.astype(F32)
        term = nt_dot(mine, all_ref[:, lo:hi])
        square = jnp.sum(wide * wide, axis=1, keepdims=True)
        gram, norms = (term, square) if index <= 1 else (gram + term, norms + square)
        inverse = lax.rsqrt(norms + 1e-06)
        raised = jnp.where(diagonal, 0.0, jnp.exp(gram * (inverse * warm) * rnorm_ref[index]))
        own_sum = jnp.sum(raised, axis=1, keepdims=True)
        pull = raised * (1.0 / own_sum + 1.0 / sums_ref[index]) - picks
        weights.append(pull * (rnorm_ref[index] * warm))
        inverses.append(inverse)
    parts = jnp.dot(
        jnp.concatenate(thirds(jnp.concatenate(weights, axis=0)), axis=0), all_ref[...],
        preferred_element_type=F32,
    )
    unit_grads = parts[: 5 * owned] + parts[5 * owned : 10 * owned] + parts[10 * owned :]
    total = jnp.zeros((owned, width_all), F32)
    column = lax.broadcasted_iota(jnp.int32, (owned, width_all), 1)
    embed = own_ref[...].astype(F32)
    for index in range(5):
        inside = column < widths[index]
        mine = jnp.where(inside, embed, 0.0)
        grad = jnp.where(inside, unit_grads[index * owned : (index + 1) * owned], 0.0)
        along = jnp.sum(mine * grad, axis=1, keepdims=True)
        inverse = inverses[index]
        total += inverse * grad - (inverse * inverse * inverse * along) * mine
    grad_ref[...] = total


SEQUENCE = (
    "A0", "I", "B0", "A", "T", "C0", "A", "B", "A", "C", "B", "A", "X", "B", "C", "A", "B", "C", "A", "B", "A", "C",
    "B", "AF", "C", "B", "S0", "C", "S", "BF", "C", "S", "C", "SF", "CF",
)

VMEM_LIMIT = 58 * 1024 * 1024


def kernel_call(body, name, flops, nbytes, **options):
    return pl.pallas_call(
        body,
        compiler_params=pltpu.CompilerParams(vmem_limit_bytes=VMEM_LIMIT),
        cost_estimate=pl.CostEstimate(flops=flops, bytes_accessed=nbytes, transcendentals=0),
        name=name,
        **options,
    )


def fixed(shape):
    return pl.BlockSpec(shape, lambda *_: (0,) * len(shape))


def windows(length, step=128):
    return [(at, max(0, at - step), min(length, at + 2 * step)) for at in range(0, length, step)]


def segment_row(seg_ref):
    return seg_ref[pl.ds(pl.program_id(0), 1), :].astype(F32)


def segment_column(seg):
    return jnp.broadcast_to(seg, (128, seg.shape[1])).T


def masks_into(bias_ref, seg_ref):
    seg = segment_row(seg_ref)
    column = segment_column(seg)
    for index, (at, lo, hi) in enumerate(windows(seg.shape[1])):
        same = column[lo:hi, :] == seg[:, at : at + 128]
        bias = jnp.where(same, 0.0, -1e9)
        bias_ref[index, : hi - lo, :] = jnp.concatenate([bias, bias], axis=1)


def pair_stack(two):
    lane = lax.broadcasted_iota(jnp.int32, two.shape, 1)
    nought = jnp.zeros_like(two)
    half = two.shape[1] // 2
    return jnp.concatenate(
        [jnp.where(lane < half, two, nought), jnp.where(lane < half, nought, two)], axis=0
    )


def pair_merge(both):
    size = both.shape[1] // 2
    row = lax.broadcasted_iota(jnp.int32, (both.shape[0], size), 0)
    return jnp.where(row < both.shape[0] // 2, both[:, :size], both[:, size:])


def attend_kernel(x_ref, seg_ref, w_ref, bq_ref, bv_ref, wo_ref, bo_ref, gain_ref,
                  shift_ref, q_ref, k_ref, v_ref, mixed_t_ref, lse_ref, hat_ref, rstd_ref, low_ref,
                  x_t_ref, low_t_ref, bias_ref, mixed_ref):
    length, width = x_ref.shape
    x = x_ref[...]
    masks_into(bias_ref, seg_ref)
    q = jnp.dot(x, w_ref[:, :width], preferred_element_type=F32) + bq_ref[...][None, :]
    q_ref[...] = (q.astype(BF).astype(F32) * (width // HEADS) ** -0.5).astype(BF)
    k_ref[...] = jnp.dot(x, w_ref[:, width : 2 * width], preferred_element_type=F32).astype(BF)
    v_ref[...] = (jnp.dot(x, w_ref[:, 2 * width :], preferred_element_type=F32) + bv_ref[...][None, :]).astype(BF)
    jobs = [(pair, index) + win for pair in range(HEADS // 2) for index, win in enumerate(windows(length))]

    def scores(job):
        pair, index, at, lo, hi = job
        lanes = slice(pair * 128, pair * 128 + 128)
        stacked = pair_stack(q_ref[at : at + 128, lanes])
        return nt_dot(k_ref[lo:hi, lanes], stacked)

    ahead = scores(jobs[0])
    for number, job in enumerate(jobs):
        pair, index, at, lo, hi = job
        lanes = slice(pair * 128, pair * 128 + 128)
        raw = ahead
        if number + 1 < len(jobs):
            ahead = scores(jobs[number + 1])
        masked = raw + bias_ref[index, : hi - lo, :]
        top = jnp.max(masked, axis=0, keepdims=True)
        raised = jnp.exp(masked - top)
        total = jnp.sum(raised, axis=0, keepdims=True)
        log_total = top + jnp.log(total)
        for side in (0, 1):
            head = 2 * pair + side
            lse_ref[head // 4, head % 4 : head % 4 + 1, at : at + 128] = log_total[:, side * 128 : side * 128 + 128]
        if index == 0:
            values_t = v_ref[:, lanes].T
        both = jnp.dot(values_t[:, lo:hi], raised.astype(BF), preferred_element_type=F32)
        merged = pair_merge(both * (1.0 / total))
        mixed_t_ref[lanes, at : at + 128] = merged.astype(BF)
        mixed_ref[at : at + 128, lanes] = merged.T.astype(BF)
    attn = jnp.dot(mixed_ref[...], wo_ref[...], preferred_element_type=F32) + bo_ref[...][None, :]
    total = x.astype(F32) + attn
    center = total - jnp.mean(total, axis=1, keepdims=True)
    rstd = lax.rsqrt(jnp.mean(center * center, axis=1, keepdims=True) + 1e-05)
    hat = center * rstd
    hat_ref[...] = hat
    rstd_ref[...] = rstd
    low = (hat * gain_ref[...][None, :] + shift_ref[...][None, :]).astype(BF)
    low_ref[...] = low
    low_t_ref[...] = low.T
    x_t_ref[...] = x.T


def attend(x, seg, w, bq, bv, wo, bo, gain, shift):
    tokens, width = x.shape
    rows, length = seg.shape
    row_block = lambda *tail: pl.BlockSpec((length,) + tail, lambda r: (r, 0))
    return kernel_call(
        attend_kernel, "attend", 2 * tokens * width * width * 4 + 4 * tokens * 384 * width * 2, 20 << 20,
        grid=(rows,),
        in_specs=[
            row_block(width), fixed(seg.shape), fixed(w.shape), fixed(bq.shape), fixed(bv.shape), fixed(wo.shape), fixed(bo.shape),
            fixed(gain.shape), fixed(shift.shape),
        ],
        out_specs=(
            row_block(width), row_block(width), row_block(width),
            pl.BlockSpec((width, length), lambda r: (0, r)),
            pl.BlockSpec((HEADS // 4, 4, length), lambda r: (r, 0, 0)),
            row_block(width), row_block(1), row_block(width),
            pl.BlockSpec((width, length), lambda r: (0, r)), pl.BlockSpec((width, length), lambda r: (0, r)),
        ),
        out_shape=(
            jax.ShapeDtypeStruct((tokens, width), BF), jax.ShapeDtypeStruct((tokens, width), BF),
            jax.ShapeDtypeStruct((tokens, width), BF), jax.ShapeDtypeStruct((width, tokens), BF),
            jax.ShapeDtypeStruct((rows * HEADS // 4, 4, length), F32), jax.ShapeDtypeStruct((tokens, width), F32),
            jax.ShapeDtypeStruct((tokens, 1), F32), jax.ShapeDtypeStruct((tokens, width), BF),
            jax.ShapeDtypeStruct((width, tokens), BF), jax.ShapeDtypeStruct((width, tokens), BF),
        ),
        scratch_shapes=[
            pltpu.VMEM((length // 128, 384, 256), F32), pltpu.VMEM((length, width), BF),
        ],
    )(x, seg, w, bq, bv, wo, bo, gain, shift)


def gelu_parts(v):
    bell = jnp.exp(v * v * -0.5)
    t = 1.0 / (1.0 + (0.3275911 * 0.5 ** 0.5) * jnp.abs(v))
    poly = ((((0.5 * 1.061405429 * t - 0.5 * 1.453152027) * t + 0.5 * 1.421413741) * t
             - 0.5 * 0.284496736) * t + 0.5 * 0.254829592) * t
    tail = poly * bell
    share = jnp.where(v >= 0.0, 1.0 - tail, tail)
    return v * share, share + v * bell * 0.3989422804014327


def feed_kernel(chunk, hat_ref, low_ref, seg_ref, gain1_ref, shift1_ref, w1_ref, b1_ref, w2_ref, b2_ref,
                gain_ref, shift_ref, act_t_ref, slope_ref, hat2_ref, rstd2_ref, out_ref, embed_ref,
                pooled_ref):
    length, width = hat_ref.shape
    hidden = w1_ref.shape[1]
    low = low_ref[...]
    count = hidden // chunk

    def entry(i):
        return jnp.dot(low, w1_ref[:, i * chunk : (i + 1) * chunk], preferred_element_type=F32)

    total = hat_ref[...] * gain1_ref[...][None, :] + shift1_ref[...][None, :] + b2_ref[...][None, :]
    ahead = entry(0)
    for i in range(count):
        cols = slice(i * chunk, (i + 1) * chunk)
        inner = ahead + b1_ref[cols][None, :]
        if i + 1 < count:
            ahead = entry(i + 1)
        value, slope = gelu_parts(inner)
        value = value.astype(BF)
        act_t_ref[cols, :] = value.T
        slope_ref[:, cols] = slope.astype(BF)
        total += jnp.dot(value, w2_ref[cols, :], preferred_element_type=F32)
    center = total - jnp.mean(total, axis=1, keepdims=True)
    rstd = lax.rsqrt(jnp.mean(center * center, axis=1, keepdims=True) + 1e-05)
    hat = center * rstd
    hat2_ref[...] = hat
    rstd2_ref[...] = rstd
    out = hat * gain_ref[...][None, :] + shift_ref[...][None, :]
    out_ref[...] = out.astype(BF)
    number = lax.broadcasted_iota(jnp.int32, (S_ROW, length), 0)
    onehot = (segment_row(seg_ref) == number.astype(F32)).astype(F32)
    tokens_in = jnp.sum(onehot, axis=1, keepdims=True)
    onehot = onehot.astype(BF)
    sums = jnp.zeros((S_ROW, width), F32)
    for part in thirds(out):
        sums += jnp.dot(onehot, part, preferred_element_type=F32)
    row = pl.program_id(0)
    pooled_ref[pl.ds(row * S_ROW, S_ROW), :] = sums / tokens_in

    @pl.when(row == pl.num_programs(0) - 1)
    def _():
        embed_ref[...] = pooled_ref[...].astype(BF)


def feed(hat, low, seg, gain1, shift1, w1, b1, w2, b2, gain, shift):
    tokens, width = hat.shape
    rows, length = seg.shape
    hidden = w1.shape[1]
    row_block = lambda *tail: pl.BlockSpec((length,) + tail, lambda r: (r, 0))
    return kernel_call(
        partial(feed_kernel, 512), "feed", 4 * tokens * width * hidden, 30 << 20,
        grid=(rows,),
        in_specs=[
            row_block(width), row_block(width), fixed(seg.shape),
        ] + [fixed(a.shape) for a in (gain1, shift1, w1, b1, w2, b2, gain, shift)],
        out_specs=(
            pl.BlockSpec((hidden, length), lambda r: (0, r)), row_block(hidden), row_block(width), row_block(1),
            row_block(width),
            fixed((rows * S_ROW, width)),
        ),
        out_shape=(
            jax.ShapeDtypeStruct((hidden, tokens), BF), jax.ShapeDtypeStruct((tokens, hidden), BF),
            jax.ShapeDtypeStruct((tokens, width), F32), jax.ShapeDtypeStruct((tokens, 1), F32),
            jax.ShapeDtypeStruct((tokens, width), BF), jax.ShapeDtypeStruct((rows * S_ROW, width), BF),
        ),
        scratch_shapes=[pltpu.VMEM((rows * S_ROW, width), F32)],
    )(hat, low, seg, gain1, shift1, w1, b1, w2, b2, gain, shift)


def norm_back(grad, hat, rstd, gain):
    inside = grad * gain
    first = jnp.mean(inside, axis=1, keepdims=True)
    second = jnp.mean(inside * hat, axis=1, keepdims=True)
    return (inside - first - hat * second) * rstd


def copies(pairs, sems):
    return [pltpu.make_async_copy(src, dst, sems.at[i]) for i, (src, dst) in enumerate(pairs)]


def outer_back_kernel(block, masks, info_ref, pick_ref, cool_ref, there_ref, own_ref, partner_ref, seg_ref, rstd_ref,
                      gain_ref, act_t_ref, hat_hbm, loss_ref, gain_grad_ref, shift_grad_ref, bias_grad_ref,
                      send_ref, keep_ref, second_hbm, outer_hbm, embed_grad_ref, all_ref, sums_ref, rnorm_ref,
                      hat_ref, second_ref, outer_ref, sems):
    step = pl.program_id(0)
    rows, length = seg_ref.shape
    width = gain_ref.shape[0]
    load, *store = copies([(hat_hbm, hat_ref), (second_ref, second_hbm), (outer_ref, outer_hbm)], sems)

    @pl.when(step == 0)
    def _():
        load.start()
        contrast_into(block, masks, info_ref[0], cool_ref, pick_ref, there_ref, own_ref, partner_ref,
                      loss_ref, embed_grad_ref, all_ref, sums_ref, rnorm_ref)
        load.wait()
        gains, shifts, biases = [], [], []
        for row in range(rows):
            span = slice(row * length, (row + 1) * length)
            seg = seg_ref[row : row + 1, :].astype(F32)
            number = lax.broadcasted_iota(jnp.int32, (S_ROW, length), 0).astype(F32)
            tokens_in = jnp.sum((seg == number).astype(F32), axis=1, keepdims=True)
            each = embed_grad_ref[row * S_ROW : (row + 1) * S_ROW, :] / tokens_in
            stack = [p.astype(F32) for p in thirds(each)] + [jnp.zeros((128 - 3 * S_ROW, width), F32)]
            lane = lax.broadcasted_iota(jnp.int32, (length, 128), 1)
            pick = (lane < 3 * S_ROW) & ((lane % S_ROW).astype(F32) == segment_column(seg))
            grad = jnp.dot(
                pick.astype(BF), jnp.concatenate(stack).astype(BF), preferred_element_type=F32
            )
            hat = hat_ref[span, :]
            second = norm_back(grad, hat, rstd_ref[span, :], gain_ref[...][None, :])
            low = second.astype(BF)
            second_ref[span, :] = second
            outer_ref[span, :] = low
            gains.append(column_sum(grad * hat))
            shifts.append(column_sum(grad))
            biases.append(column_sum(low.astype(F32)))
        gain_grad_ref[...] = sum(gains)
        shift_grad_ref[...] = sum(shifts)
        bias_grad_ref[...] = sum(biases)
        for copy in store:
            copy.start()

    weight = jnp.dot(act_t_ref[...], outer_ref[...], preferred_element_type=F32).astype(BF)
    half = pl.num_programs(0) // 2

    @pl.when(step < half)
    def _():
        send_ref[...] = weight

    @pl.when(step >= half)
    def _():
        keep_ref[...] = weight

    @pl.when(step == pl.num_programs(0) - 1)
    def _():
        for copy in store:
            copy.wait()


def gather_embeds(own, place):
    there, masks = own, [0]
    for stage in place.spread:
        there = jnp.concatenate([there] + [place.exchange(there, pair) for pair in stage])
        masks = masks + [m ^ pair[0] for pair in stage for m in masks]
    return there, masks


def outer_back(own, partner, coolness, seg, hat, rstd, gain, act_t, place, chunk=512):
    there, masks = gather_embeds(own, place)
    owned, width = own.shape
    count = owned * len(masks)
    tokens = hat.shape[0]
    hidden = act_t.shape[0]
    steps = hidden // chunk
    half = steps // 2
    whole = lambda shape: pl.BlockSpec(shape, lambda i, *_: (0,) * len(shape))
    smem, hbm = pl.BlockSpec(memory_space=pltpu.SMEM), pl.BlockSpec(memory_space=pl.ANY)
    vector = jax.ShapeDtypeStruct((1, width), F32)
    turn = lambda i, info: (lax.rem(i + half * (1 - info[1]), steps), 0)
    return kernel_call(
        partial(outer_back_kernel, min(count, 256), masks), "outer_back", 2 * tokens * hidden * width, 20 << 20,
        grid_spec=pltpu.PrefetchScalarGridSpec(
            num_scalar_prefetch=1,
            grid=(steps,),
            in_specs=[smem, smem, whole(there.shape), whole(own.shape), whole(partner.shape), whole(seg.shape),
                      whole(rstd.shape), whole(gain.shape), pl.BlockSpec((chunk, tokens), turn), hbm],
            out_specs=(
                whole((1, 1)), whole((1, width)), whole((1, width)), whole((1, width)),
                pl.BlockSpec((chunk, width), lambda i, info: (jnp.minimum(i, half - 1), 0)),
                pl.BlockSpec((chunk, width), lambda i, info: (jnp.maximum(i - half, 0), 0)), hbm, hbm,
            ),
            scratch_shapes=[
                pltpu.VMEM((owned, width), F32), pltpu.VMEM((count, width), BF), pltpu.VMEM((5, 1, count), F32),
                pltpu.VMEM((5, 1, count), F32), pltpu.VMEM((tokens, width), F32),
                pltpu.VMEM((tokens, width), F32), pltpu.VMEM((tokens, width), BF), pltpu.SemaphoreType.DMA((3,)),
            ],
        ),
        out_shape=(
            jax.ShapeDtypeStruct((1, 1), F32), vector, vector, vector,
            jax.ShapeDtypeStruct((hidden // 2, width), BF), jax.ShapeDtypeStruct((hidden // 2, width), BF),
            jax.ShapeDtypeStruct((tokens, width), F32), jax.ShapeDtypeStruct((tokens, width), BF),
        ),
    )(jnp.stack([place.me, place.core]), partner, coolness, there, own, partner, seg, rstd, gain, act_t, hat)


def inner_back_kernel(rows, info_ref, outer_ref, low_t_ref, slope_ref, w2_ref, w1_ref, rstd_ref, gain_ref, second_hbm,
                      hat_hbm, mixed_t_hbm, wo_hbm, send_ref, keep_ref, bias_send_ref, bias_keep_ref, mixed_grad_ref,
                      merge_ref, gain_grad_ref, shift_grad_ref, merge_bias_ref, first_hbm,
                      normed_ref, second_ref, hat_ref, mixed_t_ref, wo_ref, sems, out_sems):
    step, last = pl.program_id(0), pl.num_programs(0) - 1
    length = outer_ref.shape[0] // rows
    loads = copies([(second_hbm, second_ref), (hat_hbm, hat_ref), (mixed_t_hbm, mixed_t_ref), (wo_hbm, wo_ref)], sems)

    @pl.when(step == 0)
    def _():
        for copy in loads:
            copy.start()

    active = nt_dot(outer_ref[...], w2_ref[...])
    inner = (active * slope_ref[...].astype(F32)).astype(BF)
    bias = column_sum(inner.astype(F32))
    weight = jnp.dot(low_t_ref[...], inner, preferred_element_type=F32).astype(BF)
    normed = nt_dot(inner, w1_ref[...])

    @pl.when(step <= last // 2)
    def _():
        bias_send_ref[...] = bias
        send_ref[...] = weight

    @pl.when(step > last // 2)
    def _():
        bias_keep_ref[...] = bias
        keep_ref[...] = weight

    @pl.when(step == 0)
    def _():
        normed_ref[...] = normed

    @pl.when(step > 0)
    def _():
        normed_ref[...] += normed

    @pl.when(step == last)
    def _():
        for copy in loads:
            copy.wait()
        gains, shifts, biases, merges, stores = [], [], [], [], []
        for row in range(rows):
            span = slice(row * length, (row + 1) * length)
            hat = hat_ref[span, :]
            grad = normed_ref[span, :] + second_ref[span, :]
            first = norm_back(grad, hat, rstd_ref[span, :], gain_ref[...][None, :])
            normed_ref[span, :] = first
            store = pltpu.make_async_copy(normed_ref.at[span, :], first_hbm.at[span, :], out_sems.at[row])
            store.start()
            stores.append(store)
            low = first.astype(BF)
            gains.append(column_sum(grad * hat))
            shifts.append(column_sum(grad))
            biases.append(column_sum(low.astype(F32)))
            mixed_grad_ref[span, :] = nt_dot(low, wo_ref[...]).astype(BF)
            merges.append(jnp.dot(mixed_t_ref[:, span], low, preferred_element_type=F32))
        merge_ref[...] = sum(merges).astype(BF)
        gain_grad_ref[...] = sum(gains)
        shift_grad_ref[...] = sum(shifts)
        merge_bias_ref[...] = sum(biases)
        for store in stores:
            store.wait()


def inner_back(outer, second, low_t, slope, w2, w1, hat, rstd, gain, mixed_t, wo, rows, place, chunk=512):
    tokens, width = outer.shape
    hidden = slope.shape[1]
    steps = hidden // chunk
    half = steps // 2
    whole = lambda shape: pl.BlockSpec(shape, lambda i, *_: (0,) * len(shape))
    hbm = pl.BlockSpec(memory_space=pl.ANY)
    turn = lambda i, info: lax.rem(i + half * (1 - info[1]), steps)
    early = lambda i: jnp.minimum(i, half - 1)
    late = lambda i: jnp.maximum(i - half, 0)
    vector = jax.ShapeDtypeStruct((1, width), F32)
    part = jax.ShapeDtypeStruct((half * width, chunk), BF)
    bias = jax.ShapeDtypeStruct((1, hidden // 2), F32)
    return kernel_call(
        partial(inner_back_kernel, rows), "inner_back", 6 * tokens * hidden * width, 40 << 20,
        grid_spec=pltpu.PrefetchScalarGridSpec(
            num_scalar_prefetch=1,
            grid=(steps,),
            in_specs=[
                whole(outer.shape), whole(low_t.shape),
                pl.BlockSpec((tokens, chunk), lambda i, info: (0, turn(i, info))),
                pl.BlockSpec((chunk, width), lambda i, info: (turn(i, info), 0)),
                pl.BlockSpec((width, chunk), lambda i, info: (0, turn(i, info))),
                whole(rstd.shape), whole(gain.shape), hbm, hbm, hbm, hbm,
            ],
            out_specs=(
                pl.BlockSpec((width, chunk), lambda i, info: (early(i), 0)),
                pl.BlockSpec((width, chunk), lambda i, info: (late(i), 0)),
                pl.BlockSpec((1, chunk), lambda i, info: (0, early(i))),
                pl.BlockSpec((1, chunk), lambda i, info: (0, late(i))),
                whole((tokens, width)), whole((width, width)), whole((1, width)), whole((1, width)),
                whole((1, width)), hbm,
            ),
            scratch_shapes=[
                pltpu.VMEM((tokens, width), F32), pltpu.VMEM((tokens, width), F32), pltpu.VMEM((tokens, width), F32),
                pltpu.VMEM(mixed_t.shape, BF), pltpu.VMEM(wo.shape, BF), pltpu.SemaphoreType.DMA((4,)),
                pltpu.SemaphoreType.DMA((rows,)),
            ],
        ),
        out_shape=(
            part, part, bias, bias, jax.ShapeDtypeStruct((tokens, width), BF),
            jax.ShapeDtypeStruct((width, width), BF), vector, vector, vector,
            jax.ShapeDtypeStruct((tokens, width), F32),
        ),
    )(jnp.stack([place.me, place.core]), outer, low_t, slope, w2, w1, rstd, gain, second, hat, mixed_t, wo)


def attend_back_kernel(pairs, core_ref, x_t_ref, merge_ref, seg_ref, lse_ref, q_ref, k_ref, v_ref, grad_ref,
                       dq_ref, dk_ref, dv_ref, send_ref, keep_ref, bq_ref, bv_ref,
                       bias_ref, k_sum_ref, v_sum_ref, weight_ref):
    row = pl.program_id(0)
    length = q_ref.shape[0]
    masks_into(bias_ref, seg_ref)
    k_sum_ref[...] = jnp.zeros_like(k_sum_ref)
    v_sum_ref[...] = jnp.zeros_like(v_sum_ref)
    jobs = [(pair, index) + win for pair in range(pairs) for index, win in enumerate(windows(length))]

    def begin(job):
        pair, index, at, lo, hi = job
        lanes = slice(pair * 128, pair * 128 + 128)
        query = pair_stack(q_ref[at : at + 128, lanes])
        grad = pair_stack(grad_ref[at : at + 128, lanes])
        return query, grad, nt_dot(k_ref[lo:hi, lanes], query), nt_dot(v_ref[lo:hi, lanes], grad)

    ahead = begin(jobs[0])
    for number, job in enumerate(jobs):
        pair, index, at, lo, hi = job
        lanes = slice(pair * 128, pair * 128 + 128)
        query, grad, raw, prob_grad = ahead
        if number + 1 < len(jobs):
            ahead = begin(jobs[number + 1])
        log_total = jnp.concatenate(
            [lse_ref[head // 4, head % 4 : head % 4 + 1, at : at + 128] for head in (2 * pair, 2 * pair + 1)],
            axis=1
        )
        probs = jnp.exp(raw + bias_ref[index, : hi - lo, :] - log_total)
        weighed = probs * prob_grad
        raw_grad = (weighed - probs * jnp.sum(weighed, axis=0, keepdims=True)).astype(BF)
        v_sum_ref[lo:hi, lanes] += jnp.dot(probs.astype(BF), grad, preferred_element_type=F32)
        k_sum_ref[lo:hi, lanes] += jnp.dot(raw_grad, query, preferred_element_type=F32)
        if index == 0:
            keys_t = k_ref[:, lanes].T
        both = jnp.dot(keys_t[:, lo:hi], raw_grad, preferred_element_type=F32)
        merged = pair_merge(both) * 0.125
        dq_ref[at : at + 128, lanes] = merged.T.astype(BF)
    dk_ref[...] = k_sum_ref[...].astype(BF)
    dv_ref[...] = v_sum_ref[...].astype(BF)

    @pl.when(row == 0)
    def _():
        for ref in (weight_ref, bq_ref, bv_ref):
            ref[...] = jnp.zeros_like(ref)

    bq_ref[...] += column_sum(dq_ref[...].astype(F32))
    bv_ref[...] += column_sum(dv_ref[...].astype(F32))
    for index, ref in enumerate((dq_ref, dk_ref, dv_ref)):
        weight_ref[index] += jnp.dot(x_t_ref[...], ref[...], preferred_element_type=F32)

    @pl.when(row == pl.num_programs(0) - 1)
    def _():
        for mine, first, second in ((0, keep_ref, send_ref), (1, send_ref, keep_ref)):
            @pl.when(core_ref[0] == mine)
            def _(first=first, second=second):
                first[...] = weight_ref[:2].astype(BF)
                second[0] = weight_ref[2].astype(BF)
                second[1] = merge_ref[...]


def attend_back(x_t, merge, seg, lse, q, k, v, grad, place):
    tokens, width = q.shape
    rows, length = seg.shape
    part = pl.BlockSpec((length, width), lambda r, core: (r, 0))
    whole = lambda shape: pl.BlockSpec(shape, lambda i, *_: (0,) * len(shape))
    groups = HEADS // 4
    half = jax.ShapeDtypeStruct((2, width, width), BF)
    return kernel_call(
        partial(attend_back_kernel, HEADS // 2), "attend_back",
        10 * tokens * 384 * width * 2 + 6 * tokens * width * width, 30 << 20,
        grid_spec=pltpu.PrefetchScalarGridSpec(
            num_scalar_prefetch=1,
            grid=(rows,),
            in_specs=[
                pl.BlockSpec((width, length), lambda r, core: (0, r)), whole(merge.shape), whole(seg.shape),
                pl.BlockSpec((groups, 4, length), lambda r, core: (r, 0, 0)), part, part, part, part,
            ],
            out_specs=(part, part, part, whole(half.shape), whole(half.shape), whole((1, width)), whole((1, width))),
            scratch_shapes=[
                pltpu.VMEM((length // 128, 384, 256), F32), pltpu.VMEM((length, width), F32),
                pltpu.VMEM((length, width), F32), pltpu.VMEM((3, width, width), F32),
            ],
        ),
        out_shape=(jax.ShapeDtypeStruct((tokens, width), BF),) * 3 + (half, half)
        + (jax.ShapeDtypeStruct((1, width), F32),) * 2,
    )(place.core.reshape(1), x_t, merge, seg, lse, q, k, v, grad)


def input_back_kernel(first_ref, *refs):
    *grads, w_ref, out_ref = refs
    width = first_ref.shape[1]
    total = first_ref[...]
    for index, ref in enumerate(grads):
        total += nt_dot(ref[...], w_ref[:, index * width : (index + 1) * width])
    out_ref[...] = total


def input_back(first, grads, w, block=512):
    tokens, width = first.shape
    rows = lambda cols: pl.BlockSpec((block, cols), lambda i: (i, 0))
    return kernel_call(
        input_back_kernel, "input_back", 6 * tokens * width * width, 15 << 20,
        grid=(tokens // block,),
        in_specs=[rows(width)] + [rows(g.shape[1]) for g in grads] + [fixed(w.shape)],
        out_specs=rows(width),
        out_shape=jax.ShapeDtypeStruct((tokens, width), F32),
    )(first, *grads, w)


def halves(place, count):
    def pick(mine):
        def index(i, core):
            lower = core[0] == (0 if mine else 1)
            return (jnp.where(lower, jnp.minimum(i, count - 1), jnp.maximum(i - count, 0)), 0)
        return index
    return pick(True), pick(False)


def finish_kernel(count, core_ref, kept_ref, got_ref, *out_refs):
    step = pl.program_id(0)
    lower = step < count
    mine = lower == (core_ref[0] == 0)
    if len(out_refs) == 1:
        @pl.when(mine)
        def _():
            out_refs[0][...] = kept_ref[...].astype(F32)

        @pl.when(jnp.logical_not(mine))
        def _():
            out_refs[0][...] = got_ref[...].astype(F32)
        return
    value = jnp.where(mine, kept_ref[...].astype(F32), got_ref[...].astype(F32))
    last = step == 2 * count - 1
    for ref, when in zip(out_refs, (jnp.logical_not(last), last)):
        @pl.when(when)
        def _(ref=ref):
            ref[...] = value


def finish(one, order, place, rows, outs):
    while one.up:
        one.advance(order)
    kept, got = one.kept, order.after(one.got[0])
    half, cols = kept.shape
    count = half // rows
    first, second = halves(place, count)
    result = kernel_call(
        partial(finish_kernel, count), "finish", 0, half * cols * 12,
        grid_spec=pltpu.PrefetchScalarGridSpec(
            num_scalar_prefetch=1,
            grid=(2 * count,),
            in_specs=[pl.BlockSpec((rows, cols), first), pl.BlockSpec((rows, cols), second)],
            out_specs=[pl.BlockSpec(block, index) for _, block, index in outs],
        ),
        out_shape=[jax.ShapeDtypeStruct(shape, F32) for shape, _, _ in outs],
    )(place.core.reshape(1), kept, got)
    order.done(*result)
    return result


def on_device(
    incoming_activations,
    span_identifiers,
    partner_global_index,
    softmax_coolness,
    triple_kernel_panel,
    asking_shift,
    content_shift,
    mixer_result_kernel,
    mixer_result_shift,
    initial_standardize_scale,
    initial_standardize_shift,
    perceptron_entry_kernel,
    perceptron_entry_shift,
    perceptron_result_kernel,
    perceptron_result_shift,
    later_standardize_scale,
    later_standardize_shift,
):
    rows, length = span_identifiers.shape
    width = incoming_activations.shape[1]
    hidden = perceptron_entry_kernel.shape[1]
    place, order = Place(), Order()
    seg = span_identifiers
    q, k, v, mixed_t, lse, hat1, rstd1, low, x_t, low_t = attend(
        incoming_activations, seg, triple_kernel_panel, asking_shift, content_shift, mixer_result_kernel,
        mixer_result_shift, initial_standardize_scale, initial_standardize_shift,
    )
    act_t, slope, hat2, rstd2, layer_out, embed = feed(
        hat1, low, seg, initial_standardize_scale, initial_standardize_shift, perceptron_entry_kernel,
        perceptron_entry_shift, perceptron_result_kernel, perceptron_result_shift, later_standardize_scale,
        later_standardize_shift,
    )
    (
        loss, gain2_grad, shift2_grad, outer_bias_grad, outer_send, outer_keep, second, outer,
    ) = outer_back(
        embed, partner_global_index, softmax_coolness, seg, hat2, rstd2, later_standardize_scale, act_t, place
    )
    order.done(outer)
    got, sums = {}, {}

    def inner():
        (
            got["inner_send"], got["inner_keep"], got["bias_theirs"], got["bias_ours"], got["mixed_grad"],
            got["merge"], *got["norm"], got["first"],
        ) = inner_back(
            order.after(outer), second, low_t, slope, perceptron_result_kernel, perceptron_entry_kernel, hat1,
            rstd1, initial_standardize_scale, mixed_t, mixer_result_kernel, rows, place,
        )
        order.done(got["mixed_grad"])

    def attention():
        *got["grads"], got["rest_send"], got["rest_keep"], got["q_bias"], got["v_bias"] = attend_back(
            x_t, got["merge"], seg, lse, q, k, v, order.after(got["mixed_grad"]), place
        )
        order.done(got["rest_send"])

    def inputs():
        got["input_grad"] = input_back(order.after(got["first"]), got["grads"], triple_kernel_panel)
        order.done(got["input_grad"])

    def start(name, send, keep):
        sums[name] = Sum(place, order.after(send))
        sums[name].kept = keep
        order.done(*sums[name].sent)

    def start_outer():
        start("A", outer_send, outer_keep)

    def start_inner():
        start("B", got["inner_send"], got["inner_keep"])

    def start_rest():
        start("C", got["rest_send"].reshape(2 * width, width), got["rest_keep"].reshape(2 * width, width))

    def start_small():
        bias = [got["bias_ours"], got["bias_theirs"]]
        inner_bias = jnp.where(place.core == 0, jnp.concatenate(bias, 1), jnp.concatenate(bias[::-1], 1))
        gain1, shift1, merge_bias = got["norm"]
        parts = [got["q_bias"], got["v_bias"], merge_bias, gain1, shift1, inner_bias]
        parts += [outer_bias_grad, gain2_grad, shift2_grad]
        small = jnp.concatenate(parts, axis=1).reshape(-1, 128)
        sums["S"] = add_everywhere(order.after(small), place, order)
        next(sums["S"])

    def small_step():
        got["small"] = next(sums["S"])

    def finish_small():
        while got.get("small") is None:
            small_step()

    def finish_outer():
        got["outer_grad"], = finish(sums["A"], order, place, 384, [((hidden, width), (384, width), lambda i, c: (i, 0))])

    def finish_inner():
        got["inner_grad"], = finish(sums["B"], order, place, width, [((width, hidden), (width, 512), lambda i, c: (0, i))])

    def finish_rest():
        got["panel_grad"], got["merge_grad"] = finish(sums["C"], order, place, width, [
            ((width, 3 * width), (width, width), lambda i, c: (0, jnp.minimum(i, 2))),
            ((width, width), (width, width), lambda i, c: (0, 0)),
        ])

    actions = dict(
        I=inner, T=attention, X=inputs, A0=start_outer, B0=start_inner,
        C0=start_rest, S0=start_small, S=small_step, SF=finish_small, A=lambda: sums["A"].advance(order),
        B=lambda: sums["B"].advance(order), C=lambda: sums["C"].advance(order),
        AF=finish_outer, BF=finish_inner, CF=finish_rest,
    )
    for action in SEQUENCE:
        actions[action]()
    widths = [width] * 5 + [hidden] + [width] * 3
    small, cuts = got["small"].reshape(-1), []
    for size in widths:
        cuts.append(small[:size])
        small = small[size:]
    (
        query_bias_grad, value_bias_grad, merge_bias_grad, gain1_grad, shift1_grad,
        inner_bias_grad, outer_bias_grad, gain2_grad, shift2_grad,
    ) = cuts
    return (
        loss.reshape(1),
        layer_out,
        got["input_grad"],
        got["panel_grad"],
        query_bias_grad,
        value_bias_grad,
        got["merge_grad"],
        merge_bias_grad,
        gain1_grad,
        shift1_grad,
        got["inner_grad"],
        inner_bias_grad,
        got["outer_grad"],
        outer_bias_grad,
        gain2_grad,
        shift2_grad,
    )


def solution(mesh):
    return jax.shard_map(
        on_device,
        mesh=mesh,
        in_specs=(
            P(("wide", "narrow"), None),
            P(("wide", "narrow"), None),
            P(),
            P(),
            P(),
            P(),
            P(),
            P(),
            P(),
            P(),
            P(),
            P(),
            P(),
            P(),
            P(),
            P(),
            P(),
        ),
        out_specs=(
            P(),
            P(("wide", "narrow"), None),
            P(("wide", "narrow"), None),
            P(),
            P(),
            P(),
            P(),
            P(),
            P(),
            P(),
            P(),
            P(),
            P(),
            P(),
            P(),
            P(),
        ),
        check_vma=False,
    )
```

```python
from functools import partial

import jax
import jax.numpy as jnp
from jax import lax
from jax.experimental import pallas as pl
from jax.experimental.pallas import tpu as pltpu
from jax.sharding import PartitionSpec as P

HEADS = 12
S_ROW = 8
BOTH = ("wide", "narrow")
BF = jnp.bfloat16
F32 = jnp.float32


def tie(values, *others):
    return lax.optimization_barrier((values, others))[0]


class Place:
    def __init__(self):
        self.wide, self.narrow = lax.axis_size("wide"), lax.axis_size("narrow")
        self.count = self.wide * self.narrow
        self.core = lax.axis_index("narrow")
        self.me = lax.axis_index("wide") * self.narrow + self.core
        bits = [self.narrow << i for i in range(self.wide.bit_length() - 1)]
        self.own = [(1, 1)]
        self.pairs = [bits[i : i + 2] for i in range(0, len(bits), 2)]
        first, second = bits[0], bits[1]
        self.stages = [[(first, second)], [(second, first)]]
        self.stages += [self.combine(pair) for pair in self.pairs[1:]]
        self.spread = [self.combine(pair) for pair in self.pairs[::-1]] + [self.own]

    def combine(self, bits):
        if len(bits) == 1:
            return [(bits[0],) * 2]
        return [(m, m) for m in (bits[0], bits[1], bits[0] | bits[1])]

    def exchange(self, value, masks):
        pairs = [(i, i ^ masks[i % 2]) for i in range(self.count)]
        return lax.ppermute(value, BOTH, pairs)

    def index(self, stage):
        bit = lambda mask: (self.me // mask) % 2
        if len(stage) == 1:
            one, other = stage[0]
            return bit(one) if one == other else jnp.where(self.core == 0, bit(one), bit(other))
        return bit(stage[0][0]) + 2 * bit(stage[1][0])


class Sum:
    def __init__(self, place, send):
        self.place = place
        self.down, self.up = list(place.stages), list(place.stages[::-1]) + [place.own]
        self.sent = [send]
        self.got = [place.exchange(send, place.own[0])]
        self.stage = None

    def receive(self, order):
        got = [order.after(g) for g in self.got]
        if self.stage is None:
            return [self.kept] + got
        index = self.place.index(self.stage)
        parts = [self.kept] + got
        if len(parts) == 2:
            return [jnp.where(index == 0, jnp.concatenate(parts), jnp.concatenate(parts[::-1]))]
        ordered = []
        for at in range(len(parts)):
            value = parts[0]
            for i in range(1, len(parts)):
                value = jnp.where(index == at ^ i, parts[i], value)
            ordered.append(value)
        return [jnp.concatenate(ordered)]

    def advance(self, order):
        if not self.up:
            return
        terms = self.receive(order)
        if self.down:
            stage = self.down.pop(0)
            parts = len(stage) + 1
            index = self.place.index(stage)
            size = terms[0].shape[0] // parts
            cut = lambda at: sum(
                lax.dynamic_slice_in_dim(t, at * size, size).astype(F32) for t in terms
            )
            self.sent = [cut(index ^ (i + 1)).astype(BF) for i in range(len(stage))]
            self.kept = cut(index)
        else:
            self.stage = stage = self.up.pop(0)
            self.kept = sum(t.astype(F32) for t in terms).astype(BF) if len(terms) > 1 else terms[0]
            self.sent = [self.kept] * len(stage)
        self.got = [self.place.exchange(s, m) for s, m in zip(self.sent, stage)]
        order.done(*self.sent)


class Order:
    def __init__(self):
        self.last = ()

    def after(self, value):
        return tie(value, *self.last)

    def done(self, *values):
        self.last = values


def add_everywhere(total, place, order):
    for stage in [place.own] + place.spread[:-1]:
        got = [place.exchange(total, masks) for masks in stage]
        order.done(total)
        yield
        for part in got:
            total = total + order.after(part)
    order.done(total)
    yield total


def nt_dot(left, right):
    return lax.dot_general(left, right, (((1,), (1,)), ((), ())), preferred_element_type=F32)


def tn_dot(left, right):
    return lax.dot_general(left, right, (((0,), (0,)), ((), ())), preferred_element_type=F32)


def thirds(value):
    top = value.astype(BF)
    rest = value - top.astype(F32)
    middle = rest.astype(BF)
    return top, middle, (rest - middle.astype(F32)).astype(BF)


def column_sum(value):
    return jnp.sum(value, axis=0, keepdims=True)


def contrast_into(block, masks, me, cool_ref, pick_ref, there_ref, own_ref, partner_ref, loss_ref, grad_ref,
                  all_ref, sums_ref, rnorm_ref):
    count, width_all = all_ref.shape
    owned = own_ref.shape[0]
    for position, mask in enumerate(masks):
        at = pl.multiple_of((me ^ mask) * owned, owned)
        all_ref[pl.ds(at, owned), :] = there_ref[position * owned : (position + 1) * owned, :]
    widths = [width_all * f // 12 for f in (1, 2, 4, 8, 12)]
    warm = 1.0 / cool_ref[0]
    lane = lax.broadcasted_iota(jnp.int32, (1, 128), 1)
    first_mask = (lane < widths[0]).astype(F32)
    spans = [(0, 128, True), (0, 128, False), (128, widths[2], False), (widths[2], widths[3], False),
             (widths[3], widths[4], False)]
    partner = partner_ref[...][None, :]

    squares = jnp.zeros((8, count), F32)
    for index, (lo, hi, masked) in enumerate(spans):
        part = all_ref[:, lo:hi].astype(F32)
        if masked:
            part = part * first_mask
        term = sum(nt_dot(jnp.ones((8, hi - lo), BF), p) for p in thirds(part * part))
        squares = term if index <= 1 else squares + term
        rnorm_ref[index] = lax.rsqrt(squares[:1] + 1e-06)
    sums_ref[...] = jnp.zeros_like(sums_ref)
    hits = jnp.zeros((1, count), F32)
    for b in range(count // block):
        rows = pl.ds(b * block, block)
        row = lax.broadcasted_iota(jnp.int32, (block, count), 0) + b * block
        diagonal = row == lax.broadcasted_iota(jnp.int32, (block, count), 1)
        positive = row == partner
        gram = norms = None
        for index, (lo, hi, masked) in enumerate(spans):
            mine = all_ref[rows, lo:hi]
            if masked:
                mine = mine * first_mask.astype(BF)
            wide = mine.astype(F32)
            term = nt_dot(mine, all_ref[:, lo:hi])
            square = jnp.sum(wide * wide, axis=1, keepdims=True)
            gram, norms = (term, square) if index <= 1 else (gram + term, norms + square)
            scores = gram * (lax.rsqrt(norms + 1e-06) * warm) * rnorm_ref[index]
            sums_ref[index] += column_sum(jnp.where(diagonal, 0.0, jnp.exp(scores)))
            hits += column_sum(jnp.where(positive, scores, 0.0))
    logs = -hits
    for index in range(5):
        logs += jnp.log(sums_ref[index])
    loss_ref[...] = jnp.sum(logs, axis=1, keepdims=True)

    first = me * owned
    col = lax.broadcasted_iota(jnp.int32, (owned, count), 1)
    line = lax.broadcasted_iota(jnp.int32, (owned, count), 0)
    chosen = jnp.zeros((owned, count), jnp.int32)
    for i in range(owned):
        chosen = jnp.where(line == i, pick_ref[first + i], chosen)
    diagonal = line + first == col
    picks = (chosen == col).astype(F32) + (partner == line + first).astype(F32)
    gram = norms = None
    weights, inverses = [], []
    for index, (lo, hi, masked) in enumerate(spans):
        mine = own_ref[:, lo:hi]
        if masked:
            mine = mine * first_mask.astype(BF)
        wide = mine.astype(F32)
        term = nt_dot(mine, all_ref[:, lo:hi])
        square = jnp.sum(wide * wide, axis=1, keepdims=True)
        gram, norms = (term, square) if index <= 1 else (gram + term, norms + square)
        inverse = lax.rsqrt(norms + 1e-06)
        raised = jnp.where(diagonal, 0.0, jnp.exp(gram * (inverse * warm) * rnorm_ref[index]))
        own_sum = jnp.sum(raised, axis=1, keepdims=True)
        pull = raised * (1.0 / own_sum + 1.0 / sums_ref[index]) - picks
        weights.append(pull * (rnorm_ref[index] * warm))
        inverses.append(inverse)
    parts = jnp.dot(
        jnp.concatenate(thirds(jnp.concatenate(weights, axis=0)), axis=0), all_ref[...],
        preferred_element_type=F32,
    )
    unit_grads = parts[: 5 * owned] + parts[5 * owned : 10 * owned] + parts[10 * owned :]
    total = jnp.zeros((owned, width_all), F32)
    column = lax.broadcasted_iota(jnp.int32, (owned, width_all), 1)
    embed = own_ref[...].astype(F32)
    for index in range(5):
        inside = column < widths[index]
        mine = jnp.where(inside, embed, 0.0)
        grad = jnp.where(inside, unit_grads[index * owned : (index + 1) * owned], 0.0)
        along = jnp.sum(mine * grad, axis=1, keepdims=True)
        inverse = inverses[index]
        total += inverse * grad - (inverse * inverse * inverse * along) * mine
    grad_ref[...] = total


SEQUENCE = (
    "A0", "A", "I", "A", "B0", "B", "A", "T", "A", "B", "C0", "A", "C", "B", "A", "C", "B", "A",
    "C", "B", "C", "B", "X", "C", "S0", "B", "C", "S", "A", "BF", "S", "AF", "C", "SF", "C", "CF",
)

VMEM_LIMIT = 58 * 1024 * 1024


def kernel_call(body, name, flops, nbytes, **options):
    return pl.pallas_call(
        body,
        compiler_params=pltpu.CompilerParams(vmem_limit_bytes=VMEM_LIMIT),
        cost_estimate=pl.CostEstimate(flops=flops, bytes_accessed=nbytes, transcendentals=0),
        name=name,
        **options,
    )


def fixed(shape):
    return pl.BlockSpec(shape, lambda *_: (0,) * len(shape))


def windows(length, step=128):
    return [(at, max(0, at - step), min(length, at + 2 * step)) for at in range(0, length, step)]


def segment_row(seg_ref):
    return seg_ref[pl.ds(pl.program_id(0), 1), :].astype(F32)


def segment_column(seg):
    return jnp.broadcast_to(seg, (128, seg.shape[1])).T


def masks_into(bias_ref, seg_ref):
    seg = segment_row(seg_ref)
    column = segment_column(seg)
    for index, (at, lo, hi) in enumerate(windows(seg.shape[1])):
        same = column[lo:hi, :] == seg[:, at : at + 128]
        bias = jnp.where(same, 0.0, -1e9)
        bias_ref[index, : hi - lo, :] = jnp.concatenate([bias, bias], axis=1)


def pair_stack(two):
    lane = lax.broadcasted_iota(jnp.int32, two.shape, 1)
    nought = jnp.zeros_like(two)
    half = two.shape[1] // 2
    return jnp.concatenate(
        [jnp.where(lane < half, two, nought), jnp.where(lane < half, nought, two)], axis=0
    )


def pair_merge(both):
    size = both.shape[1] // 2
    row = lax.broadcasted_iota(jnp.int32, (both.shape[0], size), 0)
    return jnp.where(row < both.shape[0] // 2, both[:, :size], both[:, size:])


def attend_kernel(x_ref, seg_ref, w_ref, bq_ref, bv_ref, wo_ref, bo_ref, gain_ref,
                  shift_ref, q_ref, k_ref, v_ref, mixed_t_ref, lse_ref, hat_ref, rstd_ref, low_ref,
                  x_t_ref, low_t_ref, bias_ref, mixed_ref):
    length, width = x_ref.shape
    x = x_ref[...]
    masks_into(bias_ref, seg_ref)
    q = jnp.dot(x, w_ref[:, :width], preferred_element_type=F32) + bq_ref[...][None, :]
    q_ref[...] = (q.astype(BF).astype(F32) * (width // HEADS) ** -0.5).astype(BF)
    k_ref[...] = jnp.dot(x, w_ref[:, width : 2 * width], preferred_element_type=F32).astype(BF)
    v_ref[...] = (jnp.dot(x, w_ref[:, 2 * width :], preferred_element_type=F32) + bv_ref[...][None, :]).astype(BF)
    jobs = [(pair, index) + win for pair in range(HEADS // 2) for index, win in enumerate(windows(length))]

    def scores(job):
        pair, index, at, lo, hi = job
        lanes = slice(pair * 128, pair * 128 + 128)
        stacked = pair_stack(q_ref[at : at + 128, lanes])
        return nt_dot(k_ref[lo:hi, lanes], stacked)

    ahead = scores(jobs[0])
    for number, job in enumerate(jobs):
        pair, index, at, lo, hi = job
        lanes = slice(pair * 128, pair * 128 + 128)
        raw = ahead
        if number + 1 < len(jobs):
            ahead = scores(jobs[number + 1])
        masked = raw + bias_ref[index, : hi - lo, :]
        top = jnp.max(masked, axis=0, keepdims=True)
        raised = jnp.exp(masked - top)
        total = jnp.sum(raised, axis=0, keepdims=True)
        log_total = top + jnp.log(total)
        for side in (0, 1):
            head = 2 * pair + side
            lse_ref[head // 4, head % 4 : head % 4 + 1, at : at + 128] = log_total[:, side * 128 : side * 128 + 128]
        both = tn_dot((raised * (1.0 / total)).astype(BF), v_ref[lo:hi, lanes])
        lane = lax.broadcasted_iota(jnp.int32, (128, 128), 1)
        merged = jnp.where(lane < 64, both[:128], both[128:])
        mixed_ref[at : at + 128, lanes] = merged.astype(BF)
        mixed_t_ref[lanes, at : at + 128] = merged.T.astype(BF)
    attn = jnp.dot(mixed_ref[...], wo_ref[...], preferred_element_type=F32) + bo_ref[...][None, :]
    total = x.astype(F32) + attn
    center = total - jnp.mean(total, axis=1, keepdims=True)
    rstd = lax.rsqrt(jnp.mean(center * center, axis=1, keepdims=True) + 1e-05)
    hat = center * rstd
    hat_ref[...] = hat
    rstd_ref[...] = rstd
    low = (hat * gain_ref[...][None, :] + shift_ref[...][None, :]).astype(BF)
    low_ref[...] = low
    low_t_ref[...] = low.T
    x_t_ref[...] = x.T


def attend(x, seg, w, bq, bv, wo, bo, gain, shift):
    tokens, width = x.shape
    rows, length = seg.shape
    row_block = lambda *tail: pl.BlockSpec((length,) + tail, lambda r: (r, 0))
    return kernel_call(
        attend_kernel, "attend", 2 * tokens * width * width * 4 + 4 * tokens * 384 * width * 2, 20 << 20,
        grid=(rows,),
        in_specs=[
            row_block(width), fixed(seg.shape), fixed(w.shape), fixed(bq.shape), fixed(bv.shape), fixed(wo.shape), fixed(bo.shape),
            fixed(gain.shape), fixed(shift.shape),
        ],
        out_specs=(
            row_block(width), row_block(width), row_block(width),
            pl.BlockSpec((width, length), lambda r: (0, r)),
            pl.BlockSpec((HEADS // 4, 4, length), lambda r: (r, 0, 0)),
            row_block(width), row_block(1), row_block(width),
            pl.BlockSpec((width, length), lambda r: (0, r)), pl.BlockSpec((width, length), lambda r: (0, r)),
        ),
        out_shape=(
            jax.ShapeDtypeStruct((tokens, width), BF), jax.ShapeDtypeStruct((tokens, width), BF),
            jax.ShapeDtypeStruct((tokens, width), BF), jax.ShapeDtypeStruct((width, tokens), BF),
            jax.ShapeDtypeStruct((rows * HEADS // 4, 4, length), F32), jax.ShapeDtypeStruct((tokens, width), F32),
            jax.ShapeDtypeStruct((tokens, 1), F32), jax.ShapeDtypeStruct((tokens, width), BF),
            jax.ShapeDtypeStruct((width, tokens), BF), jax.ShapeDtypeStruct((width, tokens), BF),
        ),
        scratch_shapes=[
            pltpu.VMEM((length // 128, 384, 256), F32), pltpu.VMEM((length, width), BF),
        ],
    )(x, seg, w, bq, bv, wo, bo, gain, shift)


def gelu_parts(v):
    bell = jnp.exp(v * v * -0.5)
    t = 1.0 / (1.0 + (0.3275911 * 0.5 ** 0.5) * jnp.abs(v))
    poly = ((((0.5 * 1.061405429 * t - 0.5 * 1.453152027) * t + 0.5 * 1.421413741) * t
             - 0.5 * 0.284496736) * t + 0.5 * 0.254829592) * t
    tail = poly * bell
    share = jnp.where(v >= 0.0, 1.0 - tail, tail)
    return v * share, share + v * bell * 0.3989422804014327


def feed_kernel(chunk, hat_ref, low_ref, seg_ref, gain1_ref, shift1_ref, w1_ref, b1_ref, w2_ref, b2_ref,
                gain_ref, shift_ref, act_t_ref, slope_ref, hat2_ref, rstd2_ref, out_ref, embed_ref,
                pooled_ref, value_ref):
    length, width = hat_ref.shape
    hidden = w1_ref.shape[1]
    low = low_ref[...]
    count = hidden // chunk

    def entry(i):
        return jnp.dot(low, w1_ref[:, i * chunk : (i + 1) * chunk], preferred_element_type=F32)

    total = hat_ref[...] * gain1_ref[...][None, :] + shift1_ref[...][None, :] + b2_ref[...][None, :]
    ahead = entry(0)
    for i in range(count):
        cols = slice(i * chunk, (i + 1) * chunk)
        inner = ahead + b1_ref[cols][None, :]
        if i + 1 < count:
            ahead = entry(i + 1)
        value, slope = gelu_parts(inner)
        value = value.astype(BF)
        act_t_ref[cols, :] = value.T
        slope_ref[:, cols] = slope.astype(BF)
        value_ref[:, cols] = value
    total += jnp.dot(value_ref[...], w2_ref[...], preferred_element_type=F32)
    center = total - jnp.mean(total, axis=1, keepdims=True)
    rstd = lax.rsqrt(jnp.mean(center * center, axis=1, keepdims=True) + 1e-05)
    hat = center * rstd
    hat2_ref[...] = hat
    rstd2_ref[...] = rstd
    out = hat * gain_ref[...][None, :] + shift_ref[...][None, :]
    out_ref[...] = out.astype(BF)
    number = lax.broadcasted_iota(jnp.int32, (S_ROW, length), 0)
    onehot = (segment_row(seg_ref) == number.astype(F32)).astype(F32)
    tokens_in = jnp.sum(onehot, axis=1, keepdims=True)
    onehot = onehot.astype(BF)
    sums = jnp.zeros((S_ROW, width), F32)
    for part in thirds(out):
        sums += jnp.dot(onehot, part, preferred_element_type=F32)
    row = pl.program_id(0)
    pooled_ref[pl.ds(row * S_ROW, S_ROW), :] = sums / tokens_in

    @pl.when(row == pl.num_programs(0) - 1)
    def _():
        embed_ref[...] = pooled_ref[...].astype(BF)


def feed(hat, low, seg, gain1, shift1, w1, b1, w2, b2, gain, shift):
    tokens, width = hat.shape
    rows, length = seg.shape
    hidden = w1.shape[1]
    row_block = lambda *tail: pl.BlockSpec((length,) + tail, lambda r: (r, 0))
    return kernel_call(
        partial(feed_kernel, 1024), "feed", 4 * tokens * width * hidden, 30 << 20,
        grid=(rows,),
        in_specs=[
            row_block(width), row_block(width), fixed(seg.shape),
        ] + [fixed(a.shape) for a in (gain1, shift1, w1, b1, w2, b2, gain, shift)],
        out_specs=(
            pl.BlockSpec((hidden, length), lambda r: (0, r)), row_block(hidden), row_block(width), row_block(1),
            row_block(width),
            fixed((rows * S_ROW, width)),
        ),
        out_shape=(
            jax.ShapeDtypeStruct((hidden, tokens), BF), jax.ShapeDtypeStruct((tokens, hidden), BF),
            jax.ShapeDtypeStruct((tokens, width), F32), jax.ShapeDtypeStruct((tokens, 1), F32),
            jax.ShapeDtypeStruct((tokens, width), BF), jax.ShapeDtypeStruct((rows * S_ROW, width), BF),
        ),
        scratch_shapes=[pltpu.VMEM((rows * S_ROW, width), F32), pltpu.VMEM((length, hidden), BF)],
    )(hat, low, seg, gain1, shift1, w1, b1, w2, b2, gain, shift)


def norm_back(grad, hat, rstd, gain):
    inside = grad * gain
    first = jnp.mean(inside, axis=1, keepdims=True)
    second = jnp.mean(inside * hat, axis=1, keepdims=True)
    return (inside - first - hat * second) * rstd


def line_into(ref, vectors):
    ref[...] = jnp.zeros_like(ref)
    at = 0
    for vector in vectors:
        ref[:, at : at + vector.shape[1]] = vector
        at += vector.shape[1]


def copies(pairs, sems):
    return [pltpu.make_async_copy(src, dst, sems.at[i]) for i, (src, dst) in enumerate(pairs)]


def outer_back_kernel(block, masks, info_ref, pick_ref, cool_ref, there_ref, own_ref, partner_ref, seg_ref, rstd_ref,
                      gain_ref, act_t_ref, hat_hbm, loss_ref, line_ref, send_ref,
                      keep_ref, second_hbm, outer_hbm, embed_grad_ref, all_ref, sums_ref, rnorm_ref,
                      hat_ref, second_ref, outer_ref, sems):
    step = pl.program_id(0)
    rows, length = seg_ref.shape
    width = gain_ref.shape[0]
    load, *store = copies([(hat_hbm, hat_ref), (second_ref, second_hbm), (outer_ref, outer_hbm)], sems)

    @pl.when(step == 0)
    def _():
        load.start()
        contrast_into(block, masks, info_ref[0], cool_ref, pick_ref, there_ref, own_ref, partner_ref,
                      loss_ref, embed_grad_ref, all_ref, sums_ref, rnorm_ref)
        load.wait()
        gains, shifts, biases = [], [], []
        for row in range(rows):
            span = slice(row * length, (row + 1) * length)
            seg = seg_ref[row : row + 1, :].astype(F32)
            number = lax.broadcasted_iota(jnp.int32, (S_ROW, length), 0).astype(F32)
            tokens_in = jnp.sum((seg == number).astype(F32), axis=1, keepdims=True)
            each = embed_grad_ref[row * S_ROW : (row + 1) * S_ROW, :] / tokens_in
            stack = [p.astype(F32) for p in thirds(each)] + [jnp.zeros((128 - 3 * S_ROW, width), F32)]
            lane = lax.broadcasted_iota(jnp.int32, (length, 128), 1)
            pick = (lane < 3 * S_ROW) & ((lane % S_ROW).astype(F32) == segment_column(seg))
            grad = jnp.dot(
                pick.astype(BF), jnp.concatenate(stack).astype(BF), preferred_element_type=F32
            )
            hat = hat_ref[span, :]
            second = norm_back(grad, hat, rstd_ref[span, :], gain_ref[...][None, :])
            low = second.astype(BF)
            second_ref[span, :] = second
            outer_ref[span, :] = low
            gains.append(column_sum(grad * hat))
            shifts.append(column_sum(grad))
            biases.append(column_sum(low.astype(F32)))
        line_into(line_ref, [sum(biases), sum(gains), sum(shifts)])
        for copy in store:
            copy.start()

    weight = jnp.dot(act_t_ref[...], outer_ref[...], preferred_element_type=F32).astype(BF)
    half = pl.num_programs(0) // 2

    @pl.when(step < half)
    def _():
        send_ref[...] = weight

    @pl.when(step >= half)
    def _():
        keep_ref[...] = weight

    @pl.when(step == pl.num_programs(0) - 1)
    def _():
        for copy in store:
            copy.wait()


def gather_embeds(own, place):
    there, masks = own, [0]
    for stage in place.spread:
        there = jnp.concatenate([there] + [place.exchange(there, pair) for pair in stage])
        masks = masks + [m ^ pair[0] for pair in stage for m in masks]
    return there, masks


def outer_back(own, partner, coolness, seg, hat, rstd, gain, act_t, place, chunk=768):
    there, masks = gather_embeds(own, place)
    owned, width = own.shape
    count = owned * len(masks)
    tokens = hat.shape[0]
    hidden = act_t.shape[0]
    steps = hidden // chunk
    half = steps // 2
    whole = lambda shape: pl.BlockSpec(shape, lambda i, *_: (0,) * len(shape))
    smem, hbm = pl.BlockSpec(memory_space=pltpu.SMEM), pl.BlockSpec(memory_space=pl.ANY)
    vmem = pl.BlockSpec(memory_space=pltpu.VMEM)
    turn = lambda i, info: (lax.rem(i + half * (1 - info[1]), steps), 0)
    return kernel_call(
        partial(outer_back_kernel, min(count, 256), masks), "outer_back", 2 * tokens * hidden * width, 20 << 20,
        grid_spec=pltpu.PrefetchScalarGridSpec(
            num_scalar_prefetch=1,
            grid=(steps,),
            in_specs=[smem, smem, vmem, vmem, whole(partner.shape), whole(seg.shape),
                      whole(rstd.shape), whole(gain.shape), pl.BlockSpec((chunk, tokens), turn), hbm],
            out_specs=(
                whole((1, 1)), whole((1, hidden)),
                pl.BlockSpec((chunk, width), lambda i, info: (jnp.minimum(i, half - 1), 0)),
                pl.BlockSpec((chunk, width), lambda i, info: (jnp.maximum(i - half, 0), 0)), hbm, hbm,
            ),
            scratch_shapes=[
                pltpu.VMEM((owned, width), F32), pltpu.VMEM((count, width), BF), pltpu.VMEM((5, 1, count), F32),
                pltpu.VMEM((5, 1, count), F32), pltpu.VMEM((tokens, width), F32),
                pltpu.VMEM((tokens, width), F32), pltpu.VMEM((tokens, width), BF), pltpu.SemaphoreType.DMA((3,)),
            ],
        ),
        out_shape=(
            jax.ShapeDtypeStruct((1, 1), F32), jax.ShapeDtypeStruct((1, hidden), F32),
            jax.ShapeDtypeStruct((hidden // 2, width), BF), jax.ShapeDtypeStruct((hidden // 2, width), BF),
            jax.ShapeDtypeStruct((tokens, width), F32), jax.ShapeDtypeStruct((tokens, width), BF),
        ),
    )(jnp.stack([place.me, place.core]), partner, coolness, there, own, partner, seg, rstd, gain, act_t, hat)


def inner_back_kernel(rows, info_ref, outer_ref, low_t_ref, slope_ref, w2_ref, w1_ref, rstd_ref, gain_ref, second_hbm,
                      hat_hbm, mixed_t_hbm, wo_hbm, send_ref, keep_ref, bias_ref, mixed_grad_ref, merge_ref, line_ref,
                      first_hbm,
                      normed_ref, second_ref, hat_ref, mixed_t_ref, wo_ref, sems, out_sems):
    step, last = pl.program_id(0), pl.num_programs(0) - 1
    length = outer_ref.shape[0] // rows
    loads = copies([(second_hbm, second_ref), (hat_hbm, hat_ref), (mixed_t_hbm, mixed_t_ref), (wo_hbm, wo_ref)], sems)

    @pl.when(step == 0)
    def _():
        for copy in loads:
            copy.start()

    active = nt_dot(outer_ref[...], w2_ref[...])
    inner = (active * slope_ref[...].astype(F32)).astype(BF)
    bias_ref[...] = column_sum(inner.astype(F32))
    weight = jnp.dot(low_t_ref[...], inner, preferred_element_type=F32).astype(BF)
    normed = nt_dot(inner, w1_ref[...])

    @pl.when(step <= last // 2)
    def _():
        send_ref[...] = weight

    @pl.when(step > last // 2)
    def _():
        keep_ref[...] = weight

    @pl.when(step == 0)
    def _():
        normed_ref[...] = normed

    @pl.when(step > 0)
    def _():
        normed_ref[...] += normed

    @pl.when(step == last)
    def _():
        for copy in loads:
            copy.wait()
        gains, shifts, biases, merges, stores = [], [], [], [], []
        for row in range(rows):
            span = slice(row * length, (row + 1) * length)
            hat = hat_ref[span, :]
            grad = normed_ref[span, :] + second_ref[span, :]
            first = norm_back(grad, hat, rstd_ref[span, :], gain_ref[...][None, :])
            normed_ref[span, :] = first
            store = pltpu.make_async_copy(normed_ref.at[span, :], first_hbm.at[span, :], out_sems.at[row])
            store.start()
            stores.append(store)
            low = first.astype(BF)
            gains.append(column_sum(grad * hat))
            shifts.append(column_sum(grad))
            biases.append(column_sum(low.astype(F32)))
            mixed_grad_ref[span, :] = nt_dot(low, wo_ref[...]).astype(BF)
            merges.append(jnp.dot(mixed_t_ref[:, span], low, preferred_element_type=F32))
        merge_ref[...] = sum(merges).astype(BF)
        line_into(line_ref, [sum(biases), sum(gains), sum(shifts)])
        for store in stores:
            store.wait()


def inner_back(outer, second, low_t, slope, w2, w1, hat, rstd, gain, mixed_t, wo, rows, place, chunk=512):
    tokens, width = outer.shape
    hidden = slope.shape[1]
    steps = hidden // chunk
    half = steps // 2
    whole = lambda shape: pl.BlockSpec(shape, lambda i, *_: (0,) * len(shape))
    hbm = pl.BlockSpec(memory_space=pl.ANY)
    turn = lambda i, info: lax.rem(i + half * (1 - info[1]), steps)
    early = lambda i: jnp.minimum(i, half - 1)
    late = lambda i: jnp.maximum(i - half, 0)
    line = jax.ShapeDtypeStruct((1, hidden), F32)
    part = jax.ShapeDtypeStruct((half * width, chunk), BF)
    return kernel_call(
        partial(inner_back_kernel, rows), "inner_back", 6 * tokens * hidden * width, 40 << 20,
        grid_spec=pltpu.PrefetchScalarGridSpec(
            num_scalar_prefetch=1,
            grid=(steps,),
            in_specs=[
                whole(outer.shape), whole(low_t.shape),
                pl.BlockSpec((tokens, chunk), lambda i, info: (0, turn(i, info))),
                pl.BlockSpec((chunk, width), lambda i, info: (turn(i, info), 0)),
                pl.BlockSpec((width, chunk), lambda i, info: (0, turn(i, info))),
                whole(rstd.shape), whole(gain.shape), hbm, hbm, hbm, hbm,
            ],
            out_specs=(
                pl.BlockSpec((width, chunk), lambda i, info: (early(i), 0)),
                pl.BlockSpec((width, chunk), lambda i, info: (late(i), 0)),
                pl.BlockSpec((1, chunk), lambda i, info: (0, turn(i, info))),
                whole((tokens, width)), whole((width, width)), whole((1, hidden)), hbm,
            ),
            scratch_shapes=[
                pltpu.VMEM((tokens, width), F32), pltpu.VMEM((tokens, width), F32), pltpu.VMEM((tokens, width), F32),
                pltpu.VMEM(mixed_t.shape, BF), pltpu.VMEM(wo.shape, BF), pltpu.SemaphoreType.DMA((4,)),
                pltpu.SemaphoreType.DMA((rows,)),
            ],
        ),
        out_shape=(
            part, part, line, jax.ShapeDtypeStruct((tokens, width), BF),
            jax.ShapeDtypeStruct((width, width), BF), line,
            jax.ShapeDtypeStruct((tokens, width), F32),
        ),
    )(jnp.stack([place.me, place.core]), outer, low_t, slope, w2, w1, rstd, gain, second, hat, mixed_t, wo)


def attend_back_kernel(pairs, core_ref, x_t_ref, merge_ref, seg_ref, lse_ref, q_ref, k_ref, v_ref, grad_ref,
                       dq_ref, dk_ref, dv_ref, send_ref, keep_ref, line_ref,
                       bias_ref, k_sum_ref, v_sum_ref, weight_ref):
    row = pl.program_id(0)
    length = q_ref.shape[0]
    masks_into(bias_ref, seg_ref)
    k_sum_ref[...] = jnp.zeros_like(k_sum_ref)
    v_sum_ref[...] = jnp.zeros_like(v_sum_ref)
    jobs = [(pair, index) + win for pair in range(pairs) for index, win in enumerate(windows(length))]

    def begin(job):
        pair, index, at, lo, hi = job
        lanes = slice(pair * 128, pair * 128 + 128)
        query = pair_stack(q_ref[at : at + 128, lanes])
        grad = pair_stack(grad_ref[at : at + 128, lanes])
        return query, grad, nt_dot(k_ref[lo:hi, lanes], query), nt_dot(v_ref[lo:hi, lanes], grad)

    ahead = begin(jobs[0])
    for number, job in enumerate(jobs):
        pair, index, at, lo, hi = job
        lanes = slice(pair * 128, pair * 128 + 128)
        query, grad, raw, prob_grad = ahead
        if number + 1 < len(jobs):
            ahead = begin(jobs[number + 1])
        log_total = jnp.concatenate(
            [lse_ref[head // 4, head % 4 : head % 4 + 1, at : at + 128] for head in (2 * pair, 2 * pair + 1)],
            axis=1
        )
        probs = jnp.exp(raw + bias_ref[index, : hi - lo, :] - log_total)
        weighed = probs * prob_grad
        raw_grad = (weighed - probs * jnp.sum(weighed, axis=0, keepdims=True)).astype(BF)
        v_sum_ref[lo:hi, lanes] += jnp.dot(probs.astype(BF), grad, preferred_element_type=F32)
        k_sum_ref[lo:hi, lanes] += jnp.dot(raw_grad, query, preferred_element_type=F32)
        if index == 0:
            keys_t = k_ref[:, lanes].T
        both = jnp.dot(keys_t[:, lo:hi], raw_grad, preferred_element_type=F32)
        merged = pair_merge(both) * 0.125
        dq_ref[at : at + 128, lanes] = merged.T.astype(BF)
    dk_ref[...] = k_sum_ref[...].astype(BF)
    dv_ref[...] = v_sum_ref[...].astype(BF)

    @pl.when(row == 0)
    def _():
        for ref in (weight_ref, line_ref):
            ref[...] = jnp.zeros_like(ref)

    width = dq_ref.shape[1]
    line_ref[:, :width] += column_sum(dq_ref[...].astype(F32))
    line_ref[:, width : 2 * width] += column_sum(dv_ref[...].astype(F32))
    for index, ref in enumerate((dq_ref, dk_ref, dv_ref)):
        weight_ref[index] += jnp.dot(x_t_ref[...], ref[...], preferred_element_type=F32)

    @pl.when(row == pl.num_programs(0) - 1)
    def _():
        for mine, first, second in ((0, keep_ref, send_ref), (1, send_ref, keep_ref)):
            @pl.when(core_ref[0] == mine)
            def _(first=first, second=second):
                first[...] = weight_ref[:2].astype(BF)
                second[0] = weight_ref[2].astype(BF)
                second[1] = merge_ref[...]


def attend_back(x_t, merge, seg, lse, q, k, v, grad, place):
    tokens, width = q.shape
    rows, length = seg.shape
    part = pl.BlockSpec((length, width), lambda r, core: (r, 0))
    whole = lambda shape: pl.BlockSpec(shape, lambda i, *_: (0,) * len(shape))
    groups = HEADS // 4
    half = jax.ShapeDtypeStruct((2, width, width), BF)
    return kernel_call(
        partial(attend_back_kernel, HEADS // 2), "attend_back",
        10 * tokens * 384 * width * 2 + 6 * tokens * width * width, 30 << 20,
        grid_spec=pltpu.PrefetchScalarGridSpec(
            num_scalar_prefetch=1,
            grid=(rows,),
            in_specs=[
                pl.BlockSpec((width, length), lambda r, core: (0, r)), whole(merge.shape), whole(seg.shape),
                pl.BlockSpec((groups, 4, length), lambda r, core: (r, 0, 0)), part, part, part, part,
            ],
            out_specs=(part, part, part, whole(half.shape), whole(half.shape), whole((1, 4 * width))),
            scratch_shapes=[
                pltpu.VMEM((length // 128, 384, 256), F32), pltpu.VMEM((length, width), F32),
                pltpu.VMEM((length, width), F32), pltpu.VMEM((3, width, width), F32),
            ],
        ),
        out_shape=(jax.ShapeDtypeStruct((tokens, width), BF),) * 3
        + (half, half, jax.ShapeDtypeStruct((1, 4 * width), F32)),
    )(place.core.reshape(1), x_t, merge, seg, lse, q, k, v, grad)


def input_back_kernel(first_ref, *refs):
    *grads, w_ref, out_ref = refs
    width = first_ref.shape[1]
    total = first_ref[...]
    for index, ref in enumerate(grads):
        total += nt_dot(ref[...], w_ref[:, index * width : (index + 1) * width])
    out_ref[...] = total


def input_back(first, grads, w, block=512):
    tokens, width = first.shape
    rows = lambda cols: pl.BlockSpec((block, cols), lambda i: (i, 0))
    return kernel_call(
        input_back_kernel, "input_back", 6 * tokens * width * width, 15 << 20,
        grid=(tokens // block,),
        in_specs=[rows(width)] + [rows(g.shape[1]) for g in grads] + [fixed(w.shape)],
        out_specs=rows(width),
        out_shape=jax.ShapeDtypeStruct((tokens, width), F32),
    )(first, *grads, w)


def finish_kernel(plan, core_ref, kept_ref, got_ref, *refs):
    *outs, out_ref, out_sems = refs
    core = core_ref[0]
    rows = out_ref.shape[1]
    stores = []
    for index, (kind, at, target) in enumerate(plan):
        span = slice(at * rows, (at + 1) * rows)
        kept, got = kept_ref[span, :].astype(F32), got_ref[span, :].astype(F32)
        own = core == (0 if kind == "low" else 1)
        out_ref[index] = kept if kind == "kept" else got if kind == "got" else jnp.where(own, kept, got)
        stores.append(pltpu.make_async_copy(out_ref.at[index], target(outs, core), out_sems.at[index]))
        stores[-1].start()
    for store in stores:
        store.wait()


def finish(one, order, place, rows, plan, shapes):
    while one.up:
        one.advance(order)
    kept, got = one.kept, order.after(one.got[0])
    half, cols = kept.shape
    hbm = pl.BlockSpec(memory_space=pl.ANY)
    result = kernel_call(
        partial(finish_kernel, plan), "finish", 0, half * cols * 12,
        in_specs=[pl.BlockSpec(memory_space=pltpu.SMEM)] + [pl.BlockSpec(memory_space=pltpu.VMEM)] * 2,
        out_specs=[hbm] * len(shapes),
        out_shape=[jax.ShapeDtypeStruct(shape, F32) for shape in shapes],
        scratch_shapes=[
            pltpu.VMEM((len(plan), rows, cols), F32), pltpu.SemaphoreType.DMA((len(plan),)),
        ],
    )(place.core.reshape(1), kept, got)
    order.done(*result)
    return result


def on_device(
    incoming_activations,
    span_identifiers,
    partner_global_index,
    softmax_coolness,
    triple_kernel_panel,
    asking_shift,
    content_shift,
    mixer_result_kernel,
    mixer_result_shift,
    initial_standardize_scale,
    initial_standardize_shift,
    perceptron_entry_kernel,
    perceptron_entry_shift,
    perceptron_result_kernel,
    perceptron_result_shift,
    later_standardize_scale,
    later_standardize_shift,
):
    rows, length = span_identifiers.shape
    width = incoming_activations.shape[1]
    hidden = perceptron_entry_kernel.shape[1]
    place, order = Place(), Order()
    seg = span_identifiers
    q, k, v, mixed_t, lse, hat1, rstd1, low, x_t, low_t = attend(
        incoming_activations, seg, triple_kernel_panel, asking_shift, content_shift, mixer_result_kernel,
        mixer_result_shift, initial_standardize_scale, initial_standardize_shift,
    )
    act_t, slope, hat2, rstd2, layer_out, embed = feed(
        hat1, low, seg, initial_standardize_scale, initial_standardize_shift, perceptron_entry_kernel,
        perceptron_entry_shift, perceptron_result_kernel, perceptron_result_shift, later_standardize_scale,
        later_standardize_shift,
    )
    (
        loss, second_line, outer_send, outer_keep, second, outer,
    ) = outer_back(
        embed, partner_global_index, softmax_coolness, seg, hat2, rstd2, later_standardize_scale, act_t, place
    )
    order.done(outer)
    got, sums, blocks = {}, {}, hidden // 512 // 2

    def inner():
        (
            got["inner_send"], got["inner_keep"], got["inner_line"], got["mixed_grad"], got["merge"],
            got["first_line"], got["first"],
        ) = inner_back(
            order.after(outer), second, low_t, slope, perceptron_result_kernel, perceptron_entry_kernel, hat1,
            rstd1, initial_standardize_scale, mixed_t, mixer_result_kernel, rows, place,
        )
        order.done(got["mixed_grad"])

    def attention():
        *got["grads"], got["rest_send"], got["rest_keep"], got["rest_line"] = attend_back(
            x_t, got["merge"], seg, lse, q, k, v, order.after(got["mixed_grad"]), place
        )
        order.done(got["rest_send"])

    def inputs():
        got["input_grad"] = input_back(order.after(got["first"]), got["grads"], triple_kernel_panel)
        order.done(got["input_grad"])

    def start(name, send, keep):
        sums[name] = Sum(place, order.after(send))
        sums[name].kept = keep
        order.done(*sums[name].sent)

    def start_outer():
        start("A", outer_send, outer_keep)

    def start_inner():
        start("B", got["inner_send"], got["inner_keep"])

    def start_rest():
        start("C", got["rest_send"].reshape(2 * width, width), got["rest_keep"].reshape(2 * width, width))

    def start_small():
        lines = [second_line, got["inner_line"], got["first_line"], got["rest_line"]]
        small = jnp.concatenate(lines, axis=0)
        sums["S"] = add_everywhere(order.after(small), place, order)
        next(sums["S"])

    def small_step():
        got["small"] = next(sums["S"])

    def finish_small():
        while got.get("small") is None:
            small_step()

    def finish_outer():
        def lines(at, upper):
            def target(outs, core):
                half = core if upper else 1 - core
                return outs[0].at[pl.ds(pl.multiple_of((half * 4 + at) * (hidden // 8), hidden // 8), hidden // 8), :]
            return target
        plan = [("kept", i, lines(i, True)) for i in range(4)] + [("got", i, lines(i, False)) for i in range(4)]
        got["outer_grad"], = finish(sums["A"], order, place, hidden // 8, plan, [(hidden, width)])

    def finish_inner():
        def columns(at, upper):
            def target(outs, core):
                half = core if upper else 1 - core
                return outs[0].at[:, pl.ds(pl.multiple_of((half * blocks + at) * 512, 512), 512)]
            return target
        plan = [("kept", i, columns(i, True)) for i in range(blocks)]
        plan += [("got", i, columns(i, False)) for i in range(blocks)]
        got["inner_grad"], = finish(sums["B"], order, place, width, plan, [(width, hidden)])

    def finish_rest():
        whole = lambda outs, core: outs[1]
        column = lambda at: lambda outs, core: outs[0].at[:, pl.ds(pl.multiple_of(at(core) * width, width), width)]
        plan = [
            ("kept", 0, column(lambda core: 2 * core)), ("got", 0, column(lambda core: 2 - 2 * core)),
            ("low", 1, column(lambda core: 1)), ("high", 1, whole),
        ]
        got["panel_grad"], got["merge_grad"] = finish(
            sums["C"], order, place, width, plan, [(width, 3 * width), (width, width)]
        )

    actions = dict(
        I=inner, T=attention, X=inputs, A0=start_outer, B0=start_inner,
        C0=start_rest, S0=start_small, S=small_step, SF=finish_small, A=lambda: sums["A"].advance(order),
        B=lambda: sums["B"].advance(order), C=lambda: sums["C"].advance(order),
        AF=finish_outer, BF=finish_inner, CF=finish_rest,
    )
    for action in SEQUENCE:
        actions[action]()
    small = got["small"]
    cut = lambda row, at: small[row, at * width : (at + 1) * width]
    outer_bias_grad, gain2_grad, shift2_grad = cut(0, 0), cut(0, 1), cut(0, 2)
    inner_bias_grad = small[1]
    merge_bias_grad, gain1_grad, shift1_grad = cut(2, 0), cut(2, 1), cut(2, 2)
    query_bias_grad, value_bias_grad = cut(3, 0), cut(3, 1)
    return (
        loss.reshape(1),
        layer_out,
        got["input_grad"],
        got["panel_grad"],
        query_bias_grad,
        value_bias_grad,
        got["merge_grad"],
        merge_bias_grad,
        gain1_grad,
        shift1_grad,
        got["inner_grad"],
        inner_bias_grad,
        got["outer_grad"],
        outer_bias_grad,
        gain2_grad,
        shift2_grad,
    )


def solution(mesh):
    return jax.shard_map(
        on_device,
        mesh=mesh,
        in_specs=(
            P(("wide", "narrow"), None),
            P(("wide", "narrow"), None),
            P(),
            P(),
            P(),
            P(),
            P(),
            P(),
            P(),
            P(),
            P(),
            P(),
            P(),
            P(),
            P(),
            P(),
            P(),
        ),
        out_specs=(
            P(),
            P(("wide", "narrow"), None),
            P(("wide", "narrow"), None),
            P(),
            P(),
            P(),
            P(),
            P(),
            P(),
            P(),
            P(),
            P(),
            P(),
            P(),
            P(),
            P(),
        ),
        check_vma=False,
    )
```

```python
from functools import partial

import jax
import jax.numpy as jnp
from jax import lax
from jax.experimental import pallas as pl
from jax.experimental.pallas import tpu as pltpu
from jax.sharding import PartitionSpec as P

HEADS = 12
S_ROW = 8
BOTH = ("wide", "narrow")
BF = jnp.bfloat16
F32 = jnp.float32


def tie(values, *others):
    return lax.optimization_barrier((values, others))[0]


class Place:
    def __init__(self):
        self.wide, self.narrow = lax.axis_size("wide"), lax.axis_size("narrow")
        self.count = self.wide * self.narrow
        self.core = lax.axis_index("narrow")
        self.me = lax.axis_index("wide") * self.narrow + self.core
        bits = [self.narrow << i for i in range(self.wide.bit_length() - 1)]
        self.own = [(1, 1)]
        self.pairs = [bits[i : i + 2] for i in range(0, len(bits), 2)]
        first, second = bits[0], bits[1]
        self.stages = [[(first, second)], [(second, first)]]
        self.stages += [self.combine(pair) for pair in self.pairs[1:]]
        self.spread = [self.combine(pair) for pair in self.pairs[::-1]] + [self.own]

    def combine(self, bits):
        if len(bits) == 1:
            return [(bits[0],) * 2]
        return [(m, m) for m in (bits[0], bits[1], bits[0] | bits[1])]

    def exchange(self, value, masks):
        pairs = [(i, i ^ masks[i % 2]) for i in range(self.count)]
        return lax.ppermute(value, BOTH, pairs)

    def index(self, stage):
        bit = lambda mask: (self.me // mask) % 2
        if len(stage) == 1:
            one, other = stage[0]
            return bit(one) if one == other else jnp.where(self.core == 0, bit(one), bit(other))
        return bit(stage[0][0]) + 2 * bit(stage[1][0])


class Sum:
    def __init__(self, place, send):
        self.place = place
        self.down, self.up = list(place.stages), list(place.stages[::-1]) + [place.own]
        self.sent = [send]
        self.got = [place.exchange(send, place.own[0])]
        self.stage = None

    def receive(self, order):
        got = [order.after(g) for g in self.got]
        if self.stage is None:
            return [self.kept] + got
        index = self.place.index(self.stage)
        parts = [self.kept] + got
        if len(parts) == 2:
            return [jnp.where(index == 0, jnp.concatenate(parts), jnp.concatenate(parts[::-1]))]
        ordered = []
        for at in range(len(parts)):
            value = parts[0]
            for i in range(1, len(parts)):
                value = jnp.where(index == at ^ i, parts[i], value)
            ordered.append(value)
        return [jnp.concatenate(ordered)]

    def advance(self, order):
        if not self.up:
            return
        terms = self.receive(order)
        if self.down:
            stage = self.down.pop(0)
            parts = len(stage) + 1
            index = self.place.index(stage)
            size = terms[0].shape[0] // parts
            cut = lambda at: sum(
                lax.dynamic_slice_in_dim(t, at * size, size).astype(F32) for t in terms
            )
            self.sent = [cut(index ^ (i + 1)).astype(BF) for i in range(len(stage))]
            self.kept = cut(index)
        else:
            self.stage = stage = self.up.pop(0)
            self.kept = sum(t.astype(F32) for t in terms).astype(BF) if len(terms) > 1 else terms[0]
            self.sent = [self.kept] * len(stage)
        self.got = [self.place.exchange(s, m) for s, m in zip(self.sent, stage)]
        order.done(*self.sent)


class Order:
    def __init__(self):
        self.last = ()

    def after(self, value):
        return tie(value, *self.last)

    def done(self, *values):
        self.last = values


def add_everywhere(total, place, order):
    for stage in [place.own] + place.spread[:-1]:
        got = [place.exchange(total, masks) for masks in stage]
        order.done(total)
        yield
        for part in got:
            total = total + order.after(part)
    order.done(total)
    yield total


def nt_dot(left, right):
    return lax.dot_general(left, right, (((1,), (1,)), ((), ())), preferred_element_type=F32)


def tn_dot(left, right):
    return lax.dot_general(left, right, (((0,), (0,)), ((), ())), preferred_element_type=F32)


def thirds(value):
    top = value.astype(BF)
    rest = value - top.astype(F32)
    middle = rest.astype(BF)
    return top, middle, (rest - middle.astype(F32)).astype(BF)


def column_sum(value):
    return jnp.sum(value, axis=0, keepdims=True)


def contrast_into(block, masks, me, cool_ref, pick_ref, there_ref, own_ref, partner_ref, loss_ref, grad_ref,
                  all_ref, sums_ref, rnorm_ref):
    count, width_all = all_ref.shape
    owned = own_ref.shape[0]
    for position, mask in enumerate(masks):
        at = pl.multiple_of((me ^ mask) * owned, owned)
        all_ref[pl.ds(at, owned), :] = there_ref[position * owned : (position + 1) * owned, :]
    widths = [width_all * f // 12 for f in (1, 2, 4, 8, 12)]
    warm = 1.0 / cool_ref[0]
    lane = lax.broadcasted_iota(jnp.int32, (1, 128), 1)
    first_mask = (lane < widths[0]).astype(F32)
    spans = [(0, 128, True), (0, 128, False), (128, widths[2], False), (widths[2], widths[3], False),
             (widths[3], widths[4], False)]
    partner = partner_ref[...][None, :]

    squares = jnp.zeros((8, count), F32)
    for index, (lo, hi, masked) in enumerate(spans):
        part = all_ref[:, lo:hi].astype(F32)
        if masked:
            part = part * first_mask
        term = sum(nt_dot(jnp.ones((8, hi - lo), BF), p) for p in thirds(part * part))
        squares = term if index <= 1 else squares + term
        rnorm_ref[index] = lax.rsqrt(squares[:1] + 1e-06)
    sums_ref[...] = jnp.zeros_like(sums_ref)
    hits = jnp.zeros((1, count), F32)
    for b in range(count // block):
        rows = pl.ds(b * block, block)
        row = lax.broadcasted_iota(jnp.int32, (block, count), 0) + b * block
        diagonal = row == lax.broadcasted_iota(jnp.int32, (block, count), 1)
        positive = row == partner
        gram = norms = None
        for index, (lo, hi, masked) in enumerate(spans):
            mine = all_ref[rows, lo:hi]
            if masked:
                mine = mine * first_mask.astype(BF)
            wide = mine.astype(F32)
            term = nt_dot(mine, all_ref[:, lo:hi])
            square = jnp.sum(wide * wide, axis=1, keepdims=True)
            gram, norms = (term, square) if index <= 1 else (gram + term, norms + square)
            scores = gram * (lax.rsqrt(norms + 1e-06) * warm) * rnorm_ref[index]
            sums_ref[index] += column_sum(jnp.where(diagonal, 0.0, jnp.exp(scores)))
            hits += column_sum(jnp.where(positive, scores, 0.0))
    logs = -hits
    for index in range(5):
        logs += jnp.log(sums_ref[index])
    loss_ref[...] = jnp.sum(logs, axis=1, keepdims=True)

    first = me * owned
    col = lax.broadcasted_iota(jnp.int32, (owned, count), 1)
    line = lax.broadcasted_iota(jnp.int32, (owned, count), 0)
    chosen = jnp.zeros((owned, count), jnp.int32)
    for i in range(owned):
        chosen = jnp.where(line == i, pick_ref[first + i], chosen)
    diagonal = line + first == col
    picks = (chosen == col).astype(F32) + (partner == line + first).astype(F32)
    gram = norms = None
    weights, inverses = [], []
    for index, (lo, hi, masked) in enumerate(spans):
        mine = own_ref[:, lo:hi]
        if masked:
            mine = mine * first_mask.astype(BF)
        wide = mine.astype(F32)
        term = nt_dot(mine, all_ref[:, lo:hi])
        square = jnp.sum(wide * wide, axis=1, keepdims=True)
        gram, norms = (term, square) if index <= 1 else (gram + term, norms + square)
        inverse = lax.rsqrt(norms + 1e-06)
        raised = jnp.where(diagonal, 0.0, jnp.exp(gram * (inverse * warm) * rnorm_ref[index]))
        own_sum = jnp.sum(raised, axis=1, keepdims=True)
        pull = raised * (1.0 / own_sum + 1.0 / sums_ref[index]) - picks
        weights.append(pull * (rnorm_ref[index] * warm))
        inverses.append(inverse)
    parts = jnp.dot(
        jnp.concatenate(thirds(jnp.concatenate(weights, axis=0)), axis=0), all_ref[...],
        preferred_element_type=F32,
    )
    unit_grads = parts[: 5 * owned] + parts[5 * owned : 10 * owned] + parts[10 * owned :]
    total = jnp.zeros((owned, width_all), F32)
    column = lax.broadcasted_iota(jnp.int32, (owned, width_all), 1)
    embed = own_ref[...].astype(F32)
    for index in range(5):
        inside = column < widths[index]
        mine = jnp.where(inside, embed, 0.0)
        grad = jnp.where(inside, unit_grads[index * owned : (index + 1) * owned], 0.0)
        along = jnp.sum(mine * grad, axis=1, keepdims=True)
        inverse = inverses[index]
        total += inverse * grad - (inverse * inverse * inverse * along) * mine
    grad_ref[...] = total


SEQUENCE = (
    "A0", "A", "I", "A", "B0", "B", "A", "T", "A", "B", "C0", "A", "C", "B", "A", "C", "B", "A",
    "C", "B", "C", "B", "X", "C", "S0", "B", "C", "S", "A", "BF", "S", "AF", "C", "SF", "C", "CF",
)


def kernel_call(body, name, flops, nbytes, limit=58, **options):
    return pl.pallas_call(
        body,
        compiler_params=pltpu.CompilerParams(vmem_limit_bytes=limit << 20),
        cost_estimate=pl.CostEstimate(flops=flops, bytes_accessed=nbytes, transcendentals=0),
        name=name,
        **options,
    )


def fixed(shape):
    return pl.BlockSpec(shape, lambda *_: (0,) * len(shape))


def windows(length, step=128):
    return [(at, max(0, at - step), min(length, at + 2 * step)) for at in range(0, length, step)]


def segment_row(seg_ref):
    return seg_ref[pl.ds(pl.program_id(0), 1), :].astype(F32)


def segment_column(seg):
    return jnp.broadcast_to(seg, (128, seg.shape[1])).T


def masks_into(bias_ref, seg_ref):
    seg = segment_row(seg_ref)
    column = segment_column(seg)
    for index, (at, lo, hi) in enumerate(windows(seg.shape[1])):
        same = column[lo:hi, :] == seg[:, at : at + 128]
        bias = jnp.where(same, 0.0, -1e9)
        bias_ref[index, : hi - lo, :] = jnp.concatenate([bias, bias], axis=1)


def pair_stack(two):
    lane = lax.broadcasted_iota(jnp.int32, two.shape, 1)
    nought = jnp.zeros_like(two)
    half = two.shape[1] // 2
    return jnp.concatenate(
        [jnp.where(lane < half, two, nought), jnp.where(lane < half, nought, two)], axis=0
    )


def pair_merge(both):
    size = both.shape[1] // 2
    row = lax.broadcasted_iota(jnp.int32, (both.shape[0], size), 0)
    return jnp.where(row < both.shape[0] // 2, both[:, :size], both[:, size:])


def attend_kernel(x_ref, seg_ref, w_ref, bq_ref, bv_ref, wo_ref, bo_ref, gain_ref,
                  shift_ref, q_ref, k_ref, v_ref, mixed_t_ref, lse_ref, hat_ref, rstd_ref, low_ref,
                  x_t_ref, low_t_ref, bias_ref, mixed_ref):
    length, width = x_ref.shape
    x = x_ref[...]
    masks_into(bias_ref, seg_ref)
    q = jnp.dot(x, w_ref[:, :width], preferred_element_type=F32) + bq_ref[...][None, :]
    q_ref[...] = (q.astype(BF).astype(F32) * (width // HEADS) ** -0.5).astype(BF)
    k_ref[...] = jnp.dot(x, w_ref[:, width : 2 * width], preferred_element_type=F32).astype(BF)
    v_ref[...] = (jnp.dot(x, w_ref[:, 2 * width :], preferred_element_type=F32) + bv_ref[...][None, :]).astype(BF)
    jobs = [(pair, index) + win for pair in range(HEADS // 2) for index, win in enumerate(windows(length))]

    def scores(job):
        pair, index, at, lo, hi = job
        lanes = slice(pair * 128, pair * 128 + 128)
        stacked = pair_stack(q_ref[at : at + 128, lanes])
        return nt_dot(k_ref[lo:hi, lanes], stacked)

    ahead = scores(jobs[0])
    for number, job in enumerate(jobs):
        pair, index, at, lo, hi = job
        lanes = slice(pair * 128, pair * 128 + 128)
        raw = ahead
        if number + 1 < len(jobs):
            ahead = scores(jobs[number + 1])
        masked = raw + bias_ref[index, : hi - lo, :]
        top = jnp.max(masked, axis=0, keepdims=True)
        raised = jnp.exp(masked - top)
        total = jnp.sum(raised, axis=0, keepdims=True)
        log_total = top + jnp.log(total)
        for side in (0, 1):
            head = 2 * pair + side
            lse_ref[head // 4, head % 4 : head % 4 + 1, at : at + 128] = log_total[:, side * 128 : side * 128 + 128]
        both = tn_dot((raised * (1.0 / total)).astype(BF), v_ref[lo:hi, lanes])
        lane = lax.broadcasted_iota(jnp.int32, (128, 128), 1)
        merged = jnp.where(lane < 64, both[:128], both[128:])
        mixed_ref[at : at + 128, lanes] = merged.astype(BF)
        mixed_t_ref[lanes, at : at + 128] = merged.T.astype(BF)
    attn = jnp.dot(mixed_ref[...], wo_ref[...], preferred_element_type=F32) + bo_ref[...][None, :]
    total = x.astype(F32) + attn
    center = total - jnp.mean(total, axis=1, keepdims=True)
    rstd = lax.rsqrt(jnp.mean(center * center, axis=1, keepdims=True) + 1e-05)
    hat = center * rstd
    hat_ref[...] = hat
    rstd_ref[...] = rstd
    low = (hat * gain_ref[...][None, :] + shift_ref[...][None, :]).astype(BF)
    low_ref[...] = low
    low_t_ref[...] = low.T
    x_t_ref[...] = x.T


def attend(x, seg, w, bq, bv, wo, bo, gain, shift):
    tokens, width = x.shape
    rows, length = seg.shape
    row_block = lambda *tail: pl.BlockSpec((length,) + tail, lambda r: (r, 0))
    return kernel_call(
        attend_kernel, "attend", 2 * tokens * width * width * 4 + 4 * tokens * 384 * width * 2, 20 << 20,
        grid=(rows,),
        in_specs=[
            row_block(width), fixed(seg.shape), fixed(w.shape), fixed(bq.shape), fixed(bv.shape), fixed(wo.shape), fixed(bo.shape),
            fixed(gain.shape), fixed(shift.shape),
        ],
        out_specs=(
            row_block(width), row_block(width), row_block(width),
            pl.BlockSpec((width, length), lambda r: (0, r)),
            pl.BlockSpec((HEADS // 4, 4, length), lambda r: (r, 0, 0)),
            row_block(width), row_block(1), row_block(width),
            pl.BlockSpec((width, length), lambda r: (0, r)), pl.BlockSpec((width, length), lambda r: (0, r)),
        ),
        out_shape=(
            jax.ShapeDtypeStruct((tokens, width), BF), jax.ShapeDtypeStruct((tokens, width), BF),
            jax.ShapeDtypeStruct((tokens, width), BF), jax.ShapeDtypeStruct((width, tokens), BF),
            jax.ShapeDtypeStruct((rows * HEADS // 4, 4, length), F32), jax.ShapeDtypeStruct((tokens, width), F32),
            jax.ShapeDtypeStruct((tokens, 1), F32), jax.ShapeDtypeStruct((tokens, width), BF),
            jax.ShapeDtypeStruct((width, tokens), BF), jax.ShapeDtypeStruct((width, tokens), BF),
        ),
        scratch_shapes=[
            pltpu.VMEM((length // 128, 384, 256), F32), pltpu.VMEM((length, width), BF),
        ],
    )(x, seg, w, bq, bv, wo, bo, gain, shift)


def gelu_parts(v):
    bell = jnp.exp(v * v * -0.5)
    t = 1.0 / (1.0 + (0.3275911 * 0.5 ** 0.5) * jnp.abs(v))
    poly = ((((0.5 * 1.061405429 * t - 0.5 * 1.453152027) * t + 0.5 * 1.421413741) * t
             - 0.5 * 0.284496736) * t + 0.5 * 0.254829592) * t
    tail = poly * bell
    share = jnp.where(v >= 0.0, 1.0 - tail, tail)
    return v * share, share + v * bell * 0.3989422804014327


def feed_kernel(chunk, hat_ref, low_ref, seg_ref, gain1_ref, shift1_ref, w1_ref, b1_ref, w2_ref, b2_ref,
                gain_ref, shift_ref, act_t_ref, slope_ref, hat2_ref, rstd2_ref, out_ref, embed_ref,
                pooled_ref, value_ref):
    length, width = hat_ref.shape
    hidden = w1_ref.shape[1]
    low = low_ref[...]
    count = hidden // chunk

    def entry(i):
        return jnp.dot(low, w1_ref[:, i * chunk : (i + 1) * chunk], preferred_element_type=F32)

    total = hat_ref[...] * gain1_ref[...][None, :] + shift1_ref[...][None, :] + b2_ref[...][None, :]
    ahead = entry(0)
    for i in range(count):
        cols = slice(i * chunk, (i + 1) * chunk)
        inner = ahead + b1_ref[cols][None, :]
        if i + 1 < count:
            ahead = entry(i + 1)
        value, slope = gelu_parts(inner)
        value = value.astype(BF)
        act_t_ref[cols, :] = value.T
        slope_ref[:, cols] = slope.astype(BF)
        value_ref[:, cols] = value
    total += jnp.dot(value_ref[...], w2_ref[...], preferred_element_type=F32)
    center = total - jnp.mean(total, axis=1, keepdims=True)
    rstd = lax.rsqrt(jnp.mean(center * center, axis=1, keepdims=True) + 1e-05)
    hat = center * rstd
    hat2_ref[...] = hat
    rstd2_ref[...] = rstd
    out = hat * gain_ref[...][None, :] + shift_ref[...][None, :]
    out_ref[...] = out.astype(BF)
    number = lax.broadcasted_iota(jnp.int32, (S_ROW, length), 0)
    onehot = (segment_row(seg_ref) == number.astype(F32)).astype(F32)
    tokens_in = jnp.sum(onehot, axis=1, keepdims=True)
    onehot = onehot.astype(BF)
    sums = jnp.zeros((S_ROW, width), F32)
    for part in thirds(out):
        sums += jnp.dot(onehot, part, preferred_element_type=F32)
    row = pl.program_id(0)
    pooled_ref[pl.ds(row * S_ROW, S_ROW), :] = sums / tokens_in

    @pl.when(row == pl.num_programs(0) - 1)
    def _():
        embed_ref[...] = pooled_ref[...].astype(BF)


def feed(hat, low, seg, gain1, shift1, w1, b1, w2, b2, gain, shift):
    tokens, width = hat.shape
    rows, length = seg.shape
    hidden = w1.shape[1]
    row_block = lambda *tail: pl.BlockSpec((length,) + tail, lambda r: (r, 0))
    return kernel_call(
        partial(feed_kernel, 1024), "feed", 4 * tokens * width * hidden, 30 << 20,
        grid=(rows,),
        in_specs=[
            row_block(width), row_block(width), fixed(seg.shape),
        ] + [fixed(a.shape) for a in (gain1, shift1, w1, b1, w2, b2, gain, shift)],
        out_specs=(
            pl.BlockSpec((hidden, length), lambda r: (0, r)), row_block(hidden), row_block(width), row_block(1),
            row_block(width),
            fixed((rows * S_ROW, width)),
        ),
        out_shape=(
            jax.ShapeDtypeStruct((hidden, tokens), BF), jax.ShapeDtypeStruct((tokens, hidden), BF),
            jax.ShapeDtypeStruct((tokens, width), F32), jax.ShapeDtypeStruct((tokens, 1), F32),
            jax.ShapeDtypeStruct((tokens, width), BF), jax.ShapeDtypeStruct((rows * S_ROW, width), BF),
        ),
        scratch_shapes=[pltpu.VMEM((rows * S_ROW, width), F32), pltpu.VMEM((length, hidden), BF)],
    )(hat, low, seg, gain1, shift1, w1, b1, w2, b2, gain, shift)


def norm_back(grad, hat, rstd, gain):
    inside = grad * gain
    first = jnp.mean(inside, axis=1, keepdims=True)
    second = jnp.mean(inside * hat, axis=1, keepdims=True)
    return (inside - first - hat * second) * rstd


def line_into(ref, vectors):
    ref[...] = jnp.zeros_like(ref)
    at = 0
    for vector in vectors:
        ref[:, at : at + vector.shape[1]] = vector
        at += vector.shape[1]


def copies(pairs, sems):
    return [pltpu.make_async_copy(src, dst, sems.at[i]) for i, (src, dst) in enumerate(pairs)]


def outer_back_kernel(block, masks, info_ref, pick_ref, cool_ref, there_ref, own_ref, partner_ref, seg_ref, rstd_ref,
                      gain_ref, act_t_ref, hat_hbm, loss_ref, line_ref, send_ref,
                      keep_ref, second_hbm, outer_hbm, embed_grad_ref, all_ref, sums_ref, rnorm_ref,
                      hat_ref, second_ref, outer_ref, sems):
    step = pl.program_id(0)
    rows, length = seg_ref.shape
    width = gain_ref.shape[0]
    load, *store = copies([(hat_hbm, hat_ref), (second_ref, second_hbm), (outer_ref, outer_hbm)], sems)

    @pl.when(step == 0)
    def _():
        load.start()
        contrast_into(block, masks, info_ref[0], cool_ref, pick_ref, there_ref, own_ref, partner_ref,
                      loss_ref, embed_grad_ref, all_ref, sums_ref, rnorm_ref)
        load.wait()
        gains, shifts, biases = [], [], []
        for row in range(rows):
            span = slice(row * length, (row + 1) * length)
            seg = seg_ref[row : row + 1, :].astype(F32)
            number = lax.broadcasted_iota(jnp.int32, (S_ROW, length), 0).astype(F32)
            tokens_in = jnp.sum((seg == number).astype(F32), axis=1, keepdims=True)
            each = embed_grad_ref[row * S_ROW : (row + 1) * S_ROW, :] / tokens_in
            stack = [p.astype(F32) for p in thirds(each)] + [jnp.zeros((128 - 3 * S_ROW, width), F32)]
            lane = lax.broadcasted_iota(jnp.int32, (length, 128), 1)
            pick = (lane < 3 * S_ROW) & ((lane % S_ROW).astype(F32) == segment_column(seg))
            grad = jnp.dot(
                pick.astype(BF), jnp.concatenate(stack).astype(BF), preferred_element_type=F32
            )
            hat = hat_ref[span, :]
            second = norm_back(grad, hat, rstd_ref[span, :], gain_ref[...][None, :])
            low = second.astype(BF)
            second_ref[span, :] = second
            outer_ref[span, :] = low
            gains.append(column_sum(grad * hat))
            shifts.append(column_sum(grad))
            biases.append(column_sum(low.astype(F32)))
        line_into(line_ref, [sum(biases), sum(gains), sum(shifts)])
        for copy in store:
            copy.start()

    weight = jnp.dot(act_t_ref[...], outer_ref[...], preferred_element_type=F32).astype(BF)
    half = pl.num_programs(0) // 2

    @pl.when(step < half)
    def _():
        send_ref[...] = weight

    @pl.when(step >= half)
    def _():
        keep_ref[...] = weight

    @pl.when(step == pl.num_programs(0) - 1)
    def _():
        for copy in store:
            copy.wait()


def gather_embeds(own, place):
    there, masks = own, [0]
    for stage in place.spread:
        there = jnp.concatenate([there] + [place.exchange(there, pair) for pair in stage])
        masks = masks + [m ^ pair[0] for pair in stage for m in masks]
    return there, masks


def outer_back(own, partner, coolness, seg, hat, rstd, gain, act_t, place, chunk=768):
    there, masks = gather_embeds(own, place)
    owned, width = own.shape
    count = owned * len(masks)
    tokens = hat.shape[0]
    hidden = act_t.shape[0]
    steps = hidden // chunk
    half = steps // 2
    whole = lambda shape: pl.BlockSpec(shape, lambda i, *_: (0,) * len(shape))
    smem, hbm = pl.BlockSpec(memory_space=pltpu.SMEM), pl.BlockSpec(memory_space=pl.ANY)
    vmem = pl.BlockSpec(memory_space=pltpu.VMEM)
    turn = lambda i, info: (lax.rem(i + half * (1 - info[1]), steps), 0)
    return kernel_call(
        partial(outer_back_kernel, min(count, 256), masks), "outer_back", 2 * tokens * hidden * width, 20 << 20,
        grid_spec=pltpu.PrefetchScalarGridSpec(
            num_scalar_prefetch=1,
            grid=(steps,),
            in_specs=[smem, smem, vmem, vmem, whole(partner.shape), whole(seg.shape),
                      whole(rstd.shape), whole(gain.shape), pl.BlockSpec((chunk, tokens), turn), hbm],
            out_specs=(
                whole((1, 1)), whole((1, hidden)),
                pl.BlockSpec((chunk, width), lambda i, info: (jnp.minimum(i, half - 1), 0)),
                pl.BlockSpec((chunk, width), lambda i, info: (jnp.maximum(i - half, 0), 0)), hbm, hbm,
            ),
            scratch_shapes=[
                pltpu.VMEM((owned, width), F32), pltpu.VMEM((count, width), BF), pltpu.VMEM((5, 1, count), F32),
                pltpu.VMEM((5, 1, count), F32), pltpu.VMEM((tokens, width), F32),
                pltpu.VMEM((tokens, width), F32), pltpu.VMEM((tokens, width), BF), pltpu.SemaphoreType.DMA((3,)),
            ],
        ),
        out_shape=(
            jax.ShapeDtypeStruct((1, 1), F32), jax.ShapeDtypeStruct((1, hidden), F32),
            jax.ShapeDtypeStruct((hidden // 2, width), BF), jax.ShapeDtypeStruct((hidden // 2, width), BF),
            jax.ShapeDtypeStruct((tokens, width), F32), jax.ShapeDtypeStruct((tokens, width), BF),
        ),
    )(jnp.stack([place.me, place.core]), partner, coolness, there, own, partner, seg, rstd, gain, act_t, hat)


def inner_back_kernel(rows, info_ref, outer_ref, low_t_ref, slope_ref, w2_ref, w1_ref, rstd_ref, gain_ref, second_hbm,
                      hat_hbm, mixed_t_hbm, wo_hbm, send_ref, keep_ref, bias_ref, mixed_grad_ref, merge_ref, line_ref,
                      first_hbm,
                      normed_ref, second_ref, hat_ref, mixed_t_ref, wo_ref, sems, out_sems):
    step, last = pl.program_id(0), pl.num_programs(0) - 1
    length = outer_ref.shape[0] // rows
    loads = copies([(second_hbm, second_ref), (hat_hbm, hat_ref), (mixed_t_hbm, mixed_t_ref), (wo_hbm, wo_ref)], sems)

    @pl.when(step == 0)
    def _():
        for copy in loads:
            copy.start()

    active = nt_dot(outer_ref[...], w2_ref[...])
    inner = (active * slope_ref[...].astype(F32)).astype(BF)
    bias_ref[...] = column_sum(inner.astype(F32))
    weight = jnp.dot(low_t_ref[...], inner, preferred_element_type=F32).astype(BF)
    normed = nt_dot(inner, w1_ref[...])

    @pl.when(step <= last // 2)
    def _():
        send_ref[...] = weight

    @pl.when(step > last // 2)
    def _():
        keep_ref[...] = weight

    @pl.when(step == 0)
    def _():
        normed_ref[...] = normed

    @pl.when(step > 0)
    def _():
        normed_ref[...] += normed

    @pl.when(step == last)
    def _():
        for copy in loads:
            copy.wait()
        gains, shifts, biases, merges, stores = [], [], [], [], []
        for row in range(rows):
            span = slice(row * length, (row + 1) * length)
            hat = hat_ref[span, :]
            grad = normed_ref[span, :] + second_ref[span, :]
            first = norm_back(grad, hat, rstd_ref[span, :], gain_ref[...][None, :])
            normed_ref[span, :] = first
            store = pltpu.make_async_copy(normed_ref.at[span, :], first_hbm.at[span, :], out_sems.at[row])
            store.start()
            stores.append(store)
            low = first.astype(BF)
            gains.append(column_sum(grad * hat))
            shifts.append(column_sum(grad))
            biases.append(column_sum(low.astype(F32)))
            mixed_grad_ref[span, :] = nt_dot(low, wo_ref[...]).astype(BF)
            merges.append(jnp.dot(mixed_t_ref[:, span], low, preferred_element_type=F32))
        merge_ref[...] = sum(merges).astype(BF)
        line_into(line_ref, [sum(biases), sum(gains), sum(shifts)])
        for store in stores:
            store.wait()


def inner_back(outer, second, low_t, slope, w2, w1, hat, rstd, gain, mixed_t, wo, rows, place, chunk=512):
    tokens, width = outer.shape
    hidden = slope.shape[1]
    steps = hidden // chunk
    half = steps // 2
    whole = lambda shape: pl.BlockSpec(shape, lambda i, *_: (0,) * len(shape))
    hbm = pl.BlockSpec(memory_space=pl.ANY)
    turn = lambda i, info: lax.rem(i + half * (1 - info[1]), steps)
    early = lambda i: jnp.minimum(i, half - 1)
    late = lambda i: jnp.maximum(i - half, 0)
    line = jax.ShapeDtypeStruct((1, hidden), F32)
    part = jax.ShapeDtypeStruct((half * width, chunk), BF)
    return kernel_call(
        partial(inner_back_kernel, rows), "inner_back", 6 * tokens * hidden * width, 40 << 20, limit=46,
        grid_spec=pltpu.PrefetchScalarGridSpec(
            num_scalar_prefetch=1,
            grid=(steps,),
            in_specs=[
                whole(outer.shape), whole(low_t.shape),
                pl.BlockSpec((tokens, chunk), lambda i, info: (0, turn(i, info))),
                pl.BlockSpec((chunk, width), lambda i, info: (turn(i, info), 0)),
                pl.BlockSpec((width, chunk), lambda i, info: (0, turn(i, info))),
                whole(rstd.shape), whole(gain.shape), hbm, hbm, hbm, hbm,
            ],
            out_specs=(
                pl.BlockSpec((width, chunk), lambda i, info: (early(i), 0)),
                pl.BlockSpec((width, chunk), lambda i, info: (late(i), 0)),
                pl.BlockSpec((1, chunk), lambda i, info: (0, turn(i, info))),
                whole((tokens, width)), whole((width, width)), whole((1, hidden)), hbm,
            ),
            scratch_shapes=[
                pltpu.VMEM((tokens, width), F32), pltpu.VMEM((tokens, width), F32), pltpu.VMEM((tokens, width), F32),
                pltpu.VMEM(mixed_t.shape, BF), pltpu.VMEM(wo.shape, BF), pltpu.SemaphoreType.DMA((4,)),
                pltpu.SemaphoreType.DMA((rows,)),
            ],
        ),
        out_shape=(
            part, part, line, jax.ShapeDtypeStruct((tokens, width), BF),
            jax.ShapeDtypeStruct((width, width), BF), line,
            jax.ShapeDtypeStruct((tokens, width), F32),
        ),
    )(jnp.stack([place.me, place.core]), outer, low_t, slope, w2, w1, rstd, gain, second, hat, mixed_t, wo)


def attend_back_kernel(pairs, core_ref, x_t_ref, merge_ref, seg_ref, lse_ref, q_ref, k_ref, v_ref, grad_ref,
                       dq_ref, dk_ref, dv_ref, send_ref, keep_ref, line_ref,
                       bias_ref, k_sum_ref, v_sum_ref, weight_ref):
    row = pl.program_id(0)
    length = q_ref.shape[0]
    masks_into(bias_ref, seg_ref)
    k_sum_ref[...] = jnp.zeros_like(k_sum_ref)
    v_sum_ref[...] = jnp.zeros_like(v_sum_ref)
    jobs = [(pair, index) + win for pair in range(pairs) for index, win in enumerate(windows(length))]

    def begin(job):
        pair, index, at, lo, hi = job
        lanes = slice(pair * 128, pair * 128 + 128)
        query = pair_stack(q_ref[at : at + 128, lanes])
        grad = pair_stack(grad_ref[at : at + 128, lanes])
        return query, grad, nt_dot(k_ref[lo:hi, lanes], query), nt_dot(v_ref[lo:hi, lanes], grad)

    ahead = begin(jobs[0])
    for number, job in enumerate(jobs):
        pair, index, at, lo, hi = job
        lanes = slice(pair * 128, pair * 128 + 128)
        query, grad, raw, prob_grad = ahead
        if number + 1 < len(jobs):
            ahead = begin(jobs[number + 1])
        log_total = jnp.concatenate(
            [lse_ref[head // 4, head % 4 : head % 4 + 1, at : at + 128] for head in (2 * pair, 2 * pair + 1)],
            axis=1
        )
        probs = jnp.exp(raw + bias_ref[index, : hi - lo, :] - log_total)
        weighed = probs * prob_grad
        raw_grad = (weighed - probs * jnp.sum(weighed, axis=0, keepdims=True)).astype(BF)
        v_sum_ref[lo:hi, lanes] += jnp.dot(probs.astype(BF), grad, preferred_element_type=F32)
        k_sum_ref[lo:hi, lanes] += jnp.dot(raw_grad, query, preferred_element_type=F32)
        if index == 0:
            keys_t = k_ref[:, lanes].T
        both = jnp.dot(keys_t[:, lo:hi], raw_grad, preferred_element_type=F32)
        merged = pair_merge(both) * 0.125
        dq_ref[at : at + 128, lanes] = merged.T.astype(BF)
    dk_ref[...] = k_sum_ref[...].astype(BF)
    dv_ref[...] = v_sum_ref[...].astype(BF)

    @pl.when(row == 0)
    def _():
        for ref in (weight_ref, line_ref):
            ref[...] = jnp.zeros_like(ref)

    width = dq_ref.shape[1]
    line_ref[:, :width] += column_sum(dq_ref[...].astype(F32))
    line_ref[:, width : 2 * width] += column_sum(dv_ref[...].astype(F32))
    for index, ref in enumerate((dq_ref, dk_ref, dv_ref)):
        weight_ref[index] += jnp.dot(x_t_ref[...], ref[...], preferred_element_type=F32)

    @pl.when(row == pl.num_programs(0) - 1)
    def _():
        for mine, first, second in ((0, keep_ref, send_ref), (1, send_ref, keep_ref)):
            @pl.when(core_ref[0] == mine)
            def _(first=first, second=second):
                first[...] = weight_ref[:2].astype(BF)
                second[0] = weight_ref[2].astype(BF)
                second[1] = merge_ref[...]


def attend_back(x_t, merge, seg, lse, q, k, v, grad, place):
    tokens, width = q.shape
    rows, length = seg.shape
    part = pl.BlockSpec((length, width), lambda r, core: (r, 0))
    whole = lambda shape: pl.BlockSpec(shape, lambda i, *_: (0,) * len(shape))
    groups = HEADS // 4
    half = jax.ShapeDtypeStruct((2, width, width), BF)
    return kernel_call(
        partial(attend_back_kernel, HEADS // 2), "attend_back",
        10 * tokens * 384 * width * 2 + 6 * tokens * width * width, 30 << 20, limit=40,
        grid_spec=pltpu.PrefetchScalarGridSpec(
            num_scalar_prefetch=1,
            grid=(rows,),
            in_specs=[
                pl.BlockSpec((width, length), lambda r, core: (0, r)), whole(merge.shape), whole(seg.shape),
                pl.BlockSpec((groups, 4, length), lambda r, core: (r, 0, 0)), part, part, part, part,
            ],
            out_specs=(part, part, part, whole(half.shape), whole(half.shape), whole((1, 4 * width))),
            scratch_shapes=[
                pltpu.VMEM((length // 128, 384, 256), F32), pltpu.VMEM((length, width), F32),
                pltpu.VMEM((length, width), F32), pltpu.VMEM((3, width, width), F32),
            ],
        ),
        out_shape=(jax.ShapeDtypeStruct((tokens, width), BF),) * 3
        + (half, half, jax.ShapeDtypeStruct((1, 4 * width), F32)),
    )(place.core.reshape(1), x_t, merge, seg, lse, q, k, v, grad)


def input_back_kernel(first_ref, *refs):
    *grads, w_ref, out_ref = refs
    width = first_ref.shape[1]
    total = first_ref[...]
    for index, ref in enumerate(grads):
        total += nt_dot(ref[...], w_ref[:, index * width : (index + 1) * width])
    out_ref[...] = total


def input_back(first, grads, w, block=512):
    tokens, width = first.shape
    rows = lambda cols: pl.BlockSpec((block, cols), lambda i: (i, 0))
    return kernel_call(
        input_back_kernel, "input_back", 6 * tokens * width * width, 15 << 20,
        grid=(tokens // block,),
        in_specs=[rows(width)] + [rows(g.shape[1]) for g in grads] + [fixed(w.shape)],
        out_specs=rows(width),
        out_shape=jax.ShapeDtypeStruct((tokens, width), F32),
    )(first, *grads, w)


def finish_kernel(plan, core_ref, kept_ref, got_ref, *refs):
    *outs, out_ref, out_sems = refs
    core = core_ref[0]
    rows = out_ref.shape[1]
    stores = []
    for index, (kind, at, target) in enumerate(plan):
        span = slice(at * rows, (at + 1) * rows)
        kept, got = kept_ref[span, :].astype(F32), got_ref[span, :].astype(F32)
        own = core == (0 if kind == "low" else 1)
        out_ref[index] = kept if kind == "kept" else got if kind == "got" else jnp.where(own, kept, got)
        stores.append(pltpu.make_async_copy(out_ref.at[index], target(outs, core), out_sems.at[index]))
        stores[-1].start()
    for store in stores:
        store.wait()


def finish(one, order, place, rows, plan, shapes):
    while one.up:
        one.advance(order)
    kept, got = one.kept, order.after(one.got[0])
    half, cols = kept.shape
    hbm = pl.BlockSpec(memory_space=pl.ANY)
    result = kernel_call(
        partial(finish_kernel, plan), "finish", 0, half * cols * 12, limit=24,
        in_specs=[pl.BlockSpec(memory_space=pltpu.SMEM)] + [pl.BlockSpec(memory_space=pltpu.VMEM)] * 2,
        out_specs=[hbm] * len(shapes),
        out_shape=[jax.ShapeDtypeStruct(shape, F32) for shape in shapes],
        scratch_shapes=[
            pltpu.VMEM((len(plan), rows, cols), F32), pltpu.SemaphoreType.DMA((len(plan),)),
        ],
    )(place.core.reshape(1), kept, got)
    order.done(*result)
    return result


def on_device(
    incoming_activations,
    span_identifiers,
    partner_global_index,
    softmax_coolness,
    triple_kernel_panel,
    asking_shift,
    content_shift,
    mixer_result_kernel,
    mixer_result_shift,
    initial_standardize_scale,
    initial_standardize_shift,
    perceptron_entry_kernel,
    perceptron_entry_shift,
    perceptron_result_kernel,
    perceptron_result_shift,
    later_standardize_scale,
    later_standardize_shift,
):
    rows, length = span_identifiers.shape
    width = incoming_activations.shape[1]
    hidden = perceptron_entry_kernel.shape[1]
    place, order = Place(), Order()
    seg = span_identifiers
    q, k, v, mixed_t, lse, hat1, rstd1, low, x_t, low_t = attend(
        incoming_activations, seg, triple_kernel_panel, asking_shift, content_shift, mixer_result_kernel,
        mixer_result_shift, initial_standardize_scale, initial_standardize_shift,
    )
    act_t, slope, hat2, rstd2, layer_out, embed = feed(
        hat1, low, seg, initial_standardize_scale, initial_standardize_shift, perceptron_entry_kernel,
        perceptron_entry_shift, perceptron_result_kernel, perceptron_result_shift, later_standardize_scale,
        later_standardize_shift,
    )
    (
        loss, second_line, outer_send, outer_keep, second, outer,
    ) = outer_back(
        embed, partner_global_index, softmax_coolness, seg, hat2, rstd2, later_standardize_scale, act_t, place
    )
    order.done(outer)
    got, sums, blocks = {}, {}, hidden // 512 // 2

    def inner():
        (
            got["inner_send"], got["inner_keep"], got["inner_line"], got["mixed_grad"], got["merge"],
            got["first_line"], got["first"],
        ) = inner_back(
            order.after(outer), second, low_t, slope, perceptron_result_kernel, perceptron_entry_kernel, hat1,
            rstd1, initial_standardize_scale, mixed_t, mixer_result_kernel, rows, place,
        )
        order.done(got["mixed_grad"])

    def attention():
        *got["grads"], got["rest_send"], got["rest_keep"], got["rest_line"] = attend_back(
            x_t, got["merge"], seg, lse, q, k, v, order.after(got["mixed_grad"]), place
        )
        order.done(got["rest_send"])

    def inputs():
        got["input_grad"] = input_back(order.after(got["first"]), got["grads"], triple_kernel_panel)
        order.done(got["input_grad"])

    def start(name, send, keep):
        sums[name] = Sum(place, order.after(send))
        sums[name].kept = keep
        order.done(*sums[name].sent)

    def start_outer():
        start("A", outer_send, outer_keep)

    def start_inner():
        start("B", got["inner_send"], got["inner_keep"])

    def start_rest():
        start("C", got["rest_send"].reshape(2 * width, width), got["rest_keep"].reshape(2 * width, width))

    def start_small():
        lines = [second_line, got["inner_line"], got["first_line"], got["rest_line"]]
        small = jnp.concatenate(lines, axis=0)
        sums["S"] = add_everywhere(order.after(small), place, order)
        next(sums["S"])

    def small_step():
        got["small"] = next(sums["S"])

    def finish_small():
        while got.get("small") is None:
            small_step()

    def finish_outer():
        def lines(at, upper):
            def target(outs, core):
                half = core if upper else 1 - core
                return outs[0].at[pl.ds(pl.multiple_of((half * 4 + at) * (hidden // 8), hidden // 8), hidden // 8), :]
            return target
        plan = [("kept", i, lines(i, True)) for i in range(4)] + [("got", i, lines(i, False)) for i in range(4)]
        got["outer_grad"], = finish(sums["A"], order, place, hidden // 8, plan, [(hidden, width)])

    def finish_inner():
        def columns(at, upper):
            def target(outs, core):
                half = core if upper else 1 - core
                return outs[0].at[:, pl.ds(pl.multiple_of((half * blocks + at) * 512, 512), 512)]
            return target
        plan = [("kept", i, columns(i, True)) for i in range(blocks)]
        plan += [("got", i, columns(i, False)) for i in range(blocks)]
        got["inner_grad"], = finish(sums["B"], order, place, width, plan, [(width, hidden)])

    def finish_rest():
        whole = lambda outs, core: outs[1]
        column = lambda at: lambda outs, core: outs[0].at[:, pl.ds(pl.multiple_of(at(core) * width, width), width)]
        plan = [
            ("kept", 0, column(lambda core: 2 * core)), ("got", 0, column(lambda core: 2 - 2 * core)),
            ("low", 1, column(lambda core: 1)), ("high", 1, whole),
        ]
        got["panel_grad"], got["merge_grad"] = finish(
            sums["C"], order, place, width, plan, [(width, 3 * width), (width, width)]
        )

    actions = dict(
        I=inner, T=attention, X=inputs, A0=start_outer, B0=start_inner,
        C0=start_rest, S0=start_small, S=small_step, SF=finish_small, A=lambda: sums["A"].advance(order),
        B=lambda: sums["B"].advance(order), C=lambda: sums["C"].advance(order),
        AF=finish_outer, BF=finish_inner, CF=finish_rest,
    )
    for action in SEQUENCE:
        actions[action]()
    small = got["small"]
    cut = lambda row, at: small[row, at * width : (at + 1) * width]
    outer_bias_grad, gain2_grad, shift2_grad = cut(0, 0), cut(0, 1), cut(0, 2)
    inner_bias_grad = small[1]
    merge_bias_grad, gain1_grad, shift1_grad = cut(2, 0), cut(2, 1), cut(2, 2)
    query_bias_grad, value_bias_grad = cut(3, 0), cut(3, 1)
    return (
        loss.reshape(1),
        layer_out,
        got["input_grad"],
        got["panel_grad"],
        query_bias_grad,
        value_bias_grad,
        got["merge_grad"],
        merge_bias_grad,
        gain1_grad,
        shift1_grad,
        got["inner_grad"],
        inner_bias_grad,
        got["outer_grad"],
        outer_bias_grad,
        gain2_grad,
        shift2_grad,
    )


def solution(mesh):
    return jax.shard_map(
        on_device,
        mesh=mesh,
        in_specs=(
            P(("wide", "narrow"), None),
            P(("wide", "narrow"), None),
            P(),
            P(),
            P(),
            P(),
            P(),
            P(),
            P(),
            P(),
            P(),
            P(),
            P(),
            P(),
            P(),
            P(),
            P(),
        ),
        out_specs=(
            P(),
            P(("wide", "narrow"), None),
            P(("wide", "narrow"), None),
            P(),
            P(),
            P(),
            P(),
            P(),
            P(),
            P(),
            P(),
            P(),
            P(),
            P(),
            P(),
            P(),
        ),
        check_vma=False,
    )
```

```python
from functools import partial

import jax
import jax.numpy as jnp
from jax import lax
from jax.experimental import pallas as pl
from jax.experimental.pallas import tpu as pltpu
from jax.sharding import PartitionSpec as P

HEADS = 12
S_ROW = 8
BOTH = ("wide", "narrow")
BF = jnp.bfloat16
F32 = jnp.float32


def tie(values, *others):
    return lax.optimization_barrier((values, others))[0]


class Place:
    def __init__(self):
        self.wide, self.narrow = lax.axis_size("wide"), lax.axis_size("narrow")
        self.count = self.wide * self.narrow
        self.core = lax.axis_index("narrow")
        self.me = lax.axis_index("wide") * self.narrow + self.core
        bits = [self.narrow << i for i in range(self.wide.bit_length() - 1)]
        self.own = [(1, 1)]
        self.pairs = [bits[i : i + 2] for i in range(0, len(bits), 2)]
        first, second = bits[0], bits[1]
        self.stages = [[(first, second)], [(second, first)]]
        self.stages += [self.combine(pair) for pair in self.pairs[1:]]
        self.spread = [self.combine(pair) for pair in self.pairs[::-1]] + [self.own]

    def combine(self, bits):
        if len(bits) == 1:
            return [(bits[0],) * 2]
        return [(m, m) for m in (bits[0], bits[1], bits[0] | bits[1])]

    def exchange(self, value, masks):
        pairs = [(i, i ^ masks[i % 2]) for i in range(self.count)]
        return lax.ppermute(value, BOTH, pairs)

    def index(self, stage):
        bit = lambda mask: (self.me // mask) % 2
        if len(stage) == 1:
            one, other = stage[0]
            return bit(one) if one == other else jnp.where(self.core == 0, bit(one), bit(other))
        return bit(stage[0][0]) + 2 * bit(stage[1][0])


class Sum:
    def __init__(self, place, send):
        self.place = place
        self.down, self.up = list(place.stages), list(place.stages[::-1]) + [place.own]
        self.sent = [send]
        self.got = [place.exchange(send, place.own[0])]
        self.stage = None

    def receive(self, order):
        got = [order.after(g) for g in self.got]
        if self.stage is None:
            return [self.kept] + got
        index = self.place.index(self.stage)
        parts = [self.kept] + got
        if len(parts) == 2:
            return [jnp.where(index == 0, jnp.concatenate(parts), jnp.concatenate(parts[::-1]))]
        ordered = []
        for at in range(len(parts)):
            value = parts[0]
            for i in range(1, len(parts)):
                value = jnp.where(index == at ^ i, parts[i], value)
            ordered.append(value)
        return [jnp.concatenate(ordered)]

    def advance(self, order):
        if not self.up:
            return
        terms = self.receive(order)
        if self.down:
            stage = self.down.pop(0)
            parts = len(stage) + 1
            index = self.place.index(stage)
            size = terms[0].shape[0] // parts
            cut = lambda at: sum(
                lax.dynamic_slice_in_dim(t, at * size, size).astype(F32) for t in terms
            )
            self.sent = [cut(index ^ (i + 1)).astype(BF) for i in range(len(stage))]
            self.kept = cut(index)
        else:
            self.stage = stage = self.up.pop(0)
            self.kept = sum(t.astype(F32) for t in terms).astype(BF) if len(terms) > 1 else terms[0]
            self.sent = [self.kept] * len(stage)
        self.got = [self.place.exchange(s, m) for s, m in zip(self.sent, stage)]
        order.done(*self.sent)


class Order:
    def __init__(self):
        self.last = ()

    def after(self, value):
        return tie(value, *self.last)

    def done(self, *values):
        self.last = values


def add_everywhere(total, place, order):
    for stage in [place.own] + place.spread[:-1]:
        got = [place.exchange(total, masks) for masks in stage]
        order.done(total)
        yield
        for part in got:
            total = total + order.after(part)
    order.done(total)
    yield total


def nt_dot(left, right):
    return lax.dot_general(left, right, (((1,), (1,)), ((), ())), preferred_element_type=F32)


def tn_dot(left, right):
    return lax.dot_general(left, right, (((0,), (0,)), ((), ())), preferred_element_type=F32)


def thirds(value):
    top = value.astype(BF)
    rest = value - top.astype(F32)
    middle = rest.astype(BF)
    return top, middle, (rest - middle.astype(F32)).astype(BF)


def column_sum(value):
    return jnp.sum(value, axis=0, keepdims=True)


def contrast_into(block, masks, me, cool_ref, pick_ref, there_ref, own_ref, partner_ref, loss_ref, grad_ref,
                  all_ref, sums_ref, rnorm_ref):
    count, width_all = all_ref.shape
    owned = own_ref.shape[0]
    for position, mask in enumerate(masks):
        at = pl.multiple_of((me ^ mask) * owned, owned)
        all_ref[pl.ds(at, owned), :] = there_ref[position * owned : (position + 1) * owned, :]
    widths = [width_all * f // 12 for f in (1, 2, 4, 8, 12)]
    warm = 1.0 / cool_ref[0]
    lane = lax.broadcasted_iota(jnp.int32, (1, 128), 1)
    first_mask = (lane < widths[0]).astype(F32)
    spans = [(0, 128, True), (0, 128, False), (128, widths[2], False), (widths[2], widths[3], False),
             (widths[3], widths[4], False)]
    partner = partner_ref[...][None, :]

    squares = jnp.zeros((8, count), F32)
    for index, (lo, hi, masked) in enumerate(spans):
        part = all_ref[:, lo:hi].astype(F32)
        if masked:
            part = part * first_mask
        term = sum(nt_dot(jnp.ones((8, hi - lo), BF), p) for p in thirds(part * part))
        squares = term if index <= 1 else squares + term
        rnorm_ref[index] = lax.rsqrt(squares[:1] + 1e-06)
    sums_ref[...] = jnp.zeros_like(sums_ref)
    hits = jnp.zeros((1, count), F32)
    for b in range(count // block):
        rows = pl.ds(b * block, block)
        row = lax.broadcasted_iota(jnp.int32, (block, count), 0) + b * block
        diagonal = row == lax.broadcasted_iota(jnp.int32, (block, count), 1)
        positive = row == partner
        gram = norms = None
        for index, (lo, hi, masked) in enumerate(spans):
            mine = all_ref[rows, lo:hi]
            if masked:
                mine = mine * first_mask.astype(BF)
            wide = mine.astype(F32)
            term = nt_dot(mine, all_ref[:, lo:hi])
            square = jnp.sum(wide * wide, axis=1, keepdims=True)
            gram, norms = (term, square) if index <= 1 else (gram + term, norms + square)
            scores = gram * (lax.rsqrt(norms + 1e-06) * warm) * rnorm_ref[index]
            sums_ref[index] += column_sum(jnp.where(diagonal, 0.0, jnp.exp(scores)))
            hits += column_sum(jnp.where(positive, scores, 0.0))
    logs = -hits
    for index in range(5):
        logs += jnp.log(sums_ref[index])
    loss_ref[...] = jnp.sum(logs, axis=1, keepdims=True)

    first = me * owned
    col = lax.broadcasted_iota(jnp.int32, (owned, count), 1)
    line = lax.broadcasted_iota(jnp.int32, (owned, count), 0)
    chosen = jnp.zeros((owned, count), jnp.int32)
    for i in range(owned):
        chosen = jnp.where(line == i, pick_ref[first + i], chosen)
    diagonal = line + first == col
    picks = (chosen == col).astype(F32) + (partner == line + first).astype(F32)
    gram = norms = None
    weights, inverses = [], []
    for index, (lo, hi, masked) in enumerate(spans):
        mine = own_ref[:, lo:hi]
        if masked:
            mine = mine * first_mask.astype(BF)
        wide = mine.astype(F32)
        term = nt_dot(mine, all_ref[:, lo:hi])
        square = jnp.sum(wide * wide, axis=1, keepdims=True)
        gram, norms = (term, square) if index <= 1 else (gram + term, norms + square)
        inverse = lax.rsqrt(norms + 1e-06)
        raised = jnp.where(diagonal, 0.0, jnp.exp(gram * (inverse * warm) * rnorm_ref[index]))
        own_sum = jnp.sum(raised, axis=1, keepdims=True)
        pull = raised * (1.0 / own_sum + 1.0 / sums_ref[index]) - picks
        weights.append(pull * (rnorm_ref[index] * warm))
        inverses.append(inverse)
    parts = jnp.dot(
        jnp.concatenate(thirds(jnp.concatenate(weights, axis=0)), axis=0), all_ref[...],
        preferred_element_type=F32,
    )
    unit_grads = parts[: 5 * owned] + parts[5 * owned : 10 * owned] + parts[10 * owned :]
    total = jnp.zeros((owned, width_all), F32)
    column = lax.broadcasted_iota(jnp.int32, (owned, width_all), 1)
    embed = own_ref[...].astype(F32)
    for index in range(5):
        inside = column < widths[index]
        mine = jnp.where(inside, embed, 0.0)
        grad = jnp.where(inside, unit_grads[index * owned : (index + 1) * owned], 0.0)
        along = jnp.sum(mine * grad, axis=1, keepdims=True)
        inverse = inverses[index]
        total += inverse * grad - (inverse * inverse * inverse * along) * mine
    grad_ref[...] = total


SEQUENCE = (
    "A0", "A", "I", "A", "B0", "B", "A", "T", "A", "B", "C0", "A", "C", "B",
    "A", "C", "B", "A", "C", "B", "C", "B", "X", "C", "S0", "B", "C", "A",
    "S", "BF", "C", "S", "AF", "SF", "C", "CF",
)


def kernel_call(body, name, flops, nbytes, limit=58, **options):
    return pl.pallas_call(
        body,
        compiler_params=pltpu.CompilerParams(vmem_limit_bytes=limit << 20),
        cost_estimate=pl.CostEstimate(flops=flops, bytes_accessed=nbytes, transcendentals=0),
        name=name,
        **options,
    )


def fixed(shape):
    return pl.BlockSpec(shape, lambda *_: (0,) * len(shape))


def windows(length, step=128):
    return [(at, max(0, at - step), min(length, at + 2 * step)) for at in range(0, length, step)]


def segment_row(seg_ref):
    return seg_ref[pl.ds(pl.program_id(0), 1), :].astype(F32)


def segment_column(seg):
    return jnp.broadcast_to(seg, (128, seg.shape[1])).T


def masks_into(bias_ref, seg_ref):
    seg = segment_row(seg_ref)
    column = segment_column(seg)
    for index, (at, lo, hi) in enumerate(windows(seg.shape[1])):
        same = column[lo:hi, :] == seg[:, at : at + 128]
        bias = jnp.where(same, 0.0, -1e9)
        bias_ref[index, : hi - lo, :] = jnp.concatenate([bias, bias], axis=1)


def pair_stack(two):
    lane = lax.broadcasted_iota(jnp.int32, two.shape, 1)
    nought = jnp.zeros_like(two)
    half = two.shape[1] // 2
    return jnp.concatenate(
        [jnp.where(lane < half, two, nought), jnp.where(lane < half, nought, two)], axis=0
    )


def pair_merge(both):
    size = both.shape[1] // 2
    row = lax.broadcasted_iota(jnp.int32, (both.shape[0], size), 0)
    return jnp.where(row < both.shape[0] // 2, both[:, :size], both[:, size:])


def attend_kernel(x_ref, seg_ref, w_ref, bq_ref, bv_ref, wo_ref, bo_ref, gain_ref,
                  shift_ref, q_ref, k_ref, v_ref, mixed_t_ref, lse_ref, hat_ref, rstd_ref, low_ref,
                  x_t_ref, low_t_ref, bias_ref, mixed_ref):
    length, width = x_ref.shape
    x = x_ref[...]
    masks_into(bias_ref, seg_ref)
    q = jnp.dot(x, w_ref[:, :width], preferred_element_type=F32) + bq_ref[...][None, :]
    q_ref[...] = (q.astype(BF).astype(F32) * (width // HEADS) ** -0.5).astype(BF)
    k_ref[...] = jnp.dot(x, w_ref[:, width : 2 * width], preferred_element_type=F32).astype(BF)
    v_ref[...] = (jnp.dot(x, w_ref[:, 2 * width :], preferred_element_type=F32) + bv_ref[...][None, :]).astype(BF)
    jobs = [(pair, index) + win for pair in range(HEADS // 2) for index, win in enumerate(windows(length))]

    def scores(job):
        pair, index, at, lo, hi = job
        lanes = slice(pair * 128, pair * 128 + 128)
        stacked = pair_stack(q_ref[at : at + 128, lanes])
        return nt_dot(k_ref[lo:hi, lanes], stacked)

    ahead = scores(jobs[0])
    for number, job in enumerate(jobs):
        pair, index, at, lo, hi = job
        lanes = slice(pair * 128, pair * 128 + 128)
        raw = ahead
        if number + 1 < len(jobs):
            ahead = scores(jobs[number + 1])
        masked = raw + bias_ref[index, : hi - lo, :]
        top = jnp.max(masked, axis=0, keepdims=True)
        raised = jnp.exp(masked - top)
        total = jnp.sum(raised, axis=0, keepdims=True)
        log_total = top + jnp.log(total)
        for side in (0, 1):
            head = 2 * pair + side
            lse_ref[head // 4, head % 4 : head % 4 + 1, at : at + 128] = log_total[:, side * 128 : side * 128 + 128]
        both = tn_dot((raised * (1.0 / total)).astype(BF), v_ref[lo:hi, lanes])
        lane = lax.broadcasted_iota(jnp.int32, (128, 128), 1)
        merged = jnp.where(lane < 64, both[:128], both[128:])
        mixed_ref[at : at + 128, lanes] = merged.astype(BF)
        mixed_t_ref[lanes, at : at + 128] = merged.T.astype(BF)
    attn = jnp.dot(mixed_ref[...], wo_ref[...], preferred_element_type=F32) + bo_ref[...][None, :]
    total = x.astype(F32) + attn
    center = total - jnp.mean(total, axis=1, keepdims=True)
    rstd = lax.rsqrt(jnp.mean(center * center, axis=1, keepdims=True) + 1e-05)
    hat = center * rstd
    hat_ref[...] = hat
    rstd_ref[...] = rstd
    low = (hat * gain_ref[...][None, :] + shift_ref[...][None, :]).astype(BF)
    low_ref[...] = low
    low_t_ref[...] = low.T
    x_t_ref[...] = x.T


def attend(x, seg, w, bq, bv, wo, bo, gain, shift):
    tokens, width = x.shape
    rows, length = seg.shape
    row_block = lambda *tail: pl.BlockSpec((length,) + tail, lambda r: (r, 0))
    return kernel_call(
        attend_kernel, "attend", 2 * tokens * width * width * 4 + 4 * tokens * 384 * width * 2, 20 << 20,
        grid=(rows,),
        in_specs=[
            row_block(width), fixed(seg.shape), fixed(w.shape), fixed(bq.shape), fixed(bv.shape), fixed(wo.shape), fixed(bo.shape),
            fixed(gain.shape), fixed(shift.shape),
        ],
        out_specs=(
            row_block(width), row_block(width), row_block(width),
            pl.BlockSpec((width, length), lambda r: (0, r)),
            pl.BlockSpec((HEADS // 4, 4, length), lambda r: (r, 0, 0)),
            row_block(width), row_block(1), row_block(width),
            pl.BlockSpec((width, length), lambda r: (0, r)), pl.BlockSpec((width, length), lambda r: (0, r)),
        ),
        out_shape=(
            jax.ShapeDtypeStruct((tokens, width), BF), jax.ShapeDtypeStruct((tokens, width), BF),
            jax.ShapeDtypeStruct((tokens, width), BF), jax.ShapeDtypeStruct((width, tokens), BF),
            jax.ShapeDtypeStruct((rows * HEADS // 4, 4, length), F32), jax.ShapeDtypeStruct((tokens, width), F32),
            jax.ShapeDtypeStruct((tokens, 1), F32), jax.ShapeDtypeStruct((tokens, width), BF),
            jax.ShapeDtypeStruct((width, tokens), BF), jax.ShapeDtypeStruct((width, tokens), BF),
        ),
        scratch_shapes=[
            pltpu.VMEM((length // 128, 384, 256), F32), pltpu.VMEM((length, width), BF),
        ],
    )(x, seg, w, bq, bv, wo, bo, gain, shift)


def gelu_parts(v):
    bell = jnp.exp(v * v * -0.5)
    t = 1.0 / (1.0 + (0.3275911 * 0.5 ** 0.5) * jnp.abs(v))
    poly = ((((0.5 * 1.061405429 * t - 0.5 * 1.453152027) * t + 0.5 * 1.421413741) * t
             - 0.5 * 0.284496736) * t + 0.5 * 0.254829592) * t
    tail = poly * bell
    share = jnp.where(v >= 0.0, 1.0 - tail, tail)
    return v * share, share + v * bell * 0.3989422804014327


def feed_kernel(chunk, hat_ref, low_ref, seg_ref, gain1_ref, shift1_ref, w1_ref, b1_ref, w2_ref, b2_ref,
                gain_ref, shift_ref, act_t_ref, slope_ref, hat2_ref, rstd2_ref, out_ref, embed_ref,
                pooled_ref, value_ref):
    length, width = hat_ref.shape
    hidden = w1_ref.shape[1]
    low = low_ref[...]
    count = hidden // chunk

    def entry(i):
        return jnp.dot(low, w1_ref[:, i * chunk : (i + 1) * chunk], preferred_element_type=F32)

    total = hat_ref[...] * gain1_ref[...][None, :] + shift1_ref[...][None, :] + b2_ref[...][None, :]
    ahead = entry(0)
    for i in range(count):
        cols = slice(i * chunk, (i + 1) * chunk)
        inner = ahead + b1_ref[cols][None, :]
        if i + 1 < count:
            ahead = entry(i + 1)
        value, slope = gelu_parts(inner)
        value = value.astype(BF)
        act_t_ref[cols, :] = value.T
        slope_ref[:, cols] = slope.astype(BF)
        value_ref[:, cols] = value
    total += jnp.dot(value_ref[...], w2_ref[...], preferred_element_type=F32)
    center = total - jnp.mean(total, axis=1, keepdims=True)
    rstd = lax.rsqrt(jnp.mean(center * center, axis=1, keepdims=True) + 1e-05)
    hat = center * rstd
    hat2_ref[...] = hat
    rstd2_ref[...] = rstd
    out = hat * gain_ref[...][None, :] + shift_ref[...][None, :]
    out_ref[...] = out.astype(BF)
    number = lax.broadcasted_iota(jnp.int32, (S_ROW, length), 0)
    onehot = (segment_row(seg_ref) == number.astype(F32)).astype(F32)
    tokens_in = jnp.sum(onehot, axis=1, keepdims=True)
    onehot = onehot.astype(BF)
    sums = jnp.zeros((S_ROW, width), F32)
    for part in thirds(out):
        sums += jnp.dot(onehot, part, preferred_element_type=F32)
    row = pl.program_id(0)
    pooled_ref[pl.ds(row * S_ROW, S_ROW), :] = sums / tokens_in

    @pl.when(row == pl.num_programs(0) - 1)
    def _():
        embed_ref[...] = pooled_ref[...].astype(BF)


def feed(hat, low, seg, gain1, shift1, w1, b1, w2, b2, gain, shift):
    tokens, width = hat.shape
    rows, length = seg.shape
    hidden = w1.shape[1]
    row_block = lambda *tail: pl.BlockSpec((length,) + tail, lambda r: (r, 0))
    return kernel_call(
        partial(feed_kernel, 1024), "feed", 4 * tokens * width * hidden, 30 << 20,
        grid=(rows,),
        in_specs=[
            row_block(width), row_block(width), fixed(seg.shape),
        ] + [fixed(a.shape) for a in (gain1, shift1, w1, b1, w2, b2, gain, shift)],
        out_specs=(
            pl.BlockSpec((hidden, length), lambda r: (0, r)), row_block(hidden), row_block(width), row_block(1),
            row_block(width),
            fixed((rows * S_ROW, width)),
        ),
        out_shape=(
            jax.ShapeDtypeStruct((hidden, tokens), BF), jax.ShapeDtypeStruct((tokens, hidden), BF),
            jax.ShapeDtypeStruct((tokens, width), F32), jax.ShapeDtypeStruct((tokens, 1), F32),
            jax.ShapeDtypeStruct((tokens, width), BF), jax.ShapeDtypeStruct((rows * S_ROW, width), BF),
        ),
        scratch_shapes=[pltpu.VMEM((rows * S_ROW, width), F32), pltpu.VMEM((length, hidden), BF)],
    )(hat, low, seg, gain1, shift1, w1, b1, w2, b2, gain, shift)


def norm_back(grad, hat, rstd, gain):
    inside = grad * gain
    first = jnp.mean(inside, axis=1, keepdims=True)
    second = jnp.mean(inside * hat, axis=1, keepdims=True)
    return (inside - first - hat * second) * rstd


def line_into(ref, vectors):
    ref[...] = jnp.zeros_like(ref)
    at = 0
    for vector in vectors:
        ref[:, at : at + vector.shape[1]] = vector
        at += vector.shape[1]


def copies(pairs, sems):
    return [pltpu.make_async_copy(src, dst, sems.at[i]) for i, (src, dst) in enumerate(pairs)]


def outer_back_kernel(block, masks, info_ref, pick_ref, cool_ref, there_ref, own_ref, partner_ref, seg_ref, rstd_ref,
                      gain_ref, act_t_ref, hat_hbm, loss_ref, line_ref, send_ref,
                      keep_ref, second_hbm, outer_hbm, embed_grad_ref, all_ref, sums_ref, rnorm_ref,
                      hat_ref, second_ref, outer_ref, sems):
    step = pl.program_id(0)
    rows, length = seg_ref.shape
    width = gain_ref.shape[0]
    load, *store = copies([(hat_hbm, hat_ref), (second_ref, second_hbm), (outer_ref, outer_hbm)], sems)

    @pl.when(step == 0)
    def _():
        load.start()
        contrast_into(block, masks, info_ref[0], cool_ref, pick_ref, there_ref, own_ref, partner_ref,
                      loss_ref, embed_grad_ref, all_ref, sums_ref, rnorm_ref)
        load.wait()
        gains, shifts, biases = [], [], []
        for row in range(rows):
            span = slice(row * length, (row + 1) * length)
            seg = seg_ref[row : row + 1, :].astype(F32)
            number = lax.broadcasted_iota(jnp.int32, (S_ROW, length), 0).astype(F32)
            tokens_in = jnp.sum((seg == number).astype(F32), axis=1, keepdims=True)
            each = embed_grad_ref[row * S_ROW : (row + 1) * S_ROW, :] / tokens_in
            stack = [p.astype(F32) for p in thirds(each)] + [jnp.zeros((128 - 3 * S_ROW, width), F32)]
            lane = lax.broadcasted_iota(jnp.int32, (length, 128), 1)
            pick = (lane < 3 * S_ROW) & ((lane % S_ROW).astype(F32) == segment_column(seg))
            grad = jnp.dot(
                pick.astype(BF), jnp.concatenate(stack).astype(BF), preferred_element_type=F32
            )
            hat = hat_ref[span, :]
            second = norm_back(grad, hat, rstd_ref[span, :], gain_ref[...][None, :])
            low = second.astype(BF)
            second_ref[span, :] = second
            outer_ref[span, :] = low
            gains.append(column_sum(grad * hat))
            shifts.append(column_sum(grad))
            biases.append(column_sum(low.astype(F32)))
        line_into(line_ref, [sum(biases), sum(gains), sum(shifts)])
        for copy in store:
            copy.start()

    weight = jnp.dot(act_t_ref[...], outer_ref[...], preferred_element_type=F32).astype(BF)
    half = pl.num_programs(0) // 2

    @pl.when(step < half)
    def _():
        send_ref[...] = weight

    @pl.when(step >= half)
    def _():
        keep_ref[...] = weight

    @pl.when(step == pl.num_programs(0) - 1)
    def _():
        for copy in store:
            copy.wait()


def gather_embeds(own, place):
    there, masks = own, [0]
    for stage in place.spread:
        there = jnp.concatenate([there] + [place.exchange(there, pair) for pair in stage])
        masks = masks + [m ^ pair[0] for pair in stage for m in masks]
    return there, masks


def outer_back(own, partner, coolness, seg, hat, rstd, gain, act_t, place, chunk=768):
    there, masks = gather_embeds(own, place)
    owned, width = own.shape
    count = owned * len(masks)
    tokens = hat.shape[0]
    hidden = act_t.shape[0]
    steps = hidden // chunk
    half = steps // 2
    whole = lambda shape: pl.BlockSpec(shape, lambda i, *_: (0,) * len(shape))
    smem, hbm = pl.BlockSpec(memory_space=pltpu.SMEM), pl.BlockSpec(memory_space=pl.ANY)
    vmem = pl.BlockSpec(memory_space=pltpu.VMEM)
    turn = lambda i, info: (lax.rem(i + half * (1 - info[1]), steps), 0)
    return kernel_call(
        partial(outer_back_kernel, min(count, 256), masks), "outer_back", 2 * tokens * hidden * width, 20 << 20,
        grid_spec=pltpu.PrefetchScalarGridSpec(
            num_scalar_prefetch=1,
            grid=(steps,),
            in_specs=[smem, smem, vmem, vmem, whole(partner.shape), whole(seg.shape),
                      whole(rstd.shape), whole(gain.shape), pl.BlockSpec((chunk, tokens), turn), hbm],
            out_specs=(
                whole((1, 1)), whole((1, hidden)),
                pl.BlockSpec((chunk, width), lambda i, info: (jnp.minimum(i, half - 1), 0)),
                pl.BlockSpec((chunk, width), lambda i, info: (jnp.maximum(i - half, 0), 0)), hbm, hbm,
            ),
            scratch_shapes=[
                pltpu.VMEM((owned, width), F32), pltpu.VMEM((count, width), BF), pltpu.VMEM((5, 1, count), F32),
                pltpu.VMEM((5, 1, count), F32), pltpu.VMEM((tokens, width), F32),
                pltpu.VMEM((tokens, width), F32), pltpu.VMEM((tokens, width), BF), pltpu.SemaphoreType.DMA((3,)),
            ],
        ),
        out_shape=(
            jax.ShapeDtypeStruct((1, 1), F32), jax.ShapeDtypeStruct((1, hidden), F32),
            jax.ShapeDtypeStruct((hidden // 2, width), BF), jax.ShapeDtypeStruct((hidden // 2, width), BF),
            jax.ShapeDtypeStruct((tokens, width), F32), jax.ShapeDtypeStruct((tokens, width), BF),
        ),
    )(jnp.stack([place.me, place.core]), partner, coolness, there, own, partner, seg, rstd, gain, act_t, hat)


def inner_back_kernel(rows, info_ref, outer_ref, low_t_ref, slope_ref, w2_ref, w1_ref, rstd_ref, gain_ref, second_hbm,
                      hat_hbm, mixed_t_hbm, wo_hbm, send_ref, keep_ref, bias_ref, mixed_grad_ref, merge_ref, line_ref,
                      first_hbm,
                      normed_ref, second_ref, hat_ref, mixed_t_ref, wo_ref, sems, out_sems):
    step, last = pl.program_id(0), pl.num_programs(0) - 1
    length = outer_ref.shape[0] // rows
    loads = copies([(second_hbm, second_ref), (hat_hbm, hat_ref), (mixed_t_hbm, mixed_t_ref), (wo_hbm, wo_ref)], sems)

    @pl.when(step == 0)
    def _():
        for copy in loads:
            copy.start()

    active = nt_dot(outer_ref[...], w2_ref[...])
    inner = (active * slope_ref[...].astype(F32)).astype(BF)
    bias_ref[...] = column_sum(inner.astype(F32))
    weight = jnp.dot(low_t_ref[...], inner, preferred_element_type=F32).astype(BF)
    normed = nt_dot(inner, w1_ref[...])

    @pl.when(step <= last // 2)
    def _():
        send_ref[...] = weight

    @pl.when(step > last // 2)
    def _():
        keep_ref[...] = weight

    @pl.when(step == 0)
    def _():
        normed_ref[...] = normed

    @pl.when(step > 0)
    def _():
        normed_ref[...] += normed

    @pl.when(step == last)
    def _():
        for copy in loads:
            copy.wait()
        gains, shifts, biases, merges, stores = [], [], [], [], []
        for row in range(rows):
            span = slice(row * length, (row + 1) * length)
            hat = hat_ref[span, :]
            grad = normed_ref[span, :] + second_ref[span, :]
            first = norm_back(grad, hat, rstd_ref[span, :], gain_ref[...][None, :])
            normed_ref[span, :] = first
            store = pltpu.make_async_copy(normed_ref.at[span, :], first_hbm.at[span, :], out_sems.at[row])
            store.start()
            stores.append(store)
            low = first.astype(BF)
            gains.append(column_sum(grad * hat))
            shifts.append(column_sum(grad))
            biases.append(column_sum(low.astype(F32)))
            mixed_grad_ref[span, :] = nt_dot(low, wo_ref[...]).astype(BF)
            merges.append(jnp.dot(mixed_t_ref[:, span], low, preferred_element_type=F32))
        merge_ref[...] = sum(merges).astype(BF)
        line_into(line_ref, [sum(biases), sum(gains), sum(shifts)])
        for store in stores:
            store.wait()


def inner_back(outer, second, low_t, slope, w2, w1, hat, rstd, gain, mixed_t, wo, rows, place, chunk=512):
    tokens, width = outer.shape
    hidden = slope.shape[1]
    steps = hidden // chunk
    half = steps // 2
    whole = lambda shape: pl.BlockSpec(shape, lambda i, *_: (0,) * len(shape))
    hbm = pl.BlockSpec(memory_space=pl.ANY)
    turn = lambda i, info: lax.rem(i + half * (1 - info[1]), steps)
    early = lambda i: jnp.minimum(i, half - 1)
    late = lambda i: jnp.maximum(i - half, 0)
    line = jax.ShapeDtypeStruct((1, hidden), F32)
    part = jax.ShapeDtypeStruct((half * width, chunk), BF)
    return kernel_call(
        partial(inner_back_kernel, rows), "inner_back", 6 * tokens * hidden * width, 40 << 20, limit=46,
        grid_spec=pltpu.PrefetchScalarGridSpec(
            num_scalar_prefetch=1,
            grid=(steps,),
            in_specs=[
                whole(outer.shape), whole(low_t.shape),
                pl.BlockSpec((tokens, chunk), lambda i, info: (0, turn(i, info))),
                pl.BlockSpec((chunk, width), lambda i, info: (turn(i, info), 0)),
                pl.BlockSpec((width, chunk), lambda i, info: (0, turn(i, info))),
                whole(rstd.shape), whole(gain.shape), hbm, hbm, hbm, hbm,
            ],
            out_specs=(
                pl.BlockSpec((width, chunk), lambda i, info: (early(i), 0)),
                pl.BlockSpec((width, chunk), lambda i, info: (late(i), 0)),
                pl.BlockSpec((1, chunk), lambda i, info: (0, turn(i, info))),
                whole((tokens, width)), whole((width, width)), whole((1, hidden)), hbm,
            ),
            scratch_shapes=[
                pltpu.VMEM((tokens, width), F32), pltpu.VMEM((tokens, width), F32), pltpu.VMEM((tokens, width), F32),
                pltpu.VMEM(mixed_t.shape, BF), pltpu.VMEM(wo.shape, BF), pltpu.SemaphoreType.DMA((4,)),
                pltpu.SemaphoreType.DMA((rows,)),
            ],
        ),
        out_shape=(
            part, part, line, jax.ShapeDtypeStruct((tokens, width), BF),
            jax.ShapeDtypeStruct((width, width), BF), line,
            jax.ShapeDtypeStruct((tokens, width), F32),
        ),
    )(jnp.stack([place.me, place.core]), outer, low_t, slope, w2, w1, rstd, gain, second, hat, mixed_t, wo)


def attend_back_kernel(pairs, core_ref, x_t_ref, merge_ref, seg_ref, lse_ref, q_ref, k_ref, v_ref, grad_ref,
                       dq_ref, dk_ref, dv_ref, send_ref, keep_ref, line_ref,
                       bias_ref, k_sum_ref, v_sum_ref, weight_ref):
    row = pl.program_id(0)
    length = q_ref.shape[0]
    masks_into(bias_ref, seg_ref)
    k_sum_ref[...] = jnp.zeros_like(k_sum_ref)
    v_sum_ref[...] = jnp.zeros_like(v_sum_ref)
    jobs = [(pair, index) + win for pair in range(pairs) for index, win in enumerate(windows(length))]

    def begin(job):
        pair, index, at, lo, hi = job
        lanes = slice(pair * 128, pair * 128 + 128)
        query = pair_stack(q_ref[at : at + 128, lanes])
        grad = pair_stack(grad_ref[at : at + 128, lanes])
        return query, grad, nt_dot(k_ref[lo:hi, lanes], query), nt_dot(v_ref[lo:hi, lanes], grad)

    ahead = begin(jobs[0])
    for number, job in enumerate(jobs):
        pair, index, at, lo, hi = job
        lanes = slice(pair * 128, pair * 128 + 128)
        query, grad, raw, prob_grad = ahead
        if number + 1 < len(jobs):
            ahead = begin(jobs[number + 1])
        log_total = jnp.concatenate(
            [lse_ref[head // 4, head % 4 : head % 4 + 1, at : at + 128] for head in (2 * pair, 2 * pair + 1)],
            axis=1
        )
        probs = jnp.exp(raw + bias_ref[index, : hi - lo, :] - log_total)
        weighed = probs * prob_grad
        raw_grad = (weighed - probs * jnp.sum(weighed, axis=0, keepdims=True)).astype(BF)
        v_sum_ref[lo:hi, lanes] += jnp.dot(probs.astype(BF), grad, preferred_element_type=F32)
        k_sum_ref[lo:hi, lanes] += jnp.dot(raw_grad, query, preferred_element_type=F32)
        if index == 0:
            keys_t = k_ref[:, lanes].T
        both = jnp.dot(keys_t[:, lo:hi], raw_grad, preferred_element_type=F32)
        merged = pair_merge(both) * 0.125
        dq_ref[at : at + 128, lanes] = merged.T.astype(BF)
    dk_ref[...] = k_sum_ref[...].astype(BF)
    dv_ref[...] = v_sum_ref[...].astype(BF)

    @pl.when(row == 0)
    def _():
        for ref in (weight_ref, line_ref):
            ref[...] = jnp.zeros_like(ref)

    width = dq_ref.shape[1]
    line_ref[:, :width] += column_sum(dq_ref[...].astype(F32))
    line_ref[:, width : 2 * width] += column_sum(dv_ref[...].astype(F32))
    for index, ref in enumerate((dq_ref, dk_ref, dv_ref)):
        weight_ref[index] += jnp.dot(x_t_ref[...], ref[...], preferred_element_type=F32)

    @pl.when(row == pl.num_programs(0) - 1)
    def _():
        for mine, first, second in ((0, keep_ref, send_ref), (1, send_ref, keep_ref)):
            @pl.when(core_ref[0] == mine)
            def _(first=first, second=second):
                first[...] = weight_ref[:2].astype(BF)
                second[0] = weight_ref[2].astype(BF)
                second[1] = merge_ref[...]


def attend_back(x_t, merge, seg, lse, q, k, v, grad, place):
    tokens, width = q.shape
    rows, length = seg.shape
    part = pl.BlockSpec((length, width), lambda r, core: (r, 0))
    whole = lambda shape: pl.BlockSpec(shape, lambda i, *_: (0,) * len(shape))
    groups = HEADS // 4
    half = jax.ShapeDtypeStruct((2, width, width), BF)
    return kernel_call(
        partial(attend_back_kernel, HEADS // 2), "attend_back",
        10 * tokens * 384 * width * 2 + 6 * tokens * width * width, 30 << 20, limit=40,
        grid_spec=pltpu.PrefetchScalarGridSpec(
            num_scalar_prefetch=1,
            grid=(rows,),
            in_specs=[
                pl.BlockSpec((width, length), lambda r, core: (0, r)), whole(merge.shape), whole(seg.shape),
                pl.BlockSpec((groups, 4, length), lambda r, core: (r, 0, 0)), part, part, part, part,
            ],
            out_specs=(part, part, part, whole(half.shape), whole(half.shape), whole((1, 4 * width))),
            scratch_shapes=[
                pltpu.VMEM((length // 128, 384, 256), F32), pltpu.VMEM((length, width), F32),
                pltpu.VMEM((length, width), F32), pltpu.VMEM((3, width, width), F32),
            ],
        ),
        out_shape=(jax.ShapeDtypeStruct((tokens, width), BF),) * 3
        + (half, half, jax.ShapeDtypeStruct((1, 4 * width), F32)),
    )(place.core.reshape(1), x_t, merge, seg, lse, q, k, v, grad)


def input_back_kernel(first_ref, *refs):
    *grads, w_ref, out_ref = refs
    width = first_ref.shape[1]
    total = first_ref[...]
    for index, ref in enumerate(grads):
        total += nt_dot(ref[...], w_ref[:, index * width : (index + 1) * width])
    out_ref[...] = total


def input_back(first, grads, w, block=512):
    tokens, width = first.shape
    rows = lambda cols: pl.BlockSpec((block, cols), lambda i: (i, 0))
    return kernel_call(
        input_back_kernel, "input_back", 6 * tokens * width * width, 15 << 20,
        grid=(tokens // block,),
        in_specs=[rows(width)] + [rows(g.shape[1]) for g in grads] + [fixed(w.shape)],
        out_specs=rows(width),
        out_shape=jax.ShapeDtypeStruct((tokens, width), F32),
    )(first, *grads, w)


def finish_kernel(plan, core_ref, kept_ref, got_ref, *refs):
    *outs, out_ref, out_sems = refs
    core = core_ref[0]
    rows = out_ref.shape[1]
    stores = []
    for index, (kind, at, target) in enumerate(plan):
        span = slice(at * rows, (at + 1) * rows)
        kept, got = kept_ref[span, :].astype(F32), got_ref[span, :].astype(F32)
        own = core == (0 if kind == "low" else 1)
        out_ref[index] = kept if kind == "kept" else got if kind == "got" else jnp.where(own, kept, got)
        stores.append(pltpu.make_async_copy(out_ref.at[index], target(outs, core), out_sems.at[index]))
        stores[-1].start()
    for store in stores:
        store.wait()


def finish(one, order, place, rows, plan, shapes):
    while one.up:
        one.advance(order)
    kept, got = one.kept, order.after(one.got[0])
    half, cols = kept.shape
    hbm = pl.BlockSpec(memory_space=pl.ANY)
    result = kernel_call(
        partial(finish_kernel, plan), "finish", 0, half * cols * 12, limit=24,
        in_specs=[pl.BlockSpec(memory_space=pltpu.SMEM)] + [pl.BlockSpec(memory_space=pltpu.VMEM)] * 2,
        out_specs=[hbm] * len(shapes),
        out_shape=[jax.ShapeDtypeStruct(shape, F32) for shape in shapes],
        scratch_shapes=[
            pltpu.VMEM((len(plan), rows, cols), F32), pltpu.SemaphoreType.DMA((len(plan),)),
        ],
    )(place.core.reshape(1), kept, got)
    order.done(*result)
    return result


def on_device(
    incoming_activations,
    span_identifiers,
    partner_global_index,
    softmax_coolness,
    triple_kernel_panel,
    asking_shift,
    content_shift,
    mixer_result_kernel,
    mixer_result_shift,
    initial_standardize_scale,
    initial_standardize_shift,
    perceptron_entry_kernel,
    perceptron_entry_shift,
    perceptron_result_kernel,
    perceptron_result_shift,
    later_standardize_scale,
    later_standardize_shift,
):
    rows, length = span_identifiers.shape
    width = incoming_activations.shape[1]
    hidden = perceptron_entry_kernel.shape[1]
    place, order = Place(), Order()
    seg = span_identifiers
    q, k, v, mixed_t, lse, hat1, rstd1, low, x_t, low_t = attend(
        incoming_activations, seg, triple_kernel_panel, asking_shift, content_shift, mixer_result_kernel,
        mixer_result_shift, initial_standardize_scale, initial_standardize_shift,
    )
    act_t, slope, hat2, rstd2, layer_out, embed = feed(
        hat1, low, seg, initial_standardize_scale, initial_standardize_shift, perceptron_entry_kernel,
        perceptron_entry_shift, perceptron_result_kernel, perceptron_result_shift, later_standardize_scale,
        later_standardize_shift,
    )
    (
        loss, second_line, outer_send, outer_keep, second, outer,
    ) = outer_back(
        embed, partner_global_index, softmax_coolness, seg, hat2, rstd2, later_standardize_scale, act_t, place
    )
    order.done(outer)
    got, sums, blocks = {}, {}, hidden // 512 // 2

    def inner():
        (
            got["inner_send"], got["inner_keep"], got["inner_line"], got["mixed_grad"], got["merge"],
            got["first_line"], got["first"],
        ) = inner_back(
            order.after(outer), second, low_t, slope, perceptron_result_kernel, perceptron_entry_kernel, hat1,
            rstd1, initial_standardize_scale, mixed_t, mixer_result_kernel, rows, place,
        )
        order.done(got["mixed_grad"])

    def attention():
        *got["grads"], got["rest_send"], got["rest_keep"], got["rest_line"] = attend_back(
            x_t, got["merge"], seg, lse, q, k, v, order.after(got["mixed_grad"]), place
        )
        order.done(got["rest_send"])

    def inputs():
        got["input_grad"] = input_back(order.after(got["first"]), got["grads"], triple_kernel_panel)
        order.done(got["input_grad"])

    def start(name, send, keep):
        sums[name] = Sum(place, order.after(send))
        sums[name].kept = keep
        order.done(*sums[name].sent)

    def start_outer():
        start("A", outer_send, outer_keep)

    def start_inner():
        start("B", got["inner_send"], got["inner_keep"])

    def start_rest():
        start("C", got["rest_send"].reshape(2 * width, width), got["rest_keep"].reshape(2 * width, width))

    def start_small():
        lines = [second_line, got["inner_line"], got["first_line"], got["rest_line"]]
        small = jnp.concatenate(lines, axis=0)
        sums["S"] = add_everywhere(order.after(small), place, order)
        next(sums["S"])

    def small_step():
        got["small"] = next(sums["S"])

    def finish_small():
        while got.get("small") is None:
            small_step()

    def finish_outer():
        def lines(at, upper):
            def target(outs, core):
                half = core if upper else 1 - core
                return outs[0].at[pl.ds(pl.multiple_of((half * 4 + at) * (hidden // 8), hidden // 8), hidden // 8), :]
            return target
        plan = [("kept", i, lines(i, True)) for i in range(4)] + [("got", i, lines(i, False)) for i in range(4)]
        got["outer_grad"], = finish(sums["A"], order, place, hidden // 8, plan, [(hidden, width)])

    def finish_inner():
        def columns(at, upper):
            def target(outs, core):
                half = core if upper else 1 - core
                return outs[0].at[:, pl.ds(pl.multiple_of((half * blocks + at) * 512, 512), 512)]
            return target
        plan = [("kept", i, columns(i, True)) for i in range(blocks)]
        plan += [("got", i, columns(i, False)) for i in range(blocks)]
        got["inner_grad"], = finish(sums["B"], order, place, width, plan, [(width, hidden)])

    def finish_rest():
        whole = lambda outs, core: outs[1]
        column = lambda at: lambda outs, core: outs[0].at[:, pl.ds(pl.multiple_of(at(core) * width, width), width)]
        plan = [
            ("kept", 0, column(lambda core: 2 * core)), ("got", 0, column(lambda core: 2 - 2 * core)),
            ("low", 1, column(lambda core: 1)), ("high", 1, whole),
        ]
        got["panel_grad"], got["merge_grad"] = finish(
            sums["C"], order, place, width, plan, [(width, 3 * width), (width, width)]
        )

    actions = dict(
        I=inner, T=attention, X=inputs, A0=start_outer, B0=start_inner,
        C0=start_rest, S0=start_small, S=small_step, SF=finish_small, A=lambda: sums["A"].advance(order),
        B=lambda: sums["B"].advance(order), C=lambda: sums["C"].advance(order),
        AF=finish_outer, BF=finish_inner, CF=finish_rest,
    )
    for action in SEQUENCE:
        actions[action]()
    small = got["small"]
    cut = lambda row, at: small[row, at * width : (at + 1) * width]
    outer_bias_grad, gain2_grad, shift2_grad = cut(0, 0), cut(0, 1), cut(0, 2)
    inner_bias_grad = small[1]
    merge_bias_grad, gain1_grad, shift1_grad = cut(2, 0), cut(2, 1), cut(2, 2)
    query_bias_grad, value_bias_grad = cut(3, 0), cut(3, 1)
    return (
        loss.reshape(1),
        layer_out,
        got["input_grad"],
        got["panel_grad"],
        query_bias_grad,
        value_bias_grad,
        got["merge_grad"],
        merge_bias_grad,
        gain1_grad,
        shift1_grad,
        got["inner_grad"],
        inner_bias_grad,
        got["outer_grad"],
        outer_bias_grad,
        gain2_grad,
        shift2_grad,
    )


def solution(mesh):
    return jax.shard_map(
        on_device,
        mesh=mesh,
        in_specs=(
            P(("wide", "narrow"), None),
            P(("wide", "narrow"), None),
            P(),
            P(),
            P(),
            P(),
            P(),
            P(),
            P(),
            P(),
            P(),
            P(),
            P(),
            P(),
            P(),
            P(),
            P(),
        ),
        out_specs=(
            P(),
            P(("wide", "narrow"), None),
            P(("wide", "narrow"), None),
            P(),
            P(),
            P(),
            P(),
            P(),
            P(),
            P(),
            P(),
            P(),
            P(),
            P(),
            P(),
            P(),
        ),
        check_vma=False,
    )
```
